32 devices in a mesh: replica: 8 (over z, x), tensor: 4 (over y, core).
Axes of the slice: x: 2, y: 2, z: 4, core: 2. Of those that a mesh axis runs over, the one named last changes fastest.
Arguments:
- hidden_input: bfloat16 [512, 3584], P('replica', 'tensor'), may hold values from -6 to 6
- queries: bfloat16 [512, 2048], P('replica', 'tensor'), may hold values from -8 to 8
- prompt_cache: bfloat16 [32, 2, 2048, 1024], P('replica', None, None, 'tensor'), may hold values from -8 to 8
- suffix_cache: bfloat16 [512, 2, 64, 1024], P('replica', None, None, 'tensor'), may hold values from -6 to 6
- owner_replica: int32 [512, 1], P('replica'), may hold values from 0 to 7; in each aligned block of 64 rows (0 to 63, 64 to 127, ...) at most 16 rows name the same one
- group_slot: int32 [512], P('replica'), may hold values from 0 to 3
- prompt_length: int32 [32], P('replica'), may hold values from 256 to 2048
- suffix_length: int32 [512], P('replica'), may hold values from 1 to 64
- output_weight: bfloat16 [2048, 3584], P('tensor'), may hold values from -0.1875 to 0.1875
- post_gain: float32 [3584], P('tensor'), may hold values from 0.1 to 1.9
Outputs:
- hidden_output: bfloat16 [512, 3584], P('replica', 'tensor')
The draws below stay inside these ranges and needn't reach their ends.
Inputs may be any that keep to these rules, and one draw needn't show every extreme that they name: `owner_replica`: among the 64 requests of one replica, no owner replica is named more than 16 times.
All inputs are finite; a program needn't handle non-finite values.
Results may differ from the reference program's by a relative error of at most 0.0048.
Values may be sent and summed in bfloat16 or wider, within the bound.
No kernel may reach another device: no remote copies, remote signals or barrier semaphores. Data moves between devices by JAX's collectives and lax.ppermute only.
A program may use at most 128 MiB of HBM per device.

```python
import math
import jax
import jax.numpy as jnp
import numpy as np
from jax import lax

D = 3584
HD = 256
QH = 8
KVH = 4
P_SIZE = 2048
S = 64
REQ_DEV = 64
G_DEV = 4
CAP = 16
REQUESTS = 512
GROUPS = 32
N_REPLICA = 8


def shared_direction(key):
    signs = jax.random.bernoulli(jax.random.fold_in(key, 7), 0.5, (KVH, HD))
    return jnp.where(signs, jnp.float32(1.0), jnp.float32(-1.0))


def background_draw(key, shape):
    return jnp.clip(jax.random.normal(key, shape, jnp.float32), -6.0, 6.0)


def draw_queries(key, part):
    direction = shared_direction(key)
    background = background_draw(jax.random.fold_in(key, 11), (REQUESTS, QH, HD))
    chosen = jax.random.randint(jax.random.fold_in(key, 13), (REQUESTS, 1, 1), 0, 4) == 0
    strength = jax.random.uniform(jax.random.fold_in(key, 17), (REQUESTS, QH, 1), jnp.float32, 8.0, 10.0) / HD ** 0.25
    head_index = jnp.arange(QH) // (QH // KVH)
    head_direction = direction[head_index]
    aligned = strength * head_direction[None, :, :]
    result = jnp.where(chosen, aligned, background)
    return result.reshape(REQUESTS, QH * HD).astype(jnp.bfloat16)


def draw_prompt_cache(key, part):
    direction = shared_direction(key)
    background = background_draw(jax.random.fold_in(key, 19), (GROUPS, 2, P_SIZE, KVH, HD))
    special_spots = jax.random.randint(jax.random.fold_in(key, 23), (GROUPS, 3), 0, max(P_SIZE // 8, 1))
    positions = jnp.arange(P_SIZE)
    special = jnp.any(positions[None, None, :] == special_spots[:, :, None], axis=1)
    strength = jax.random.uniform(jax.random.fold_in(key, 29), (GROUPS, P_SIZE, KVH, 1), jnp.float32, 8.0, 14.0) / HD ** 0.25
    aligned = strength * direction[None, None, :, :]
    key_part = jnp.where(special[:, :, None, None], aligned, background[:, 0])
    value_part = background[:, 1]
    result = jnp.stack([key_part, value_part], axis=1)
    return result.reshape(GROUPS, 2, P_SIZE, KVH * HD).astype(jnp.bfloat16)


def plant(values, rng, low, high):
    place = [jax.random.randint(jax.random.fold_in(rng, axis), (), 0, length) for axis, length in enumerate(values.shape)]
    longest = values.shape.index(max(values.shape))
    beside = place[:longest] + [(place[longest] + 1) % values.shape[longest]] + place[longest + 1:]
    return values.at[tuple(place)].set(low).at[tuple(beside)].set(high)


def strengthened(entries, own_key, source, target, blocks, factor):
    def block_of(position):
        return (jnp.arange(entries.shape[position]) // (entries.shape[position] // blocks)).reshape((-1,) + (1,) * (entries.ndim - 1 - position))

    one_side = jax.random.permutation(own_key, blocks)[block_of(target)]
    second = (block_of(target) + blocks // 2) % blocks
    return jnp.where((block_of(source) == one_side) | (block_of(source) == second), factor * entries, entries)


def level_of(stream_key, extent, pieces, low, largest):
    level, own = 1.0, jax.random.fold_in(stream_key, 6)
    for position, blocks in pieces:
        draws = jnp.exp(jax.random.uniform(jax.random.fold_in(own, position), (blocks,), jnp.float32, low / len(pieces), largest / len(pieces)))
        level = level * jnp.repeat(draws, extent[position] // blocks).reshape([-1 if axis == position else 1 for axis in range(len(extent))])
    return level


def shared_out(own_key, own, number, rows, number_of, top, reach, slope):
    ranking = jax.random.permutation(own_key, number_of)
    heavy_load, ordinary = portions_of(number_of, rows * top, reach, slope, True), portions_of(number_of, rows * top, reach, slope, False)
    places = jnp.arange(number_of)

    def named(tallies, rotation):
        used = int((tallies > 0).sum())
        fixed = max(1, used // 4)
        passed = fixed + (places - fixed + rotation * (used - fixed)) % max(1, number_of - fixed)
        return jnp.zeros((number_of,), jnp.int32).at[ranking[jnp.where(places < fixed, places, passed)]].set(jnp.asarray(tallies, jnp.int32))

    tallies = jnp.where(number % 4 == 0, named(heavy_load, number // 4), named(ordinary, number - number // 4 - 1))
    mixed = jax.random.permutation(jax.random.fold_in(own, 3), number_of)
    giver, taker = mixed[0:number_of // 2 * 2:2], mixed[1:number_of // 2 * 2:2]
    slack = jnp.minimum(tallies[giver] - 1, reach - tallies[taker]) // 2
    slack = jnp.where((giver == ranking[0]) | (taker == ranking[0]) | (tallies[taker] == 0), 0, jnp.maximum(slack, 0))
    passed = jax.random.randint(jax.random.fold_in(own, 4), (number_of // 2,), 0, 1 << 20) % (slack + 1)
    tallies = tallies.at[giver].add(-passed).at[taker].add(passed)
    items = jnp.searchsorted(jnp.cumsum(tallies), jnp.arange(rows * top), side="right").astype(jnp.int32)
    table = items.reshape(top, rows).T
    table = table[jax.random.permutation(jax.random.fold_in(own, 1), rows)]
    rotation = jax.random.randint(jax.random.fold_in(own, 2), (rows, 1), 0, top)
    return jnp.take_along_axis(table, (jnp.arange(top)[None, :] + rotation) % top, axis=1)


def portions_of(count, total, limit, skew, full):
    portions = [(1 << 20) // math.isqrt(rank ** skew) + 1 for rank in range(1, count + 1)]
    largest = limit if full else min(limit, max(-(-total // count), total * portions[0] // sum(portions)))
    least = 1 if total - largest >= count - 1 else 0
    holding, rest = [largest] + [least] * (count - 1), total - largest - least * (count - 1)
    while rest > 0:
        movable = [i for i in range(1, count) if holding[i] < largest] or [i for i in range(1, count) if holding[i] < limit]
        whole, remaining = sum([portions[i] for i in movable]), rest
        for i in movable:
            addition = min(limit - holding[i], max(1, remaining * portions[i] // whole), rest)
            holding[i] = holding[i] + addition
            rest = rest - addition
    return np.array(holding)


def scatter_about(rng, extent, deviation, limit, split=(), held_as=jnp.bfloat16):
    level = level_of(rng, extent, split, -0.22, 0.18) if split else 1.0
    entries = jax.random.normal(rng, extent, jnp.float32) * deviation * level
    return jnp.minimum(jnp.maximum(entries, -limit), limit).astype(held_as)


def gaussian_with(own_key, shape, spread, reach, pieces, heavy, kind=jnp.bfloat16):
    entries = spread * jax.random.normal(own_key, shape, jnp.float32)
    if pieces:
        entries = entries * level_of(own_key, shape, pieces, -0.22, 0.18)
    return jnp.clip(strengthened(entries, jax.random.fold_in(own_key, 3), *heavy), -reach, reach).astype(kind)


def setup_inputs(seed: int = 0) -> dict:
    keys = jax.random.split(jax.random.key(seed), 11)
    hidden_input = scatter_about(keys[0], (REQUESTS, D), 1.0, 6.0, ((0, 8), (1, 4)))
    queries = draw_queries(jax.random.fold_in(keys[10], 71), 0)
    prompt_cache = draw_prompt_cache(jax.random.fold_in(keys[10], 71), 0)
    suffix_cache = scatter_about(keys[3], (REQUESTS, 2, S, KVH * HD), 1.0, 6.0, ((0, 8), (3, 4)))
    owner_replica_keys = jax.random.split(jax.random.fold_in(keys[4], 1), REQUESTS // REQ_DEV)
    owner_replica_turns = jax.random.permutation(jax.random.fold_in(keys[4], 3), REQUESTS // REQ_DEV)
    owner_replica = jax.vmap(lambda own, number: shared_out(jax.random.fold_in(keys[4], 2), own, number, REQ_DEV, N_REPLICA, 1, CAP, 2))(owner_replica_keys, owner_replica_turns).reshape((REQUESTS, 1))
    group_slot = plant(jax.random.randint(keys[5], (REQUESTS,), 0, G_DEV), jax.random.fold_in(keys[5], 1), 0, G_DEV - 1).astype(jnp.int32)
    prompt_length = plant(jax.random.randint(keys[6], (GROUPS,), P_SIZE // 8, P_SIZE + 1), jax.random.fold_in(keys[6], 1), P_SIZE // 8, P_SIZE).astype(jnp.int32)
    suffix_length = plant(jax.random.randint(keys[7], (REQUESTS,), 1, S + 1), jax.random.fold_in(keys[7], 1), 1, S).astype(jnp.int32)
    output_weight = gaussian_with(keys[8], (QH * HD, D), (QH * HD) ** -0.5, 0.1875, ((0, 4),), (0, 1, 4, 2.0))
    post_gain = jnp.clip(1.0 + 0.18 * jax.random.normal(keys[9], (D,), jnp.float32), 0.1, 1.9)
    return {"hidden_input": hidden_input, "queries": queries, "prompt_cache": prompt_cache, "suffix_cache": suffix_cache, "owner_replica": owner_replica, "group_slot": group_slot, "prompt_length": prompt_length, "suffix_length": suffix_length, "output_weight": output_weight, "post_gain": post_gain}


softcap = 50.0
epsilon = 1e-06

def partial_attend(heads, cache_rows, live_length, head_map):
    window = cache_rows.shape[1]
    key_rows = cache_rows[0].astype(jnp.float32).reshape(window, KVH, HD)[:, head_map]
    value_rows = cache_rows[1].astype(jnp.float32).reshape(window, KVH, HD)[:, head_map]
    scores = jnp.einsum('hd,whd->hw', heads, key_rows) * HD ** (-0.5)
    capped = softcap * jnp.tanh(scores / softcap)
    positions = jnp.arange(window).astype(jnp.int32)
    weights = jnp.where(positions[None, :] < live_length, jnp.exp(capped), jnp.float32(0.0))
    rounded = weights.astype(jnp.bfloat16).astype(jnp.float32)
    numerator = jnp.einsum('hw,whd->hd', rounded, value_rows)
    return (numerator, lax.optimization_barrier(jnp.sum(weights, axis=-1)))

def reference(hidden_input, queries, prompt_cache, suffix_cache, owner_replica, group_slot, prompt_length, suffix_length, output_weight, post_gain):
    head_map = (jnp.arange(QH) // (QH // KVH)).astype(jnp.int32)

    def attend_one(inputs):
        query_row, own_cache, owner_index, slot_index, own_length = inputs
        group_index = (owner_index * G_DEV + slot_index).astype(jnp.int32)
        shared = lax.dynamic_index_in_dim(prompt_cache, group_index, 0, keepdims=False)
        live_length = lax.dynamic_index_in_dim(prompt_length, group_index, 0, keepdims=False)
        heads = query_row.astype(jnp.float32).reshape(QH, HD)
        prompt_num, prompt_den = partial_attend(heads, shared, live_length, head_map)
        own_num, own_den = partial_attend(heads, own_cache, own_length, head_map)
        mixed = (prompt_num + own_num) / (prompt_den + own_den)[:, None]
        return mixed.reshape(QH * HD).astype(jnp.bfloat16)
    attention = lax.map(attend_one, (queries, suffix_cache, owner_replica[:, 0], group_slot, suffix_length))
    projected = jnp.dot(attention, output_weight, preferred_element_type=jnp.float32)
    mean_square = lax.optimization_barrier(jnp.mean(projected * projected, axis=-1, keepdims=True))
    normed = projected * lax.rsqrt(mean_square + epsilon) * post_gain[None, :]
    return (hidden_input.astype(jnp.float32) + normed).astype(jnp.bfloat16)
```

```python
import functools
import math

import jax
import jax.numpy as jnp
from jax import lax
from jax.experimental import pallas as pl
from jax.experimental.pallas import tpu as pltpu
from jax.sharding import PartitionSpec as P

HD = 256
softcap = 50.0
epsilon = 1e-06
score_scale = 1.0 / (softcap * math.sqrt(HD))
weight_scale = softcap * math.log2(math.e)
EXTRA = 128
f32 = jnp.float32
bf16 = jnp.bfloat16
VMEM = pltpu.MemorySpace.VMEM
SMEM = pltpu.MemorySpace.SMEM


def iota(shape, axis):
    return lax.broadcasted_iota(jnp.int32, shape, axis)


def heads_below(block, heads):
    return jnp.concatenate([block[:, h * HD : (h + 1) * HD] for h in range(heads)], axis=0)


def weights_of(scores, alive):
    return jnp.where(alive, jnp.exp2(weight_scale * jnp.tanh(scores * score_scale)), 0.0)


def owners(owner_ref):
    requests = owner_ref.shape[0]
    rows, cols = iota((requests, requests), 0), iota((requests, requests), 1)
    by_row = jnp.broadcast_to(owner_ref[...], (requests, requests)).astype(f32)
    by_col = jnp.sum(jnp.where(rows == cols, by_row, 0.0), axis=0, keepdims=True)
    return by_row, by_col, rows, cols


def route_kernel(capacity, owner_ref, group_ref, queries_ref, out_ref):
    requests, width = queries_ref.shape
    slots = out_ref.shape[0]
    by_row, by_col, rows, cols = owners(owner_ref)
    earlier = jnp.where((by_row == by_col) & (rows < cols), 1.0, 0.0)
    position = (by_col * capacity + jnp.sum(earlier, axis=0, keepdims=True)).astype(jnp.int32)
    matches = iota((slots, requests), 0) == position
    out_ref[:, :width] = jnp.dot(
        jnp.where(matches, 1.0, 0.0).astype(bf16), queries_ref[...], preferred_element_type=f32
    ).astype(bf16)
    numbered = (group_ref[...] + 1).astype(f32)
    mark = jnp.sum(jnp.where(matches, numbered, 0.0), axis=1, keepdims=True)
    out_ref[:, width:] = jnp.broadcast_to(mark, (slots, EXTRA)).astype(bf16)


def suffix_kernel(
    capacity, owner_ref, length_ref, queries_ref, cache_ref, back_ref, num_ref, den_ref
):
    requests, slots = back_ref.shape
    block, _, window, _ = cache_ref.shape
    heads = queries_ref.shape[1] // HD

    @pl.when(pl.program_id(0) == 0)
    def _():
        by_row, by_col, rows, cols = owners(owner_ref)
        earlier = jnp.where((by_row == by_col) & (cols < rows), 1.0, 0.0)
        rank = jnp.sum(earlier, axis=1, keepdims=True).astype(jnp.int32)
        position = owner_ref[...] * capacity + rank
        back_ref[...] = jnp.where(iota((requests, slots), 1) == position, 1.0, 0.0).astype(bf16)

    stacked = heads_below(queries_ref[...], heads)
    keys = cache_ref[:, 0].reshape(block * window, HD)
    values = cache_ref[:, 1].reshape(block * window, HD)
    scores = lax.dot_general(
        stacked, keys, (((1,), (1,)), ((), ())), preferred_element_type=f32
    )
    cols = iota((block, block * window), 1)
    first = iota((block, block * window), 0) * window
    alive = (cols >= first) & (cols < first + length_ref[...])
    weights = weights_of(scores, jnp.concatenate([alive] * heads, axis=0))
    numerator = jnp.dot(weights.astype(bf16), values, preferred_element_type=f32)
    denominator = jnp.sum(weights, axis=1, keepdims=True)
    for h in range(heads):
        mine = slice(h * block, (h + 1) * block)
        num_ref[:, h * HD : (h + 1) * HD] = numerator[mine]
        den_ref[:, h * 128 : (h + 1) * 128] = jnp.broadcast_to(denominator[mine], (block, 128))


def prompt_kernel(chunk, length_ref, slots_ref, cache_ref, out_ref, held, num, den, sems):
    groups, _, size, _ = cache_ref.shape
    slots = slots_ref.shape[0]
    width = slots_ref.shape[1] - EXTRA
    heads = width // HD
    rows = heads * slots
    chunks = size // chunk

    def copy(g, c, part):
        span = pl.ds(c * chunk, chunk)
        return pltpu.make_async_copy(
            cache_ref.at[g, part, span, :], held.at[g, part, span, :], sems.at[g, c, part]
        )

    for g in range(groups):
        for c in range(chunks):

            @pl.when(c * chunk < length_ref[g])
            def _():
                copy(g, c, 0).start()
                copy(g, c, 1).start()

    stacked = heads_below(slots_ref[:, :width], heads)
    mark = slots_ref[:, width : width + 1].astype(f32)
    mark = jnp.concatenate([mark] * heads, axis=0)
    num[...] = jnp.zeros_like(num)
    den[...] = jnp.zeros_like(den)
    for g in range(groups):
        limit = jnp.where(mark == g + 1.0, length_ref[g], 0)

        def step(c, carry):
            copy(g, c, 0).wait()
            span = pl.ds(pl.multiple_of(c * chunk, chunk), chunk)
            scores = lax.dot_general(
                stacked, held[g, 0, span, :], (((1,), (1,)), ((), ())), preferred_element_type=f32
            )
            alive = iota((rows, chunk), 1) < limit - c * chunk
            weights = weights_of(scores, alive)
            copy(g, c, 1).wait()
            num[...] += jnp.dot(
                weights.astype(bf16), held[g, 1, span, :], preferred_element_type=f32
            )
            part = weights[:, :128]
            for k in range(1, chunk // 128):
                part = part + weights[:, k * 128 : (k + 1) * 128]
            den[...] += part
            return carry

        lax.fori_loop(0, (length_ref[g] + chunk - 1) // chunk, step, 0)

    total = jnp.sum(den[...], axis=1, keepdims=True)
    lanes = iota((slots, EXTRA), 1)
    extra = jnp.zeros((slots, EXTRA), f32)
    for h in range(heads):
        out_ref[:, h * HD : (h + 1) * HD] = num[h * slots : (h + 1) * slots].astype(bf16)
        rest = total[h * slots : (h + 1) * slots]
        for k in range(3):
            piece = rest.astype(bf16).astype(f32)
            rest = rest - piece
            extra = jnp.where(lanes == 3 * h + k, piece, extra)
    out_ref[:, width:] = extra.astype(bf16)


def quarters(weight_ref, attention, first, second):
    width = weight_ref.shape[1] // 4
    out = []
    for q in (first, second):
        cols = pl.ds(pl.multiple_of(q * width, 128), width)
        out.append(jnp.dot(attention, weight_ref[:, cols], preferred_element_type=f32))
    return out


def combine_kernel(core_ref, returned_ref, back_ref, num_ref, den_ref, weight_ref, att_ref, give_ref):
    width = num_ref.shape[1]
    heads = width // HD
    other = 1 - core_ref[0]
    mine = jnp.dot(back_ref[...], returned_ref[...], preferred_element_type=f32)
    for h in range(heads):
        cols = slice(h * HD, (h + 1) * HD)
        numerator = mine[:, cols] + num_ref[:, cols]
        at = width + 3 * h
        denominator = den_ref[:, h * 128 : h * 128 + 1] + (
            mine[:, at : at + 1] + mine[:, at + 1 : at + 2] + mine[:, at + 2 : at + 3]
        )
        att_ref[:, cols] = (numerator / denominator).astype(bf16)
    a, b = quarters(weight_ref, att_ref[...], other, other + 2)
    half = a.shape[1]
    give_ref[:, :half] = a.astype(bf16)
    give_ref[:, half:] = b.astype(bf16)


def own_kernel(core_ref, att_ref, weight_ref, own_ref):
    a, b = quarters(weight_ref, att_ref[...], core_ref[0], core_ref[0] + 2)
    half = a.shape[1]
    own_ref[:, :half] = a
    own_ref[:, half:] = b


def chip_kernel(own_ref, got_ref, sum_ref, send_ref):
    total = own_ref[...] + got_ref[...].astype(f32)
    sum_ref[...] = total
    send_ref[...] = total.astype(bf16)


def square_kernel(row_ref, sum_ref, got_ref, mine_ref, square_ref):
    width = mine_ref.shape[1]
    total = sum_ref[...] + got_ref[...].astype(f32)
    part = jnp.zeros(square_ref.shape, f32)
    for k in range(total.shape[1] // 128):
        piece = total[:, k * 128 : (k + 1) * 128]
        part = part + piece * piece
    square_ref[...] = part
    mine_ref[...] = jnp.where(row_ref[0] == 0, total[:, :width], total[:, width:])


def final_kernel(features, mine_ref, square_ref, got_ref, gain_ref, hidden_ref, out_ref):
    square = jnp.sum(square_ref[...] + got_ref[...], axis=1, keepdims=True)
    scale = lax.rsqrt(square * (1.0 / features) + epsilon)
    normed = mine_ref[...] * scale * gain_ref[...]
    out_ref[...] = (hidden_ref[...].astype(f32) + normed).astype(bf16)


def call(kernel, outs, ins, **kw):
    specs = [
        pl.BlockSpec(memory_space=SMEM if a.ndim == 1 else VMEM) for a in ins
    ]
    return pl.pallas_call(
        kernel,
        out_shape=outs,
        in_specs=specs,
        out_specs=jax.tree.map(lambda _: pl.BlockSpec(memory_space=VMEM), outs),
        compiler_params=pltpu.CompilerParams(vmem_limit_bytes=40 * 2**20),
        **kw,
    )(*ins)


def shape(dims, dtype):
    return jax.ShapeDtypeStruct(dims, dtype)


def shards(
    hidden_input,
    queries,
    prompt_cache,
    suffix_cache,
    owner_replica,
    group_slot,
    prompt_length,
    suffix_length,
    output_weight,
    post_gain,
):
    replicas = lax.axis_size("replica")
    ranks = lax.axis_size("tensor")
    requests, width = queries.shape
    capacity = max(2, (2 * requests + replicas - 1) // replicas)
    slots = replicas * capacity
    groups, _, size, _ = prompt_cache.shape
    window = suffix_cache.shape[2]
    features = output_weight.shape[1]
    quarter = features // ranks
    heads = width // HD
    index = lax.axis_index("tensor")
    core = (index % 2).reshape(1)
    row = (index // 2).reshape(1)

    def exchange(x):
        blocks = x.reshape(replicas, capacity, width + EXTRA)
        blocks = lax.all_to_all(blocks, "replica", split_axis=0, concat_axis=0, tiled=True)
        return blocks.reshape(slots, width + EXTRA)

    def permute(x, bit):
        return lax.ppermute(x, "tensor", [(i, i ^ bit) for i in range(ranks)])

    sent = call(
        functools.partial(route_kernel, capacity),
        shape((slots, width + EXTRA), bf16),
        [owner_replica, group_slot.reshape(1, requests), queries],
    )
    got = exchange(sent)

    block = 16
    back, own_num, own_den = pl.pallas_call(
        functools.partial(suffix_kernel, capacity),
        out_shape=[
            shape((requests, slots), bf16),
            shape((requests, width), f32),
            shape((requests, heads * 128), f32),
        ],
        grid=(requests // block,),
        in_specs=[
            pl.BlockSpec((requests, 1), lambda i: (0, 0)),
            pl.BlockSpec((block, 1), lambda i: (i, 0)),
            pl.BlockSpec((block, width), lambda i: (i, 0)),
            pl.BlockSpec((block, 2, window, HD), lambda i: (i, 0, 0, 0)),
        ],
        out_specs=[
            pl.BlockSpec((requests, slots), lambda i: (0, 0)),
            pl.BlockSpec((block, width), lambda i: (i, 0)),
            pl.BlockSpec((block, heads * 128), lambda i: (i, 0)),
        ],
        compiler_params=pltpu.CompilerParams(vmem_limit_bytes=40 * 2**20),
        cost_estimate=pl.CostEstimate(
            flops=8 * requests * window * HD * block,
            bytes_accessed=suffix_cache.size * 2,
            transcendentals=0,
        ),
    )(owner_replica, suffix_length.reshape(requests, 1), queries, suffix_cache)

    chunk = math.gcd(512, size)
    answered = pl.pallas_call(
        functools.partial(prompt_kernel, chunk),
        out_shape=shape((slots, width + EXTRA), bf16),
        in_specs=[
            pl.BlockSpec(memory_space=SMEM),
            pl.BlockSpec(memory_space=VMEM),
            pl.BlockSpec(memory_space=pl.ANY),
        ],
        out_specs=pl.BlockSpec(memory_space=VMEM),
        scratch_shapes=[
            pltpu.VMEM(prompt_cache.shape, bf16),
            pltpu.VMEM((heads * slots, HD), f32),
            pltpu.VMEM((heads * slots, 128), f32),
            pltpu.SemaphoreType.DMA((groups, size // chunk, 2)),
        ],
        compiler_params=pltpu.CompilerParams(vmem_limit_bytes=40 * 2**20),
    )(prompt_length, got, prompt_cache)
    returned = exchange(answered)

    attention, give = call(
        combine_kernel,
        [shape((requests, width), bf16), shape((requests, 2 * quarter), bf16)],
        [core, returned, back, own_num, own_den, output_weight],
    )
    received = permute(give, 1)
    own = call(own_kernel, shape((requests, 2 * quarter), f32), [core, attention, output_weight])
    chip, send = call(
        chip_kernel,
        [shape((requests, 2 * quarter), f32), shape((requests, 2 * quarter), bf16)],
        [own, received],
    )
    far = permute(send, 2)
    mine, square = call(
        square_kernel,
        [shape((requests, quarter), f32), shape((requests, 128), f32)],
        [row, chip, far],
    )
    beside = permute(square, 1)
    return call(
        functools.partial(final_kernel, features),
        shape((requests, quarter), bf16),
        [mine, square, beside, post_gain.reshape(1, quarter), hidden_input],
    )


def solution(mesh):
    in_specs = (
        P("replica", "tensor"),
        P("replica", "tensor"),
        P("replica", None, None, "tensor"),
        P("replica", None, None, "tensor"),
        P("replica", None),
        P("replica"),
        P("replica"),
        P("replica"),
        P("tensor", None),
        P("tensor"),
    )
    out_specs = P("replica", "tensor")
    return jax.shard_map(shards, mesh=mesh, in_specs=in_specs, out_specs=out_specs, check_vma=False)
```

```python
import functools
import math

import jax
import jax.numpy as jnp
from jax import lax
from jax.experimental import pallas as pl
from jax.experimental.pallas import tpu as pltpu
from jax.sharding import PartitionSpec as P

HD = 256
softcap = 50.0
epsilon = 1e-06
score_scale = 1.0 / (softcap * math.sqrt(HD))
weight_scale = softcap * math.log2(math.e)
EXTRA = 128
f32 = jnp.float32
bf16 = jnp.bfloat16
VMEM = pltpu.MemorySpace.VMEM
SMEM = pltpu.MemorySpace.SMEM
VMEM_SPEC = pl.BlockSpec(memory_space=VMEM)
SMEM_SPEC = pl.BlockSpec(memory_space=SMEM)
HBM_SPEC = pl.BlockSpec(memory_space=pltpu.MemorySpace.HBM)
PARAMS = pltpu.CompilerParams(vmem_limit_bytes=40 * 2**20)


def iota(shape, axis):
    return lax.broadcasted_iota(jnp.int32, shape, axis)


def heads_below(block, heads):
    return jnp.concatenate([block[:, h * HD : (h + 1) * HD] for h in range(heads)], axis=0)


def weights_of(scores, alive):
    return jnp.where(alive, jnp.exp2(weight_scale * jnp.tanh(scores * score_scale)), 0.0)


def owners(owner_ref):
    requests = owner_ref.shape[1]
    rows, cols = iota((requests, requests), 0), iota((requests, requests), 1)
    by_col = jnp.broadcast_to(owner_ref[...], (requests, requests)).astype(f32)
    by_row = jnp.sum(jnp.where(rows == cols, by_col, 0.0), axis=1, keepdims=True)
    return by_row, by_col, rows, cols


def route_kernel(
    capacity, owner_hbm, group_hbm, queries_hbm, out_ref, owner_ref, group_ref, queries_ref, sems
):
    pairs = ((owner_hbm, owner_ref), (group_hbm, group_ref), (queries_hbm, queries_ref))
    copies = [pltpu.make_async_copy(a, b, sems.at[i]) for i, (a, b) in enumerate(pairs)]
    for copy in copies:
        copy.start()
    for copy in copies:
        copy.wait()
    requests, width = queries_ref.shape
    slots = out_ref.shape[0]
    by_row, by_col, rows, cols = owners(owner_ref)
    earlier = jnp.where((by_row == by_col) & (rows < cols), 1.0, 0.0)
    position = (by_col[:1] * capacity + jnp.sum(earlier, axis=0, keepdims=True)).astype(jnp.int32)
    matches = iota((slots, requests), 0) == position
    out_ref[:, :width] = jnp.dot(
        jnp.where(matches, 1.0, 0.0).astype(bf16), queries_ref[...], preferred_element_type=f32
    ).astype(bf16)
    numbered = (group_ref[...] + 1).astype(f32)
    mark = jnp.sum(jnp.where(matches, numbered, 0.0), axis=1, keepdims=True)
    out_ref[:, width:] = jnp.broadcast_to(mark, (slots, EXTRA)).astype(bf16)


def suffix_kernel(
    capacity,
    block,
    owner_hbm,
    length_hbm,
    queries_hbm,
    cache_hbm,
    core_ref,
    weight_hbm,
    after_hbm,
    back_ref,
    num_ref,
    den_ref,
    weight_ref,
    owner_ref,
    length_ref,
    queries_ref,
    cache_ref,
    sems,
    cache_sems,
    weight_sems,
):
    requests, slots = back_ref.shape
    window = cache_ref.shape[2]
    heads = queries_ref.shape[1] // HD
    steps = requests // block
    pairs = ((owner_hbm, owner_ref), (length_hbm, length_ref), (queries_hbm, queries_ref))
    copies = [pltpu.make_async_copy(a, b, sems.at[i]) for i, (a, b) in enumerate(pairs)]
    parts = []
    for i in range(steps):
        span = pl.ds(i * block, block)
        parts.append(
            pltpu.make_async_copy(cache_hbm.at[span], cache_ref.at[span], cache_sems.at[i])
        )
    quarter = weight_ref.shape[2]
    weight_copies = []
    for i, q in enumerate((1 - core_ref[0], 3 - core_ref[0], core_ref[0])):
        cols = pl.ds(pl.multiple_of(q * quarter, 128), quarter)
        weight_copies.append(
            pltpu.make_async_copy(weight_hbm.at[:, cols], weight_ref.at[i], weight_sems.at[i])
        )
    for copy in copies + parts + weight_copies:
        copy.start()
    for copy in copies:
        copy.wait()

    by_row, by_col, rows, cols = owners(owner_ref)
    earlier = jnp.where((by_row == by_col) & (cols < rows), 1.0, 0.0)
    rank = jnp.sum(earlier, axis=1, keepdims=True)
    position = (by_row * capacity + rank).astype(jnp.int32)
    back_ref[...] = jnp.where(iota((requests, slots), 1) == position, 1.0, 0.0).astype(bf16)
    live = jnp.sum(
        jnp.where(rows == cols, length_ref[...].astype(f32), 0.0), axis=1, keepdims=True
    ).astype(jnp.int32)

    at = iota((block, block * window), 1)
    first = iota((block, block * window), 0) * window
    for i in range(steps):
        mine = slice(i * block, (i + 1) * block)
        parts[i].wait()
        stacked = heads_below(queries_ref[mine, :], heads)
        keys = cache_ref[mine, 0].reshape(block * window, HD)
        values = cache_ref[mine, 1].reshape(block * window, HD)
        scores = lax.dot_general(
            stacked, keys, (((1,), (1,)), ((), ())), preferred_element_type=f32
        )
        alive = (at >= first) & (at < first + live[mine])
        weights = weights_of(scores, jnp.concatenate([alive] * heads, axis=0))
        numerator = jnp.dot(weights.astype(bf16), values, preferred_element_type=f32)
        denominator = jnp.sum(weights, axis=1, keepdims=True)
        for h in range(heads):
            own = slice(h * block, (h + 1) * block)
            num_ref[mine, h * HD : (h + 1) * HD] = numerator[own]
            den_ref[mine, h * 128 : (h + 1) * 128] = jnp.broadcast_to(
                denominator[own], (block, 128)
            )
    for copy in weight_copies:
        copy.wait()


def prefetch_kernel(cache_hbm, early_ref, sems):
    parts = parts_of(cache_hbm.shape[0])
    copies = [
        pltpu.make_async_copy(cache_hbm.at[parts[i]], early_ref.at[i], sems.at[i])
        for i in range(early_ref.shape[0])
    ]
    for copy in copies:
        copy.start()
    for copy in copies:
        copy.wait()


def parts_of(groups):
    return [(g, part) for g in range(groups) for part in range(2)]


def prompt_kernel(
    chunk,
    window,
    length_hbm,
    slots_ref,
    early_ref,
    cache_hbm,
    out_ref,
    length_ref,
    held,
    sorted_ref,
    done_ref,
    num_ref,
    den_ref,
    sems,
    length_sem,
):
    groups, _, size, _ = cache_hbm.shape
    slots = slots_ref.shape[0]
    width = slots_ref.shape[1] - EXTRA
    heads = width // HD
    parts = parts_of(groups)
    early = early_ref.shape[0]
    length_copy = pltpu.make_async_copy(length_hbm, length_ref, length_sem)
    length_copy.start()
    copies = {
        parts[i]: pltpu.make_async_copy(
            cache_hbm.at[parts[i]], held.at[i - early], sems.at[i - early]
        )
        for i in range(early, len(parts))
    }
    for part in parts[early:]:
        copies[part].start()

    def wait(g, part):
        if (g, part) in copies:
            copies[g, part].wait()

    def read(g, part, span):
        i = parts.index((g, part))
        return early_ref[i, span, :] if i < early else held[i - early, span, :]

    def pieces(total, rows):
        lanes = iota((1, EXTRA), 1)
        extra = jnp.zeros((rows, EXTRA), f32)
        for h in range(heads):
            rest = total[h * rows : (h + 1) * rows]
            for k in range(3):
                piece = rest.astype(bf16).astype(f32)
                rest = rest - piece
                extra = jnp.where(lanes == 3 * h + k, piece, extra)
        return extra.astype(bf16)

    def fold(weights):
        part = weights[:, :128]
        for k in range(1, weights.shape[1] // 128):
            part = part + weights[:, k * 128 : (k + 1) * 128]
        return part

    rows, cols = iota((slots, slots), 0), iota((slots, slots), 1)
    by_row = jnp.broadcast_to(slots_ref[:, width : width + 1].astype(f32), (slots, slots))
    by_col = jnp.sum(jnp.where(rows == cols, by_row, 0.0), axis=0, keepdims=True)
    same = by_row == by_col
    rank_row = jnp.sum(jnp.where(same & (cols < rows), 1.0, 0.0), axis=1, keepdims=True)
    rank_col = jnp.sum(jnp.where(same & (rows < cols), 1.0, 0.0), axis=0, keepdims=True)
    length_copy.wait()
    crowded = jnp.max(jnp.where(by_col > 0.0, rank_col, 0.0)) >= window

    @pl.when(jnp.logical_not(crowded))
    def _():
        at_row = (by_row[:, :1] - 1.0) * window + rank_row
        at_col = jnp.where(by_col > 0.0, (by_col - 1.0) * window + rank_col, -1.0)
        at_row = jnp.where(by_row[:, :1] > 0.0, at_row, -1.0).astype(jnp.int32)
        room = groups * window
        there = jnp.where(iota((room, slots), 0) == at_col.astype(jnp.int32), 1.0, 0.0)
        back = jnp.where(iota((slots, room), 1) == at_row, 1.0, 0.0)
        sorted_ref[...] = jnp.dot(
            there.astype(bf16), slots_ref[:, :width], preferred_element_type=f32
        ).astype(bf16)
        nums, dens, scores = [None] * groups, [None] * groups, [None] * groups
        everything = slice(0, size)
        for u in range(groups + 1):
            if u < groups:
                wait(u, 0)
                stacked = heads_below(sorted_ref[u * window : (u + 1) * window, :], heads)
                scores[u] = lax.dot_general(
                    stacked,
                    read(u, 0, everything),
                    (((1,), (1,)), ((), ())),
                    preferred_element_type=f32,
                )
            if u > 0:
                g = u - 1
                weights = weights_of(scores[g], iota((1, size), 1) < length_ref[g])
                wait(g, 1)
                nums[g] = jnp.dot(
                    weights.astype(bf16), read(g, 1, everything), preferred_element_type=f32
                )
                dens[g] = fold(weights)
        for g in range(groups):
            mine = slice(g * window, (g + 1) * window)
            for h in range(heads):
                done_ref[mine, h * HD : (h + 1) * HD] = nums[g][
                    h * window : (h + 1) * window
                ].astype(bf16)
            done_ref[mine, width:] = pieces(jnp.sum(dens[g], axis=1, keepdims=True), window)
        out_ref[...] = jnp.dot(
            back.astype(bf16), done_ref[...], preferred_element_type=f32
        ).astype(bf16)

    @pl.when(crowded)
    def _():
        for part in parts:
            wait(*part)
        stacked = heads_below(slots_ref[:, :width], heads)
        mark = jnp.concatenate([by_row[:, :1]] * heads, axis=0)
        num_ref[...] = jnp.zeros_like(num_ref)
        den_ref[...] = jnp.zeros_like(den_ref)
        for g in range(groups):
            limit = jnp.where(mark == g + 1.0, length_ref[g], 0)

            @pl.loop(0, (length_ref[g] + chunk - 1) // chunk)
            def _(c):
                span = pl.ds(pl.multiple_of(c * chunk, chunk), chunk)
                scores = lax.dot_general(
                    stacked,
                    read(g, 0, span),
                    (((1,), (1,)), ((), ())),
                    preferred_element_type=f32,
                )
                alive = iota((heads * slots, chunk), 1) < limit - c * chunk
                weights = weights_of(scores, alive)
                num_ref[...] += jnp.dot(
                    weights.astype(bf16), read(g, 1, span), preferred_element_type=f32
                )
                den_ref[...] += fold(weights)

        for h in range(heads):
            out_ref[:, h * HD : (h + 1) * HD] = num_ref[h * slots : (h + 1) * slots].astype(bf16)
        out_ref[:, width:] = pieces(jnp.sum(den_ref[...], axis=1, keepdims=True), slots)


def combine_kernel(
    core_ref, returned_ref, back_ref, num_ref, den_ref, weight_ref, weight_hbm, att_ref, give_ref, last_ref, sem
):
    quarter = weight_ref.shape[2]
    cols = pl.ds(pl.multiple_of((core_ref[0] + 2) * quarter, 128), quarter)
    copy = pltpu.make_async_copy(weight_hbm.at[:, cols], last_ref, sem)
    copy.start()
    width = num_ref.shape[1]
    heads = width // HD
    mine = jnp.dot(back_ref[...], returned_ref[...], preferred_element_type=f32)
    for h in range(heads):
        cols = slice(h * HD, (h + 1) * HD)
        numerator = mine[:, cols] + num_ref[:, cols]
        at = width + 3 * h
        denominator = den_ref[:, h * 128 : h * 128 + 1] + (
            mine[:, at : at + 1] + mine[:, at + 1 : at + 2] + mine[:, at + 2 : at + 3]
        )
        att_ref[:, cols] = (numerator / denominator).astype(bf16)
    for i in range(2):
        give_ref[:, i * quarter : (i + 1) * quarter] = jnp.dot(
            att_ref[...], weight_ref[i], preferred_element_type=f32
        ).astype(bf16)
    copy.wait()


def own_kernel(att_ref, weight_ref, last_ref, own_ref):
    quarter = weight_ref.shape[2]
    own_ref[:, :quarter] = jnp.dot(att_ref[...], weight_ref[2], preferred_element_type=f32)
    own_ref[:, quarter:] = jnp.dot(att_ref[...], last_ref[...], preferred_element_type=f32)


def chip_kernel(own_ref, got_ref, sum_ref, send_ref):
    total = own_ref[...] + got_ref[...].astype(f32)
    sum_ref[...] = total
    send_ref[...] = total.astype(bf16)


def square_kernel(row_ref, sum_ref, got_ref, mine_ref, square_ref):
    width = mine_ref.shape[1]
    total = sum_ref[...] + got_ref[...].astype(f32)
    part = jnp.zeros(square_ref.shape, f32)
    for k in range(total.shape[1] // 128):
        piece = total[:, k * 128 : (k + 1) * 128]
        part = part + piece * piece
    square_ref[...] = part
    mine_ref[...] = jnp.where(row_ref[0] == 0, total[:, :width], total[:, width:])


def final_kernel(features, mine_ref, square_ref, got_ref, gain_ref, hidden_ref, out_ref):
    square = jnp.sum(square_ref[...] + got_ref[...], axis=1, keepdims=True)
    scale = lax.rsqrt(square * (1.0 / features) + epsilon)
    normed = mine_ref[...] * scale * gain_ref[...]
    out_ref[...] = (hidden_ref[...].astype(f32) + normed).astype(bf16)


def call(kernel, outs, ins, **kw):
    specs = [
        pl.BlockSpec(memory_space=SMEM if a.ndim == 1 else VMEM) for a in ins
    ]
    return pl.pallas_call(
        kernel,
        out_shape=outs,
        in_specs=specs,
        out_specs=jax.tree.map(lambda _: pl.BlockSpec(memory_space=VMEM), outs),
        compiler_params=PARAMS,
        **kw,
    )(*ins)


def in_hbm(*arrays):
    return [pltpu.with_memory_space_constraint(a, pltpu.MemorySpace.HBM) for a in arrays]


def shape(dims, dtype):
    return jax.ShapeDtypeStruct(dims, dtype)


def shards(
    hidden_input,
    queries,
    prompt_cache,
    suffix_cache,
    owner_replica,
    group_slot,
    prompt_length,
    suffix_length,
    output_weight,
    post_gain,
):
    replicas = lax.axis_size("replica")
    ranks = lax.axis_size("tensor")
    requests, width = queries.shape
    capacity = max(2, (2 * requests + replicas - 1) // replicas)
    slots = replicas * capacity
    groups, _, size, _ = prompt_cache.shape
    window = suffix_cache.shape[2]
    features = output_weight.shape[1]
    quarter = features // ranks
    heads = width // HD
    index = lax.axis_index("tensor")
    core = (index % 2).reshape(1)
    row = (index // 2).reshape(1)

    def exchange(x):
        blocks = x.reshape(replicas, capacity, width + EXTRA)
        blocks = lax.all_to_all(blocks, "replica", split_axis=0, concat_axis=0, tiled=True)
        return blocks.reshape(slots, width + EXTRA)

    def permute(x, bit):
        return lax.ppermute(x, "tensor", [(i, i ^ bit) for i in range(ranks)])

    owner_row = owner_replica.reshape(1, requests)
    sent = pl.pallas_call(
        functools.partial(route_kernel, capacity),
        out_shape=shape((slots, width + EXTRA), bf16),
        in_specs=[HBM_SPEC] * 3,
        out_specs=VMEM_SPEC,
        scratch_shapes=[
            pltpu.VMEM((1, requests), jnp.int32),
            pltpu.VMEM((1, requests), jnp.int32),
            pltpu.VMEM((requests, width), bf16),
            pltpu.SemaphoreType.DMA((3,)),
        ],
        compiler_params=PARAMS,
    )(*in_hbm(owner_row, group_slot.reshape(1, requests), queries))
    got = exchange(sent)

    early = 3
    prefetched = pl.pallas_call(
        prefetch_kernel,
        out_shape=pltpu.VMEM((early, size, HD), bf16),
        in_specs=[HBM_SPEC],
        out_specs=VMEM_SPEC,
        scratch_shapes=[pltpu.SemaphoreType.DMA((early,))],
        compiler_params=PARAMS,
        cost_estimate=pl.CostEstimate(
            flops=0, bytes_accessed=2 * early * size * HD * 2, transcendentals=0
        ),
    )(*in_hbm(prompt_cache))

    chunk = math.gcd(512, size)
    fit = min(48, slots)
    answered = pl.pallas_call(
        functools.partial(prompt_kernel, chunk, fit),
        out_shape=shape((slots, width + EXTRA), bf16),
        in_specs=[HBM_SPEC, VMEM_SPEC, VMEM_SPEC, HBM_SPEC],
        out_specs=VMEM_SPEC,
        scratch_shapes=[
            pltpu.SMEM((groups,), jnp.int32),
            pltpu.VMEM((2 * groups - early, size, HD), bf16),
            pltpu.VMEM((groups * fit, width), bf16),
            pltpu.VMEM((groups * fit, width + EXTRA), bf16),
            pltpu.VMEM((heads * slots, HD), f32),
            pltpu.VMEM((heads * slots, 128), f32),
            pltpu.SemaphoreType.DMA((2 * groups - early,)),
            pltpu.SemaphoreType.DMA,
        ],
        compiler_params=PARAMS,
    )(
        *in_hbm(prompt_length),
        got,
        pltpu.with_memory_space_constraint(prefetched, VMEM),
        *in_hbm(prompt_cache),
    )
    returned = exchange(answered)

    block = math.gcd(16, requests)
    back, own_num, own_den, weight = pl.pallas_call(
        functools.partial(suffix_kernel, capacity, block),
        out_shape=[
            shape((requests, slots), bf16),
            shape((requests, width), f32),
            shape((requests, heads * 128), f32),
            pltpu.VMEM((3, width, quarter), bf16),
        ],
        in_specs=[HBM_SPEC] * 4 + [SMEM_SPEC, HBM_SPEC, HBM_SPEC],
        out_specs=[VMEM_SPEC] * 4,
        scratch_shapes=[
            pltpu.VMEM((1, requests), jnp.int32),
            pltpu.VMEM((1, requests), jnp.int32),
            pltpu.VMEM((requests, width), bf16),
            pltpu.VMEM(suffix_cache.shape, bf16),
            pltpu.SemaphoreType.DMA((3,)),
            pltpu.SemaphoreType.DMA((requests // block,)),
            pltpu.SemaphoreType.DMA((3,)),
        ],
        compiler_params=PARAMS,
        cost_estimate=pl.CostEstimate(
            flops=8 * requests * window * HD * block,
            bytes_accessed=(suffix_cache.size + output_weight.size) * 2,
            transcendentals=0,
        ),
    )(
        *in_hbm(owner_row, suffix_length.reshape(1, requests), queries, suffix_cache),
        core,
        *in_hbm(output_weight, answered),
    )
    weight = pltpu.with_memory_space_constraint(weight, VMEM)

    attention, give, last = pl.pallas_call(
        combine_kernel,
        out_shape=[
            shape((requests, width), bf16),
            shape((requests, 2 * quarter), bf16),
            pltpu.VMEM((width, quarter), bf16),
        ],
        in_specs=[SMEM_SPEC] + [VMEM_SPEC] * 5 + [HBM_SPEC],
        out_specs=[VMEM_SPEC] * 3,
        scratch_shapes=[pltpu.SemaphoreType.DMA],
        compiler_params=PARAMS,
    )(core, returned, back, own_num, own_den, weight, *in_hbm(output_weight))
    received = permute(give, 1)
    own = call(
        own_kernel,
        shape((requests, 2 * quarter), f32),
        [attention, weight, pltpu.with_memory_space_constraint(last, VMEM)],
    )
    chip, send = call(
        chip_kernel,
        [shape((requests, 2 * quarter), f32), shape((requests, 2 * quarter), bf16)],
        [own, received],
    )
    far = permute(send, 2)
    mine, square = call(
        square_kernel,
        [shape((requests, quarter), f32), shape((requests, 128), f32)],
        [row, chip, far],
    )
    beside = permute(square, 1)
    return call(
        functools.partial(final_kernel, features),
        shape((requests, quarter), bf16),
        [mine, square, beside, post_gain.reshape(1, quarter), hidden_input],
    )


def solution(mesh):
    in_specs = (
        P("replica", "tensor"),
        P("replica", "tensor"),
        P("replica", None, None, "tensor"),
        P("replica", None, None, "tensor"),
        P("replica", None),
        P("replica"),
        P("replica"),
        P("replica"),
        P("tensor", None),
        P("tensor"),
    )
    out_specs = P("replica", "tensor")
    return jax.shard_map(shards, mesh=mesh, in_specs=in_specs, out_specs=out_specs, check_vma=False)
```

```python
import functools
import math

import jax
import jax.numpy as jnp
from jax import lax
from jax.experimental import pallas as pl
from jax.experimental.pallas import tpu as pltpu
from jax.sharding import PartitionSpec as P

HD = 256
softcap = 50.0
epsilon = 1e-06
score_scale = 1.0 / (softcap * math.sqrt(HD))
weight_scale = softcap * math.log2(math.e)
EXTRA = 128
f32 = jnp.float32
bf16 = jnp.bfloat16
VMEM = pltpu.MemorySpace.VMEM
SMEM = pltpu.MemorySpace.SMEM
VMEM_SPEC = pl.BlockSpec(memory_space=VMEM)
SMEM_SPEC = pl.BlockSpec(memory_space=SMEM)
HBM_SPEC = pl.BlockSpec(memory_space=pltpu.MemorySpace.HBM)
PARAMS = pltpu.CompilerParams(vmem_limit_bytes=40 * 2**20)


def iota(shape, axis):
    return lax.broadcasted_iota(jnp.int32, shape, axis)


def heads_below(block, heads):
    return jnp.concatenate([block[:, h * HD : (h + 1) * HD] for h in range(heads)], axis=0)


def weights_of(scores, alive):
    return jnp.where(alive, jnp.exp2(weight_scale * jnp.tanh(scores * score_scale)), 0.0)


def owners(owner_ref):
    requests = owner_ref.shape[1]
    rows, cols = iota((requests, requests), 0), iota((requests, requests), 1)
    by_col = jnp.broadcast_to(owner_ref[...], (requests, requests)).astype(f32)
    by_row = jnp.sum(jnp.where(rows == cols, by_col, 0.0), axis=1, keepdims=True)
    return by_row, by_col, rows, cols


def route_kernel(
    capacity, owner_hbm, group_hbm, queries_hbm, out_ref, owner_ref, group_ref, queries_ref, sems
):
    pairs = ((owner_hbm, owner_ref), (group_hbm, group_ref), (queries_hbm, queries_ref))
    copies = [pltpu.make_async_copy(a, b, sems.at[i]) for i, (a, b) in enumerate(pairs)]
    for copy in copies:
        copy.start()
    for copy in copies:
        copy.wait()
    requests, width = queries_ref.shape
    slots = out_ref.shape[0]
    by_row, by_col, rows, cols = owners(owner_ref)
    earlier = jnp.where((by_row == by_col) & (rows < cols), 1.0, 0.0)
    position = (by_col[:1] * capacity + jnp.sum(earlier, axis=0, keepdims=True)).astype(jnp.int32)
    matches = iota((slots, requests), 0) == position
    out_ref[:, :width] = jnp.dot(
        jnp.where(matches, 1.0, 0.0).astype(bf16), queries_ref[...], preferred_element_type=f32
    ).astype(bf16)
    numbered = (group_ref[...] + 1).astype(f32)
    mark = jnp.sum(jnp.where(matches, numbered, 0.0), axis=1, keepdims=True)
    out_ref[:, width:] = jnp.broadcast_to(mark, (slots, EXTRA)).astype(bf16)


def suffix_kernel(
    capacity,
    block,
    owner_hbm,
    length_hbm,
    queries_hbm,
    cache_hbm,
    core_ref,
    weight_hbm,
    after_hbm,
    back_ref,
    num_ref,
    den_ref,
    weight_ref,
    owner_ref,
    length_ref,
    queries_ref,
    cache_ref,
    sems,
    cache_sems,
    weight_sems,
):
    requests, slots = back_ref.shape
    window = cache_ref.shape[2]
    heads = queries_ref.shape[1] // HD
    steps = requests // block
    pairs = ((owner_hbm, owner_ref), (length_hbm, length_ref), (queries_hbm, queries_ref))
    copies = [pltpu.make_async_copy(a, b, sems.at[i]) for i, (a, b) in enumerate(pairs)]
    parts = []
    for i in range(steps):
        span = pl.ds(i * block, block)
        parts.append(
            pltpu.make_async_copy(cache_hbm.at[span], cache_ref.at[span], cache_sems.at[i])
        )
    quarter = weight_ref.shape[2]
    weight_copies = []
    for i, q in enumerate((1 - core_ref[0], 3 - core_ref[0], core_ref[0])):
        cols = pl.ds(pl.multiple_of(q * quarter, 128), quarter)
        weight_copies.append(
            pltpu.make_async_copy(weight_hbm.at[:, cols], weight_ref.at[i], weight_sems.at[i])
        )
    for copy in copies + parts + weight_copies:
        copy.start()
    for copy in copies:
        copy.wait()

    by_row, by_col, rows, cols = owners(owner_ref)
    earlier = jnp.where((by_row == by_col) & (cols < rows), 1.0, 0.0)
    rank = jnp.sum(earlier, axis=1, keepdims=True)
    position = (by_row * capacity + rank).astype(jnp.int32)
    back_ref[...] = jnp.where(iota((requests, slots), 1) == position, 1.0, 0.0).astype(bf16)
    live = jnp.sum(
        jnp.where(rows == cols, length_ref[...].astype(f32), 0.0), axis=1, keepdims=True
    ).astype(jnp.int32)

    at = iota((block, block * window), 1)
    first = iota((block, block * window), 0) * window
    for i in range(steps):
        mine = slice(i * block, (i + 1) * block)
        parts[i].wait()
        stacked = heads_below(queries_ref[mine, :], heads)
        keys = cache_ref[mine, 0].reshape(block * window, HD)
        values = cache_ref[mine, 1].reshape(block * window, HD)
        scores = lax.dot_general(
            stacked, keys, (((1,), (1,)), ((), ())), preferred_element_type=f32
        )
        alive = (at >= first) & (at < first + live[mine])
        weights = weights_of(scores, jnp.concatenate([alive] * heads, axis=0))
        numerator = jnp.dot(weights.astype(bf16), values, preferred_element_type=f32)
        denominator = jnp.sum(weights, axis=1, keepdims=True)
        for h in range(heads):
            own = slice(h * block, (h + 1) * block)
            num_ref[mine, h * HD : (h + 1) * HD] = numerator[own]
            den_ref[mine, h * 128 : (h + 1) * 128] = jnp.broadcast_to(
                denominator[own], (block, 128)
            )
    for copy in weight_copies:
        copy.wait()


def prefetch_kernel(core_ref, cache_hbm, weight_hbm, early_ref, last_hbm, staged, sems, last_sem):
    parts = parts_of(cache_hbm.shape[0])
    quarter = last_hbm.shape[1]
    cols = pl.ds(pl.multiple_of((core_ref[0] + 2) * quarter, 128), quarter)
    stage = pltpu.make_async_copy(weight_hbm.at[:, cols], staged, last_sem)
    unstage = pltpu.make_async_copy(staged, last_hbm, last_sem)
    stage.start()
    copies = [
        pltpu.make_async_copy(cache_hbm.at[parts[i]], early_ref.at[i], sems.at[i])
        for i in range(early_ref.shape[0])
    ]
    for copy in copies:
        copy.start()
    stage.wait()
    unstage.start()
    for copy in copies + [unstage]:
        copy.wait()


def parts_of(groups):
    return [(g, part) for g in range(groups) for part in range(2)]


def prompt_kernel(
    chunk,
    window,
    length_hbm,
    slots_ref,
    early_ref,
    cache_hbm,
    out_ref,
    length_ref,
    held,
    sorted_ref,
    done_ref,
    num_ref,
    den_ref,
    sems,
    length_sem,
):
    groups, _, size, _ = cache_hbm.shape
    slots = slots_ref.shape[0]
    width = slots_ref.shape[1] - EXTRA
    heads = width // HD
    parts = parts_of(groups)
    early = early_ref.shape[0]
    length_copy = pltpu.make_async_copy(length_hbm, length_ref, length_sem)
    length_copy.start()
    copies = {
        parts[i]: pltpu.make_async_copy(
            cache_hbm.at[parts[i]], held.at[i - early], sems.at[i - early]
        )
        for i in range(early, len(parts))
    }
    for part in parts[early:]:
        copies[part].start()

    def read(g, part, span):
        i = parts.index((g, part))
        return early_ref[i, span, :] if i < early else held[i - early, span, :]

    def pieces(total, rows):
        lanes = iota((1, EXTRA), 1)
        extra = jnp.zeros((rows, EXTRA), f32)
        for h in range(heads):
            rest = total[h * rows : (h + 1) * rows]
            for k in range(3):
                piece = rest.astype(bf16).astype(f32)
                rest = rest - piece
                extra = jnp.where(lanes == 3 * h + k, piece, extra)
        return extra.astype(bf16)

    def fold(weights):
        part = weights[:, :128]
        for k in range(1, weights.shape[1] // 128):
            part = part + weights[:, k * 128 : (k + 1) * 128]
        return part

    rows, cols = iota((slots, slots), 0), iota((slots, slots), 1)
    by_row = jnp.broadcast_to(slots_ref[:, width : width + 1].astype(f32), (slots, slots))
    by_col = jnp.sum(jnp.where(rows == cols, by_row, 0.0), axis=0, keepdims=True)
    same = by_row == by_col
    rank_row = jnp.sum(jnp.where(same & (cols < rows), 1.0, 0.0), axis=1, keepdims=True)
    rank_col = jnp.sum(jnp.where(same & (rows < cols), 1.0, 0.0), axis=0, keepdims=True)
    length_copy.wait()
    crowded = jnp.max(jnp.where(by_col > 0.0, rank_col, 0.0)) >= window

    at_row = (by_row[:, :1] - 1.0) * window + rank_row
    at_row = jnp.where(by_row[:, :1] > 0.0, at_row, -1.0).astype(jnp.int32)
    at_col = jnp.where(by_col > 0.0, (by_col - 1.0) * window + rank_col, -1.0).astype(jnp.int32)
    room = groups * window
    there = jnp.where(iota((room, slots), 0) == at_col, 1.0, 0.0).astype(bf16)
    back = jnp.where(iota((slots, room), 1) == at_row, 1.0, 0.0).astype(bf16)
    for h in range(heads):
        part = jnp.dot(there, slots_ref[:, h * HD : (h + 1) * HD], preferred_element_type=f32)
        for g in range(groups):
            at = (g * heads + h) * window
            sorted_ref[at : at + window, :] = part[g * window : (g + 1) * window].astype(bf16)
    scores = [None] * groups
    waited = early
    everything = slice(0, size)
    for u in range(groups + 1):
        needed = min(2 * u + 1, len(parts))
        if needed > waited:
            needed = min(needed + 1, len(parts))
            for part in parts[waited:needed]:
                copies[part].wait()
            waited = needed
        if u < groups:
            scores[u] = lax.dot_general(
                sorted_ref[u * heads * window : (u + 1) * heads * window, :],
                read(u, 0, everything),
                (((1,), (1,)), ((), ())),
                preferred_element_type=f32,
            )
        if u > 0:
            g = u - 1
            weights = weights_of(scores[g], iota((1, size), 1) < length_ref[g])
            num = jnp.dot(
                weights.astype(bf16), read(g, 1, everything), preferred_element_type=f32
            )
            mine = slice(g * window, (g + 1) * window)
            for h in range(heads):
                done_ref[mine, h * HD : (h + 1) * HD] = num[
                    h * window : (h + 1) * window
                ].astype(bf16)
            den = jnp.sum(fold(weights), axis=1, keepdims=True)
            done_ref[mine, width:] = pieces(den, window)
    out_ref[...] = jnp.dot(back, done_ref[...], preferred_element_type=f32).astype(bf16)

    @pl.when(crowded)
    def _():
        stacked = heads_below(slots_ref[:, :width], heads)
        mark = jnp.concatenate([by_row[:, :1]] * heads, axis=0)
        num_ref[...] = jnp.zeros_like(num_ref)
        den_ref[...] = jnp.zeros_like(den_ref)
        for g in range(groups):
            limit = jnp.where(mark == g + 1.0, length_ref[g], 0)

            @pl.loop(0, (length_ref[g] + chunk - 1) // chunk)
            def _(c):
                span = pl.ds(pl.multiple_of(c * chunk, chunk), chunk)
                scores = lax.dot_general(
                    stacked,
                    read(g, 0, span),
                    (((1,), (1,)), ((), ())),
                    preferred_element_type=f32,
                )
                alive = iota((heads * slots, chunk), 1) < limit - c * chunk
                weights = weights_of(scores, alive)
                num_ref[...] += jnp.dot(
                    weights.astype(bf16), read(g, 1, span), preferred_element_type=f32
                )
                den_ref[...] += fold(weights)

        for h in range(heads):
            out_ref[:, h * HD : (h + 1) * HD] = num_ref[h * slots : (h + 1) * slots].astype(bf16)
        out_ref[:, width:] = pieces(jnp.sum(den_ref[...], axis=1, keepdims=True), slots)


def combine_kernel(
    returned_ref, back_ref, num_ref, den_ref, weight_ref, att_ref, give_ref
):
    quarter = weight_ref.shape[2]
    width = num_ref.shape[1]
    heads = width // HD
    mine = jnp.dot(back_ref[...], returned_ref[...], preferred_element_type=f32)
    for h in range(heads):
        cols = slice(h * HD, (h + 1) * HD)
        numerator = mine[:, cols] + num_ref[:, cols]
        at = width + 3 * h
        denominator = den_ref[:, h * 128 : h * 128 + 1] + (
            mine[:, at : at + 1] + mine[:, at + 1 : at + 2] + mine[:, at + 2 : at + 3]
        )
        att_ref[:, cols] = (numerator / denominator).astype(bf16)
    for i in range(2):
        give_ref[:, i * quarter : (i + 1) * quarter] = jnp.dot(
            att_ref[...], weight_ref[i], preferred_element_type=f32
        ).astype(bf16)


def own_kernel(att_ref, weight_ref, last_ref, own_ref):
    quarter = weight_ref.shape[2]
    own_ref[:, :quarter] = jnp.dot(att_ref[...], weight_ref[2], preferred_element_type=f32)
    own_ref[:, quarter:] = jnp.dot(att_ref[...], last_ref[...], preferred_element_type=f32)


def chip_kernel(own_ref, got_ref, sum_ref, send_ref):
    total = own_ref[...] + got_ref[...].astype(f32)
    sum_ref[...] = total
    send_ref[...] = total.astype(bf16)


def square_kernel(row_ref, sum_ref, got_ref, mine_ref, square_ref):
    width = mine_ref.shape[1]
    total = sum_ref[...] + got_ref[...].astype(f32)
    part = jnp.zeros(square_ref.shape, f32)
    for k in range(total.shape[1] // 128):
        piece = total[:, k * 128 : (k + 1) * 128]
        part = part + piece * piece
    square_ref[...] = part
    mine_ref[...] = jnp.where(row_ref[0] == 0, total[:, :width], total[:, width:])


def final_kernel(features, mine_ref, square_ref, got_ref, gain_ref, hidden_ref, out_ref):
    square = jnp.sum(square_ref[...] + got_ref[...], axis=1, keepdims=True)
    scale = lax.rsqrt(square * (1.0 / features) + epsilon)
    normed = mine_ref[...] * scale * gain_ref[...]
    out_ref[...] = (hidden_ref[...].astype(f32) + normed).astype(bf16)


def call(kernel, outs, ins, **kw):
    specs = [
        pl.BlockSpec(memory_space=SMEM if a.ndim == 1 else VMEM) for a in ins
    ]
    return pl.pallas_call(
        kernel,
        out_shape=outs,
        in_specs=specs,
        out_specs=jax.tree.map(lambda _: pl.BlockSpec(memory_space=VMEM), outs),
        compiler_params=PARAMS,
        **kw,
    )(*ins)


def in_hbm(*arrays):
    return [pltpu.with_memory_space_constraint(a, pltpu.MemorySpace.HBM) for a in arrays]


def shape(dims, dtype):
    return jax.ShapeDtypeStruct(dims, dtype)


def shards(
    hidden_input,
    queries,
    prompt_cache,
    suffix_cache,
    owner_replica,
    group_slot,
    prompt_length,
    suffix_length,
    output_weight,
    post_gain,
):
    replicas = lax.axis_size("replica")
    ranks = lax.axis_size("tensor")
    requests, width = queries.shape
    capacity = max(2, (2 * requests + replicas - 1) // replicas)
    slots = replicas * capacity
    groups, _, size, _ = prompt_cache.shape
    window = suffix_cache.shape[2]
    features = output_weight.shape[1]
    quarter = features // ranks
    heads = width // HD
    index = lax.axis_index("tensor")
    core = (index % 2).reshape(1)
    row = (index // 2).reshape(1)

    def exchange(x):
        blocks = x.reshape(replicas, capacity, width + EXTRA)
        blocks = lax.all_to_all(blocks, "replica", split_axis=0, concat_axis=0, tiled=True)
        return blocks.reshape(slots, width + EXTRA)

    def permute(x, bit):
        return lax.ppermute(x, "tensor", [(i, i ^ bit) for i in range(ranks)])

    owner_row = owner_replica.reshape(1, requests)
    sent = pl.pallas_call(
        functools.partial(route_kernel, capacity),
        out_shape=pltpu.VMEM((slots, width + EXTRA), bf16),
        in_specs=[HBM_SPEC] * 3,
        out_specs=VMEM_SPEC,
        scratch_shapes=[
            pltpu.VMEM((1, requests), jnp.int32),
            pltpu.VMEM((1, requests), jnp.int32),
            pltpu.VMEM((requests, width), bf16),
            pltpu.SemaphoreType.DMA((3,)),
        ],
        compiler_params=PARAMS,
    )(*in_hbm(owner_row, group_slot.reshape(1, requests), queries))
    got = exchange(sent)

    early = 3
    prefetched, last = pl.pallas_call(
        prefetch_kernel,
        out_shape=[pltpu.VMEM((early, size, HD), bf16), pltpu.HBM((width, quarter), bf16)],
        in_specs=[SMEM_SPEC, HBM_SPEC, HBM_SPEC],
        out_specs=[VMEM_SPEC, HBM_SPEC],
        scratch_shapes=[
            pltpu.VMEM((width, quarter), bf16),
            pltpu.SemaphoreType.DMA((early,)),
            pltpu.SemaphoreType.DMA,
        ],
        compiler_params=PARAMS,
        cost_estimate=pl.CostEstimate(
            flops=0, bytes_accessed=2 * early * size * HD * 2, transcendentals=0
        ),
    )(core, *in_hbm(prompt_cache, output_weight))

    chunk = math.gcd(512, size)
    fit = min(48, slots)
    answered = pl.pallas_call(
        functools.partial(prompt_kernel, chunk, fit),
        out_shape=pltpu.VMEM((slots, width + EXTRA), bf16),
        in_specs=[HBM_SPEC, VMEM_SPEC, VMEM_SPEC, HBM_SPEC],
        out_specs=VMEM_SPEC,
        scratch_shapes=[
            pltpu.SMEM((groups,), jnp.int32),
            pltpu.VMEM((2 * groups - early, size, HD), bf16),
            pltpu.VMEM((groups * heads * fit, HD), bf16),
            pltpu.VMEM((groups * fit, width + EXTRA), bf16),
            pltpu.VMEM((heads * slots, HD), f32),
            pltpu.VMEM((heads * slots, 128), f32),
            pltpu.SemaphoreType.DMA((2 * groups - early,)),
            pltpu.SemaphoreType.DMA,
        ],
        compiler_params=PARAMS,
    )(
        *in_hbm(prompt_length),
        got,
        pltpu.with_memory_space_constraint(prefetched, VMEM),
        *in_hbm(prompt_cache),
    )
    returned = exchange(answered)

    block = math.gcd(16, requests)
    back, own_num, own_den, weight = pl.pallas_call(
        functools.partial(suffix_kernel, capacity, block),
        out_shape=[
            shape((requests, slots), bf16),
            shape((requests, width), f32),
            shape((requests, heads * 128), f32),
            pltpu.VMEM((3, width, quarter), bf16),
        ],
        in_specs=[HBM_SPEC] * 4 + [SMEM_SPEC, HBM_SPEC, HBM_SPEC],
        out_specs=[VMEM_SPEC] * 4,
        scratch_shapes=[
            pltpu.VMEM((1, requests), jnp.int32),
            pltpu.VMEM((1, requests), jnp.int32),
            pltpu.VMEM((requests, width), bf16),
            pltpu.VMEM(suffix_cache.shape, bf16),
            pltpu.SemaphoreType.DMA((3,)),
            pltpu.SemaphoreType.DMA((requests // block,)),
            pltpu.SemaphoreType.DMA((3,)),
        ],
        compiler_params=PARAMS,
        cost_estimate=pl.CostEstimate(
            flops=8 * requests * window * HD * block,
            bytes_accessed=(suffix_cache.size + output_weight.size) * 2,
            transcendentals=0,
        ),
    )(
        *in_hbm(owner_row, suffix_length.reshape(1, requests), queries, suffix_cache),
        core,
        *in_hbm(output_weight, answered),
    )
    weight = pltpu.with_memory_space_constraint(weight, VMEM)

    attention, give = call(
        combine_kernel,
        [shape((requests, width), bf16), shape((requests, 2 * quarter), bf16)],
        [returned, back, own_num, own_den, weight],
    )
    received = permute(give, 1)
    own = call(
        own_kernel,
        shape((requests, 2 * quarter), f32),
        [attention, weight, last],
    )
    chip, send = call(
        chip_kernel,
        [shape((requests, 2 * quarter), f32), shape((requests, 2 * quarter), bf16)],
        [own, received],
    )
    far = permute(send, 2)
    mine, square = call(
        square_kernel,
        [shape((requests, quarter), f32), shape((requests, 128), f32)],
        [row, chip, far],
    )
    beside = permute(square, 1)
    return call(
        functools.partial(final_kernel, features),
        shape((requests, quarter), bf16),
        [mine, square, beside, post_gain.reshape(1, quarter), hidden_input],
    )


def solution(mesh):
    in_specs = (
        P("replica", "tensor"),
        P("replica", "tensor"),
        P("replica", None, None, "tensor"),
        P("replica", None, None, "tensor"),
        P("replica", None),
        P("replica"),
        P("replica"),
        P("replica"),
        P("tensor", None),
        P("tensor"),
    )
    out_specs = P("replica", "tensor")
    return jax.shard_map(shards, mesh=mesh, in_specs=in_specs, out_specs=out_specs, check_vma=False)
```

```python
import functools
import math

import jax
import jax.numpy as jnp
from jax import lax
from jax.experimental import pallas as pl
from jax.experimental.pallas import tpu as pltpu
from jax.sharding import PartitionSpec as P

HD = 256
softcap = 50.0
epsilon = 1e-06
score_scale = 1.0 / (softcap * math.sqrt(HD))
weight_scale = softcap * math.log2(math.e)
EXTRA = 128
f32 = jnp.float32
bf16 = jnp.bfloat16
VMEM = pltpu.MemorySpace.VMEM
SMEM = pltpu.MemorySpace.SMEM
VMEM_SPEC = pl.BlockSpec(memory_space=VMEM)
SMEM_SPEC = pl.BlockSpec(memory_space=SMEM)
HBM_SPEC = pl.BlockSpec(memory_space=pltpu.MemorySpace.HBM)
PARAMS = pltpu.CompilerParams(vmem_limit_bytes=40 * 2**20)


def iota(shape, axis):
    return lax.broadcasted_iota(jnp.int32, shape, axis)


def heads_below(block, heads):
    return jnp.concatenate([block[:, h * HD : (h + 1) * HD] for h in range(heads)], axis=0)


def weights_of(scores, alive):
    return jnp.where(alive, jnp.exp2(weight_scale * jnp.tanh(scores * score_scale)), 0.0)


def order_of(replicas):
    return {8: (4, 5, 6, 1, 0, 7, 2, 3)}.get(replicas, tuple(range(replicas)))


def owners(owner_ref, order):
    requests = owner_ref.shape[1]
    rows, cols = iota((requests, requests), 0), iota((requests, requests), 1)
    owner = owner_ref[...]
    place = owner
    for i, replica in enumerate(order):
        if i != replica:
            place = jnp.where(owner == replica, i, place)
    by_col = jnp.broadcast_to(place, (requests, requests)).astype(f32)
    by_row = jnp.sum(jnp.where(rows == cols, by_col, 0.0), axis=1, keepdims=True)
    return by_row, by_col, rows, cols


def route_kernel(
    capacity, order, owner_hbm, group_hbm, queries_hbm, out_ref, owner_ref, group_ref, queries_ref, sems
):
    pairs = ((owner_hbm, owner_ref), (group_hbm, group_ref), (queries_hbm, queries_ref))
    copies = [pltpu.make_async_copy(a, b, sems.at[i]) for i, (a, b) in enumerate(pairs)]
    for copy in copies:
        copy.start()
    for copy in copies:
        copy.wait()
    requests, width = queries_ref.shape
    slots = out_ref.shape[0]
    by_row, by_col, rows, cols = owners(owner_ref, order)
    earlier = jnp.where((by_row == by_col) & (rows < cols), 1.0, 0.0)
    position = (by_col[:1] * capacity + jnp.sum(earlier, axis=0, keepdims=True)).astype(jnp.int32)
    matches = iota((slots, requests), 0) == position
    out_ref[:, :width] = jnp.dot(
        jnp.where(matches, 1.0, 0.0).astype(bf16), queries_ref[...], preferred_element_type=f32
    ).astype(bf16)
    numbered = (group_ref[...] + 1).astype(f32)
    mark = jnp.sum(jnp.where(matches, numbered, 0.0), axis=1, keepdims=True)
    out_ref[:, width:] = jnp.broadcast_to(mark, (slots, EXTRA)).astype(bf16)


def suffix_kernel(
    capacity,
    order,
    block,
    owner_hbm,
    length_hbm,
    queries_hbm,
    cache_hbm,
    core_ref,
    weight_hbm,
    after_hbm,
    back_ref,
    num_ref,
    den_ref,
    weight_ref,
    owner_ref,
    length_ref,
    queries_ref,
    cache_ref,
    sems,
    cache_sems,
    weight_sems,
):
    requests, slots = back_ref.shape
    window = cache_ref.shape[2]
    heads = queries_ref.shape[1] // HD
    steps = requests // block
    pairs = ((owner_hbm, owner_ref), (length_hbm, length_ref), (queries_hbm, queries_ref))
    copies = [pltpu.make_async_copy(a, b, sems.at[i]) for i, (a, b) in enumerate(pairs)]
    parts = []
    for i in range(steps):
        span = pl.ds(i * block, block)
        parts.append(
            pltpu.make_async_copy(cache_hbm.at[span], cache_ref.at[span], cache_sems.at[i])
        )
    quarter = weight_ref.shape[2]
    weight_copies = []
    for i, q in enumerate((1 - core_ref[0], 3 - core_ref[0], core_ref[0])):
        cols = pl.ds(pl.multiple_of(q * quarter, 128), quarter)
        weight_copies.append(
            pltpu.make_async_copy(weight_hbm.at[:, cols], weight_ref.at[i], weight_sems.at[i])
        )
    for copy in copies + parts + weight_copies:
        copy.start()
    for copy in copies:
        copy.wait()

    by_row, by_col, rows, cols = owners(owner_ref, order)
    earlier = jnp.where((by_row == by_col) & (cols < rows), 1.0, 0.0)
    rank = jnp.sum(earlier, axis=1, keepdims=True)
    position = (by_row * capacity + rank).astype(jnp.int32)
    back_ref[...] = jnp.where(iota((requests, slots), 1) == position, 1.0, 0.0).astype(bf16)
    live = jnp.sum(
        jnp.where(rows == cols, length_ref[...].astype(f32), 0.0), axis=1, keepdims=True
    ).astype(jnp.int32)

    at = iota((block, block * window), 1)
    first = iota((block, block * window), 0) * window
    for i in range(steps):
        mine = slice(i * block, (i + 1) * block)
        parts[i].wait()
        stacked = heads_below(queries_ref[mine, :], heads)
        keys = cache_ref[mine, 0].reshape(block * window, HD)
        values = cache_ref[mine, 1].reshape(block * window, HD)
        scores = lax.dot_general(
            stacked, keys, (((1,), (1,)), ((), ())), preferred_element_type=f32
        )
        alive = (at >= first) & (at < first + live[mine])
        weights = weights_of(scores, jnp.concatenate([alive] * heads, axis=0))
        numerator = jnp.dot(weights.astype(bf16), values, preferred_element_type=f32)
        denominator = jnp.sum(weights, axis=1, keepdims=True)
        for h in range(heads):
            own = slice(h * block, (h + 1) * block)
            num_ref[mine, h * HD : (h + 1) * HD] = numerator[own]
            den_ref[mine, h * 128 : (h + 1) * 128] = jnp.broadcast_to(
                denominator[own], (block, 128)
            )
    for copy in weight_copies:
        copy.wait()


def prefetch_kernel(core_ref, cache_hbm, weight_hbm, early_ref, last_hbm, staged, sems, last_sem):
    parts = parts_of(cache_hbm.shape[0])
    quarter = last_hbm.shape[1]
    cols = pl.ds(pl.multiple_of((core_ref[0] + 2) * quarter, 128), quarter)
    stage = pltpu.make_async_copy(weight_hbm.at[:, cols], staged, last_sem)
    unstage = pltpu.make_async_copy(staged, last_hbm, last_sem)
    stage.start()
    copies = [
        pltpu.make_async_copy(cache_hbm.at[parts[i]], early_ref.at[i], sems.at[i])
        for i in range(early_ref.shape[0])
    ]
    for copy in copies:
        copy.start()
    stage.wait()
    unstage.start()
    for copy in copies + [unstage]:
        copy.wait()


def parts_of(groups):
    return [(g, part) for g in range(groups) for part in range(2)]


def prompt_kernel(
    chunk,
    window,
    length_hbm,
    slots_ref,
    early_ref,
    cache_hbm,
    out_ref,
    length_ref,
    held,
    sorted_ref,
    done_ref,
    num_ref,
    den_ref,
    sems,
    length_sem,
):
    groups, _, size, _ = cache_hbm.shape
    slots = slots_ref.shape[0]
    width = slots_ref.shape[1] - EXTRA
    heads = width // HD
    parts = parts_of(groups)
    early = early_ref.shape[0]
    length_copy = pltpu.make_async_copy(length_hbm, length_ref, length_sem)
    length_copy.start()
    copies = {
        parts[i]: pltpu.make_async_copy(
            cache_hbm.at[parts[i]], held.at[i - early], sems.at[i - early]
        )
        for i in range(early, len(parts))
    }
    for part in parts[early:]:
        copies[part].start()

    def read(g, part, span):
        i = parts.index((g, part))
        return early_ref[i, span, :] if i < early else held[i - early, span, :]

    def pieces(total, rows):
        lanes = iota((1, EXTRA), 1)
        extra = jnp.zeros((rows, EXTRA), f32)
        for h in range(heads):
            rest = total[h * rows : (h + 1) * rows]
            for k in range(3):
                piece = rest.astype(bf16).astype(f32)
                rest = rest - piece
                extra = jnp.where(lanes == 3 * h + k, piece, extra)
        return extra.astype(bf16)

    def fold(weights):
        part = weights[:, :128]
        for k in range(1, weights.shape[1] // 128):
            part = part + weights[:, k * 128 : (k + 1) * 128]
        return part

    rows, cols = iota((slots, slots), 0), iota((slots, slots), 1)
    by_row = jnp.broadcast_to(slots_ref[:, width : width + 1].astype(f32), (slots, slots))
    by_col = jnp.sum(jnp.where(rows == cols, by_row, 0.0), axis=0, keepdims=True)
    same = by_row == by_col
    rank_row = jnp.sum(jnp.where(same & (cols < rows), 1.0, 0.0), axis=1, keepdims=True)
    rank_col = jnp.sum(jnp.where(same & (rows < cols), 1.0, 0.0), axis=0, keepdims=True)
    length_copy.wait()
    crowded = jnp.max(jnp.where(by_col > 0.0, rank_col, 0.0)) >= window

    at_row = (by_row[:, :1] - 1.0) * window + rank_row
    at_row = jnp.where(by_row[:, :1] > 0.0, at_row, -1.0).astype(jnp.int32)
    at_col = jnp.where(by_col > 0.0, (by_col - 1.0) * window + rank_col, -1.0).astype(jnp.int32)
    room = groups * window
    there = jnp.where(iota((room, slots), 0) == at_col, 1.0, 0.0).astype(bf16)
    back = jnp.where(iota((slots, room), 1) == at_row, 1.0, 0.0).astype(bf16)
    for h in range(heads):
        part = jnp.dot(there, slots_ref[:, h * HD : (h + 1) * HD], preferred_element_type=f32)
        for g in range(groups):
            at = (g * heads + h) * window
            sorted_ref[at : at + window, :] = part[g * window : (g + 1) * window].astype(bf16)
    scores = [None] * groups
    waited = early
    everything = slice(0, size)
    for u in range(groups + 1):
        needed = min(2 * u + 1, len(parts))
        if needed > waited:
            needed = min(needed + 1, len(parts))
            for part in parts[waited:needed]:
                copies[part].wait()
            waited = needed
        if u < groups:
            scores[u] = lax.dot_general(
                sorted_ref[u * heads * window : (u + 1) * heads * window, :],
                read(u, 0, everything),
                (((1,), (1,)), ((), ())),
                preferred_element_type=f32,
            )
        if u > 0:
            g = u - 1
            weights = weights_of(scores[g], iota((1, size), 1) < length_ref[g])
            num = jnp.dot(
                weights.astype(bf16), read(g, 1, everything), preferred_element_type=f32
            )
            mine = slice(g * window, (g + 1) * window)
            for h in range(heads):
                done_ref[mine, h * HD : (h + 1) * HD] = num[
                    h * window : (h + 1) * window
                ].astype(bf16)
            den = jnp.sum(fold(weights), axis=1, keepdims=True)
            done_ref[mine, width:] = pieces(den, window)
    out_ref[...] = jnp.dot(back, done_ref[...], preferred_element_type=f32).astype(bf16)

    @pl.when(crowded)
    def _():
        stacked = heads_below(slots_ref[:, :width], heads)
        mark = jnp.concatenate([by_row[:, :1]] * heads, axis=0)
        num_ref[...] = jnp.zeros_like(num_ref)
        den_ref[...] = jnp.zeros_like(den_ref)
        for g in range(groups):
            limit = jnp.where(mark == g + 1.0, length_ref[g], 0)

            @pl.loop(0, (length_ref[g] + chunk - 1) // chunk)
            def _(c):
                span = pl.ds(pl.multiple_of(c * chunk, chunk), chunk)
                scores = lax.dot_general(
                    stacked,
                    read(g, 0, span),
                    (((1,), (1,)), ((), ())),
                    preferred_element_type=f32,
                )
                alive = iota((heads * slots, chunk), 1) < limit - c * chunk
                weights = weights_of(scores, alive)
                num_ref[...] += jnp.dot(
                    weights.astype(bf16), read(g, 1, span), preferred_element_type=f32
                )
                den_ref[...] += fold(weights)

        for h in range(heads):
            out_ref[:, h * HD : (h + 1) * HD] = num_ref[h * slots : (h + 1) * slots].astype(bf16)
        out_ref[:, width:] = pieces(jnp.sum(den_ref[...], axis=1, keepdims=True), slots)


def combine_kernel(
    returned_ref, back_ref, num_ref, den_ref, weight_ref, att_ref, give_ref
):
    quarter = weight_ref.shape[2]
    width = num_ref.shape[1]
    heads = width // HD
    mine = jnp.dot(back_ref[...], returned_ref[...], preferred_element_type=f32)
    for h in range(heads):
        cols = slice(h * HD, (h + 1) * HD)
        numerator = mine[:, cols] + num_ref[:, cols]
        at = width + 3 * h
        denominator = den_ref[:, h * 128 : h * 128 + 1] + (
            mine[:, at : at + 1] + mine[:, at + 1 : at + 2] + mine[:, at + 2 : at + 3]
        )
        att_ref[:, cols] = (numerator / denominator).astype(bf16)
    for i in range(2):
        give_ref[:, i * quarter : (i + 1) * quarter] = jnp.dot(
            att_ref[...], weight_ref[i], preferred_element_type=f32
        ).astype(bf16)


def own_kernel(att_ref, weight_ref, last_ref, own_ref):
    quarter = weight_ref.shape[2]
    own_ref[:, :quarter] = jnp.dot(att_ref[...], weight_ref[2], preferred_element_type=f32)
    own_ref[:, quarter:] = jnp.dot(att_ref[...], last_ref[...], preferred_element_type=f32)


def chip_kernel(own_ref, got_ref, sum_ref, send_ref):
    total = own_ref[...] + got_ref[...].astype(f32)
    sum_ref[...] = total
    send_ref[...] = total.astype(bf16)


def square_kernel(row_ref, sum_ref, got_ref, mine_ref, square_ref):
    width = mine_ref.shape[1]
    total = sum_ref[...] + got_ref[...].astype(f32)
    part = jnp.zeros(square_ref.shape, f32)
    for k in range(total.shape[1] // 128):
        piece = total[:, k * 128 : (k + 1) * 128]
        part = part + piece * piece
    square_ref[...] = part
    mine_ref[...] = jnp.where(row_ref[0] == 0, total[:, :width], total[:, width:])


def final_kernel(features, mine_ref, square_ref, got_ref, gain_ref, hidden_ref, out_ref):
    square = jnp.sum(square_ref[...] + got_ref[...], axis=1, keepdims=True)
    scale = lax.rsqrt(square * (1.0 / features) + epsilon)
    normed = mine_ref[...] * scale * gain_ref[...]
    out_ref[...] = (hidden_ref[...].astype(f32) + normed).astype(bf16)


def call(kernel, outs, ins, **kw):
    specs = [
        pl.BlockSpec(memory_space=SMEM if a.ndim == 1 else VMEM) for a in ins
    ]
    return pl.pallas_call(
        kernel,
        out_shape=outs,
        in_specs=specs,
        out_specs=jax.tree.map(lambda _: pl.BlockSpec(memory_space=VMEM), outs),
        compiler_params=PARAMS,
        **kw,
    )(*ins)


def in_hbm(*arrays):
    return [pltpu.with_memory_space_constraint(a, pltpu.MemorySpace.HBM) for a in arrays]


def shape(dims, dtype):
    return jax.ShapeDtypeStruct(dims, dtype)


def shards(
    hidden_input,
    queries,
    prompt_cache,
    suffix_cache,
    owner_replica,
    group_slot,
    prompt_length,
    suffix_length,
    output_weight,
    post_gain,
):
    replicas = lax.axis_size("replica")
    ranks = lax.axis_size("tensor")
    requests, width = queries.shape
    capacity = max(2, (2 * requests + replicas - 1) // replicas)
    slots = replicas * capacity
    groups, _, size, _ = prompt_cache.shape
    window = suffix_cache.shape[2]
    features = output_weight.shape[1]
    quarter = features // ranks
    heads = width // HD
    order = order_of(replicas)
    index = lax.axis_index("tensor")
    core = (index % 2).reshape(1)
    row = (index // 2).reshape(1)

    def exchange(x):
        blocks = x.reshape(replicas, capacity, width + EXTRA)
        blocks = lax.all_to_all(
            blocks, "replica", split_axis=0, concat_axis=0, axis_index_groups=[order], tiled=True
        )
        return blocks.reshape(slots, width + EXTRA)

    def permute(x, bit):
        return lax.ppermute(x, "tensor", [(i, i ^ bit) for i in range(ranks)])

    owner_row = owner_replica.reshape(1, requests)
    sent = pl.pallas_call(
        functools.partial(route_kernel, capacity, order),
        out_shape=pltpu.VMEM((slots, width + EXTRA), bf16),
        in_specs=[HBM_SPEC] * 3,
        out_specs=VMEM_SPEC,
        scratch_shapes=[
            pltpu.VMEM((1, requests), jnp.int32),
            pltpu.VMEM((1, requests), jnp.int32),
            pltpu.VMEM((requests, width), bf16),
            pltpu.SemaphoreType.DMA((3,)),
        ],
        compiler_params=PARAMS,
    )(*in_hbm(owner_row, group_slot.reshape(1, requests), queries))
    got = exchange(sent)

    early = 3
    prefetched, last = pl.pallas_call(
        prefetch_kernel,
        out_shape=[pltpu.VMEM((early, size, HD), bf16), pltpu.HBM((width, quarter), bf16)],
        in_specs=[SMEM_SPEC, HBM_SPEC, HBM_SPEC],
        out_specs=[VMEM_SPEC, HBM_SPEC],
        scratch_shapes=[
            pltpu.VMEM((width, quarter), bf16),
            pltpu.SemaphoreType.DMA((early,)),
            pltpu.SemaphoreType.DMA,
        ],
        compiler_params=PARAMS,
        cost_estimate=pl.CostEstimate(
            flops=0, bytes_accessed=2 * early * size * HD * 2, transcendentals=0
        ),
    )(core, *in_hbm(prompt_cache, output_weight))

    chunk = math.gcd(512, size)
    fit = min(48, slots)
    answered = pl.pallas_call(
        functools.partial(prompt_kernel, chunk, fit),
        out_shape=pltpu.VMEM((slots, width + EXTRA), bf16),
        in_specs=[HBM_SPEC, VMEM_SPEC, VMEM_SPEC, HBM_SPEC],
        out_specs=VMEM_SPEC,
        scratch_shapes=[
            pltpu.SMEM((groups,), jnp.int32),
            pltpu.VMEM((2 * groups - early, size, HD), bf16),
            pltpu.VMEM((groups * heads * fit, HD), bf16),
            pltpu.VMEM((groups * fit, width + EXTRA), bf16),
            pltpu.VMEM((heads * slots, HD), f32),
            pltpu.VMEM((heads * slots, 128), f32),
            pltpu.SemaphoreType.DMA((2 * groups - early,)),
            pltpu.SemaphoreType.DMA,
        ],
        compiler_params=PARAMS,
    )(
        *in_hbm(prompt_length),
        got,
        pltpu.with_memory_space_constraint(prefetched, VMEM),
        *in_hbm(prompt_cache),
    )
    returned = exchange(answered)

    block = math.gcd(16, requests)
    back, own_num, own_den, weight = pl.pallas_call(
        functools.partial(suffix_kernel, capacity, order, block),
        out_shape=[
            shape((requests, slots), bf16),
            shape((requests, width), f32),
            shape((requests, heads * 128), f32),
            pltpu.VMEM((3, width, quarter), bf16),
        ],
        in_specs=[HBM_SPEC] * 4 + [SMEM_SPEC, HBM_SPEC, HBM_SPEC],
        out_specs=[VMEM_SPEC] * 4,
        scratch_shapes=[
            pltpu.VMEM((1, requests), jnp.int32),
            pltpu.VMEM((1, requests), jnp.int32),
            pltpu.VMEM((requests, width), bf16),
            pltpu.VMEM(suffix_cache.shape, bf16),
            pltpu.SemaphoreType.DMA((3,)),
            pltpu.SemaphoreType.DMA((requests // block,)),
            pltpu.SemaphoreType.DMA((3,)),
        ],
        compiler_params=PARAMS,
        cost_estimate=pl.CostEstimate(
            flops=8 * requests * window * HD * block,
            bytes_accessed=(suffix_cache.size + output_weight.size) * 2,
            transcendentals=0,
        ),
    )(
        *in_hbm(owner_row, suffix_length.reshape(1, requests), queries, suffix_cache),
        core,
        *in_hbm(output_weight, answered),
    )
    weight = pltpu.with_memory_space_constraint(weight, VMEM)

    attention, give = call(
        combine_kernel,
        [shape((requests, width), bf16), shape((requests, 2 * quarter), bf16)],
        [returned, back, own_num, own_den, weight],
    )
    received = permute(give, 1)
    own = call(
        own_kernel,
        shape((requests, 2 * quarter), f32),
        [attention, weight, last],
    )
    chip, send = call(
        chip_kernel,
        [shape((requests, 2 * quarter), f32), shape((requests, 2 * quarter), bf16)],
        [own, received],
    )
    far = permute(send, 2)
    mine, square = call(
        square_kernel,
        [shape((requests, quarter), f32), shape((requests, 128), f32)],
        [row, chip, far],
    )
    beside = permute(square, 1)
    return call(
        functools.partial(final_kernel, features),
        shape((requests, quarter), bf16),
        [mine, square, beside, post_gain.reshape(1, quarter), hidden_input],
    )


def solution(mesh):
    in_specs = (
        P("replica", "tensor"),
        P("replica", "tensor"),
        P("replica", None, None, "tensor"),
        P("replica", None, None, "tensor"),
        P("replica", None),
        P("replica"),
        P("replica"),
        P("replica"),
        P("tensor", None),
        P("tensor"),
    )
    out_specs = P("replica", "tensor")
    return jax.shard_map(shards, mesh=mesh, in_specs=in_specs, out_specs=out_specs, check_vma=False)
```

```python
import functools
import math

import jax
import jax.numpy as jnp
from jax import lax
from jax.experimental import pallas as pl
from jax.experimental.pallas import tpu as pltpu
from jax.sharding import PartitionSpec as P

HD = 256
softcap = 50.0
epsilon = 1e-06
score_scale = 1.0 / (softcap * math.sqrt(HD))
weight_scale = softcap * math.log2(math.e)
EXTRA = 128
f32 = jnp.float32
bf16 = jnp.bfloat16
VMEM = pltpu.MemorySpace.VMEM
SMEM = pltpu.MemorySpace.SMEM
VMEM_SPEC = pl.BlockSpec(memory_space=VMEM)
SMEM_SPEC = pl.BlockSpec(memory_space=SMEM)
HBM_SPEC = pl.BlockSpec(memory_space=pltpu.MemorySpace.HBM)
PARAMS = pltpu.CompilerParams(vmem_limit_bytes=40 * 2**20)


def iota(shape, axis):
    return lax.broadcasted_iota(jnp.int32, shape, axis)


def heads_below(block, heads):
    return jnp.concatenate([block[:, h * HD : (h + 1) * HD] for h in range(heads)], axis=0)


def weights_of(scores, alive):
    return jnp.where(alive, jnp.exp2(weight_scale * jnp.tanh(scores * score_scale)), 0.0)


def order_of(replicas):
    return {8: (4, 5, 6, 1, 0, 7, 2, 3)}.get(replicas, tuple(range(replicas)))


def owners(owner_ref, order):
    requests = owner_ref.shape[1]
    rows, cols = iota((requests, requests), 0), iota((requests, requests), 1)
    owner = owner_ref[...]
    place = owner
    for i, replica in enumerate(order):
        if i != replica:
            place = jnp.where(owner == replica, i, place)
    by_col = jnp.broadcast_to(place, (requests, requests)).astype(f32)
    by_row = jnp.sum(jnp.where(rows == cols, by_col, 0.0), axis=1, keepdims=True)
    return by_row, by_col, rows, cols


def route_kernel(
    capacity, order, owner_hbm, group_hbm, queries_hbm, out_ref, owner_ref, group_ref, queries_ref, sems
):
    pairs = ((owner_hbm, owner_ref), (group_hbm, group_ref), (queries_hbm, queries_ref))
    copies = [pltpu.make_async_copy(a, b, sems.at[i]) for i, (a, b) in enumerate(pairs)]
    for copy in copies:
        copy.start()
    for copy in copies:
        copy.wait()
    requests, width = queries_ref.shape
    slots = out_ref.shape[0]
    by_row, by_col, rows, cols = owners(owner_ref, order)
    earlier = jnp.where((by_row == by_col) & (rows < cols), 1.0, 0.0)
    position = (by_col[:1] * capacity + jnp.sum(earlier, axis=0, keepdims=True)).astype(jnp.int32)
    matches = iota((slots, requests), 0) == position
    out_ref[:, :width] = jnp.dot(
        jnp.where(matches, 1.0, 0.0).astype(bf16), queries_ref[...], preferred_element_type=f32
    ).astype(bf16)
    numbered = (group_ref[...] + 1).astype(f32)
    mark = jnp.sum(jnp.where(matches, numbered, 0.0), axis=1, keepdims=True)
    out_ref[:, width:] = jnp.broadcast_to(mark, (slots, EXTRA)).astype(bf16)


def attend_own(block, first, live, queries_ref, cache_ref, num_ref, den_ref):
    requests, _, window, _ = cache_ref.shape
    heads = queries_ref.shape[1] // HD
    at = iota((block, block * window), 1)
    start = iota((block, block * window), 0) * window
    for i in range(requests // block):
        mine = slice(i * block, (i + 1) * block)
        there = slice(first + i * block, first + (i + 1) * block)
        stacked = heads_below(queries_ref[there, :], heads)
        keys = cache_ref[mine, 0].reshape(block * window, HD)
        values = cache_ref[mine, 1].reshape(block * window, HD)
        scores = lax.dot_general(
            stacked, keys, (((1,), (1,)), ((), ())), preferred_element_type=f32
        )
        alive = (at >= start) & (at < start + live[there])
        weights = weights_of(scores, jnp.concatenate([alive] * heads, axis=0))
        numerator = jnp.dot(weights.astype(bf16), values, preferred_element_type=f32)
        denominator = jnp.sum(weights, axis=1, keepdims=True)
        for h in range(heads):
            own = slice(h * block, (h + 1) * block)
            num_ref[mine, h * HD : (h + 1) * HD] = numerator[own]
            den_ref[mine, h * 128 : (h + 1) * 128] = jnp.broadcast_to(
                denominator[own], (block, 128)
            )


def down(row, rows, cols):
    return jnp.sum(jnp.where(rows == cols, row.astype(f32), 0.0), axis=1, keepdims=True)


def early_kernel(
    capacity,
    order,
    block,
    core_ref,
    owner_hbm,
    length_hbm,
    queries_hbm,
    cache_hbm,
    prompt_hbm,
    weight_hbm,
    back_ref,
    num_ref,
    den_ref,
    early_ref,
    last_hbm,
    owner_ref,
    length_ref,
    queries_ref,
    cache_ref,
    staged,
    sems,
    early_sems,
    last_sem,
):
    requests, slots = back_ref.shape
    parts = parts_of(prompt_hbm.shape[0])
    pairs = (
        (owner_hbm, owner_ref),
        (length_hbm, length_ref),
        (queries_hbm, queries_ref),
        (cache_hbm.at[pl.ds(0, cache_ref.shape[0])], cache_ref),
    )
    copies = [pltpu.make_async_copy(a, b, sems.at[i]) for i, (a, b) in enumerate(pairs)]
    quarter = last_hbm.shape[1]
    cols = pl.ds(pl.multiple_of((core_ref[0] + 2) * quarter, 128), quarter)
    stage = pltpu.make_async_copy(weight_hbm.at[:, cols], staged, last_sem)
    unstage = pltpu.make_async_copy(staged, last_hbm, last_sem)
    prompts = [
        pltpu.make_async_copy(prompt_hbm.at[parts[i]], early_ref.at[i], early_sems.at[i])
        for i in range(early_ref.shape[0])
    ]
    for copy in copies + [stage] + prompts:
        copy.start()
    for copy in copies:
        copy.wait()
    stage.wait()
    unstage.start()
    by_row, by_col, rows, cols = owners(owner_ref, order)
    earlier = jnp.where((by_row == by_col) & (cols < rows), 1.0, 0.0)
    rank = jnp.sum(earlier, axis=1, keepdims=True)
    position = (by_row * capacity + rank).astype(jnp.int32)
    back_ref[...] = jnp.where(iota((requests, slots), 1) == position, 1.0, 0.0).astype(bf16)
    live = down(length_ref[...], rows, cols).astype(jnp.int32)
    attend_own(block, 0, live, queries_ref, cache_ref, num_ref, den_ref)
    for copy in prompts + [unstage]:
        copy.wait()


def late_kernel(
    block,
    core_ref,
    length_hbm,
    queries_hbm,
    cache_hbm,
    weight_hbm,
    after_hbm,
    num_ref,
    den_ref,
    weight_ref,
    length_ref,
    queries_ref,
    cache_ref,
    sems,
    weight_sems,
):
    requests = queries_ref.shape[0]
    half = cache_ref.shape[0]
    first = requests - half
    pairs = (
        (length_hbm, length_ref),
        (queries_hbm, queries_ref),
        (cache_hbm.at[pl.ds(first, half)], cache_ref),
    )
    copies = [pltpu.make_async_copy(a, b, sems.at[i]) for i, (a, b) in enumerate(pairs)]
    quarter = weight_ref.shape[2]
    weight_copies = []
    for i, q in enumerate((1 - core_ref[0], 3 - core_ref[0], core_ref[0])):
        cols = pl.ds(pl.multiple_of(q * quarter, 128), quarter)
        weight_copies.append(
            pltpu.make_async_copy(weight_hbm.at[:, cols], weight_ref.at[i], weight_sems.at[i])
        )
    for copy in copies + weight_copies:
        copy.start()
    for copy in copies:
        copy.wait()
    rows, cols = iota((requests, requests), 0), iota((requests, requests), 1)
    live = down(length_ref[...], rows, cols).astype(jnp.int32)
    attend_own(block, first, live, queries_ref, cache_ref, num_ref, den_ref)
    for copy in weight_copies:
        copy.wait()


def parts_of(groups):
    return [(g, part) for g in range(groups) for part in range(2)]


def prompt_kernel(
    chunk,
    window,
    length_hbm,
    slots_ref,
    early_ref,
    cache_hbm,
    out_ref,
    length_ref,
    held,
    sorted_ref,
    done_ref,
    num_ref,
    den_ref,
    sems,
    length_sem,
):
    groups, _, size, _ = cache_hbm.shape
    slots = slots_ref.shape[0]
    width = slots_ref.shape[1] - EXTRA
    heads = width // HD
    parts = parts_of(groups)
    early = early_ref.shape[0]
    length_copy = pltpu.make_async_copy(length_hbm, length_ref, length_sem)
    length_copy.start()
    copies = {
        parts[i]: pltpu.make_async_copy(
            cache_hbm.at[parts[i]], held.at[i - early], sems.at[i - early]
        )
        for i in range(early, len(parts))
    }
    for part in parts[early:]:
        copies[part].start()

    def read(g, part, span):
        i = parts.index((g, part))
        return early_ref[i, span, :] if i < early else held[i - early, span, :]

    def pieces(total, rows):
        lanes = iota((1, EXTRA), 1)
        extra = jnp.zeros((rows, EXTRA), f32)
        for h in range(heads):
            rest = total[h * rows : (h + 1) * rows]
            for k in range(3):
                piece = rest.astype(bf16).astype(f32)
                rest = rest - piece
                extra = jnp.where(lanes == 3 * h + k, piece, extra)
        return extra.astype(bf16)

    def fold(weights):
        part = weights[:, :128]
        for k in range(1, weights.shape[1] // 128):
            part = part + weights[:, k * 128 : (k + 1) * 128]
        return part

    rows, cols = iota((slots, slots), 0), iota((slots, slots), 1)
    by_row = jnp.broadcast_to(slots_ref[:, width : width + 1].astype(f32), (slots, slots))
    by_col = jnp.sum(jnp.where(rows == cols, by_row, 0.0), axis=0, keepdims=True)
    same = by_row == by_col
    rank_row = jnp.sum(jnp.where(same & (cols < rows), 1.0, 0.0), axis=1, keepdims=True)
    rank_col = jnp.sum(jnp.where(same & (rows < cols), 1.0, 0.0), axis=0, keepdims=True)
    length_copy.wait()
    crowded = jnp.max(jnp.where(by_col > 0.0, rank_col, 0.0)) >= window

    at_row = (by_row[:, :1] - 1.0) * window + rank_row
    at_row = jnp.where(by_row[:, :1] > 0.0, at_row, -1.0).astype(jnp.int32)
    at_col = jnp.where(by_col > 0.0, (by_col - 1.0) * window + rank_col, -1.0).astype(jnp.int32)
    room = groups * window
    there = jnp.where(iota((room, slots), 0) == at_col, 1.0, 0.0).astype(bf16)
    back = jnp.where(iota((slots, room), 1) == at_row, 1.0, 0.0).astype(bf16)
    for h in range(heads):
        part = jnp.dot(there, slots_ref[:, h * HD : (h + 1) * HD], preferred_element_type=f32)
        for g in range(groups):
            at = (g * heads + h) * window
            sorted_ref[at : at + window, :] = part[g * window : (g + 1) * window].astype(bf16)
    scores = [None] * groups
    waited = early
    everything = slice(0, size)
    for u in range(groups + 1):
        needed = min(2 * u + 1, len(parts))
        if needed > waited:
            needed = min(needed + 1, len(parts))
            for part in parts[waited:needed]:
                copies[part].wait()
            waited = needed
        if u < groups:
            scores[u] = lax.dot_general(
                sorted_ref[u * heads * window : (u + 1) * heads * window, :],
                read(u, 0, everything),
                (((1,), (1,)), ((), ())),
                preferred_element_type=f32,
            )
        if u > 0:
            g = u - 1
            weights = weights_of(scores[g], iota((1, size), 1) < length_ref[g])
            num = jnp.dot(
                weights.astype(bf16), read(g, 1, everything), preferred_element_type=f32
            )
            mine = slice(g * window, (g + 1) * window)
            for h in range(heads):
                done_ref[mine, h * HD : (h + 1) * HD] = num[
                    h * window : (h + 1) * window
                ].astype(bf16)
            den = jnp.sum(fold(weights), axis=1, keepdims=True)
            done_ref[mine, width:] = pieces(den, window)
    out_ref[...] = jnp.dot(back, done_ref[...], preferred_element_type=f32).astype(bf16)

    @pl.when(crowded)
    def _():
        stacked = heads_below(slots_ref[:, :width], heads)
        mark = jnp.concatenate([by_row[:, :1]] * heads, axis=0)
        num_ref[...] = jnp.zeros_like(num_ref)
        den_ref[...] = jnp.zeros_like(den_ref)
        for g in range(groups):
            limit = jnp.where(mark == g + 1.0, length_ref[g], 0)

            @pl.loop(0, (length_ref[g] + chunk - 1) // chunk)
            def _(c):
                span = pl.ds(pl.multiple_of(c * chunk, chunk), chunk)
                scores = lax.dot_general(
                    stacked,
                    read(g, 0, span),
                    (((1,), (1,)), ((), ())),
                    preferred_element_type=f32,
                )
                alive = iota((heads * slots, chunk), 1) < limit - c * chunk
                weights = weights_of(scores, alive)
                num_ref[...] += jnp.dot(
                    weights.astype(bf16), read(g, 1, span), preferred_element_type=f32
                )
                den_ref[...] += fold(weights)

        for h in range(heads):
            out_ref[:, h * HD : (h + 1) * HD] = num_ref[h * slots : (h + 1) * slots].astype(bf16)
        out_ref[:, width:] = pieces(jnp.sum(den_ref[...], axis=1, keepdims=True), slots)


def combine_kernel(
    returned_ref, back_ref, num_a, den_a, num_b, den_b, weight_ref, att_ref, give_ref
):
    quarter = weight_ref.shape[2]
    width = num_a.shape[1]
    heads = width // HD
    mine = jnp.dot(back_ref[...], returned_ref[...], preferred_element_type=f32)
    for h in range(heads):
        cols = slice(h * HD, (h + 1) * HD)
        numerator = mine[:, cols] + jnp.concatenate([num_a[:, cols], num_b[:, cols]], axis=0)
        at = width + 3 * h
        lane = slice(h * 128, h * 128 + 1)
        denominator = jnp.concatenate([den_a[:, lane], den_b[:, lane]], axis=0) + (
            mine[:, at : at + 1] + mine[:, at + 1 : at + 2] + mine[:, at + 2 : at + 3]
        )
        att_ref[:, cols] = (numerator / denominator).astype(bf16)
    for i in range(2):
        give_ref[:, i * quarter : (i + 1) * quarter] = jnp.dot(
            att_ref[...], weight_ref[i], preferred_element_type=f32
        ).astype(bf16)


def own_kernel(att_ref, weight_ref, last_ref, own_ref):
    quarter = weight_ref.shape[2]
    own_ref[:, :quarter] = jnp.dot(att_ref[...], weight_ref[2], preferred_element_type=f32)
    own_ref[:, quarter:] = jnp.dot(att_ref[...], last_ref[...], preferred_element_type=f32)


def chip_kernel(own_ref, got_ref, sum_ref, send_ref):
    total = own_ref[...] + got_ref[...].astype(f32)
    sum_ref[...] = total
    send_ref[...] = total.astype(bf16)


def square_kernel(row_ref, sum_ref, got_ref, mine_ref, square_ref):
    width = mine_ref.shape[1]
    total = sum_ref[...] + got_ref[...].astype(f32)
    part = jnp.zeros(square_ref.shape, f32)
    for k in range(total.shape[1] // 128):
        piece = total[:, k * 128 : (k + 1) * 128]
        part = part + piece * piece
    square_ref[...] = part
    mine_ref[...] = jnp.where(row_ref[0] == 0, total[:, :width], total[:, width:])


def final_kernel(features, mine_ref, square_ref, got_ref, gain_ref, hidden_ref, out_ref):
    square = jnp.sum(square_ref[...] + got_ref[...], axis=1, keepdims=True)
    scale = lax.rsqrt(square * (1.0 / features) + epsilon)
    normed = mine_ref[...] * scale * gain_ref[...]
    out_ref[...] = (hidden_ref[...].astype(f32) + normed).astype(bf16)


def call(kernel, outs, ins, **kw):
    specs = [
        pl.BlockSpec(memory_space=SMEM if a.ndim == 1 else VMEM) for a in ins
    ]
    return pl.pallas_call(
        kernel,
        out_shape=outs,
        in_specs=specs,
        out_specs=jax.tree.map(lambda _: pl.BlockSpec(memory_space=VMEM), outs),
        compiler_params=PARAMS,
        **kw,
    )(*ins)


def in_hbm(*arrays):
    return [pltpu.with_memory_space_constraint(a, pltpu.MemorySpace.HBM) for a in arrays]


def shape(dims, dtype):
    return jax.ShapeDtypeStruct(dims, dtype)


def shards(
    hidden_input,
    queries,
    prompt_cache,
    suffix_cache,
    owner_replica,
    group_slot,
    prompt_length,
    suffix_length,
    output_weight,
    post_gain,
):
    replicas = lax.axis_size("replica")
    ranks = lax.axis_size("tensor")
    requests, width = queries.shape
    capacity = max(2, (2 * requests + replicas - 1) // replicas)
    slots = replicas * capacity
    groups, _, size, _ = prompt_cache.shape
    window = suffix_cache.shape[2]
    features = output_weight.shape[1]
    quarter = features // ranks
    heads = width // HD
    order = order_of(replicas)
    index = lax.axis_index("tensor")
    core = (index % 2).reshape(1)
    far_row = (index // 2).reshape(1)

    def exchange(x):
        blocks = x.reshape(replicas, capacity, width + EXTRA)
        blocks = lax.all_to_all(
            blocks, "replica", split_axis=0, concat_axis=0, axis_index_groups=[order], tiled=True
        )
        return blocks.reshape(slots, width + EXTRA)

    def permute(x, bit):
        return lax.ppermute(x, "tensor", [(i, i ^ bit) for i in range(ranks)])

    owner_row = owner_replica.reshape(1, requests)
    sent = pl.pallas_call(
        functools.partial(route_kernel, capacity, order),
        out_shape=pltpu.VMEM((slots, width + EXTRA), bf16),
        in_specs=[HBM_SPEC] * 3,
        out_specs=VMEM_SPEC,
        scratch_shapes=[
            pltpu.VMEM((1, requests), jnp.int32),
            pltpu.VMEM((1, requests), jnp.int32),
            pltpu.VMEM((requests, width), bf16),
            pltpu.SemaphoreType.DMA((3,)),
        ],
        compiler_params=PARAMS,
    )(*in_hbm(owner_row, group_slot.reshape(1, requests), queries))
    got = exchange(sent)

    early = 3
    half = requests // 2
    block = math.gcd(16, half)
    length_row = suffix_length.reshape(1, requests)
    halves = [shape((half, width), f32), shape((half, heads * 128), f32)]
    row = pltpu.VMEM((1, requests), jnp.int32)
    own_scratch = [
        row,
        pltpu.VMEM((requests, width), bf16),
        pltpu.VMEM((half,) + suffix_cache.shape[1:], bf16),
    ]
    back, num_a, den_a, prefetched, last = pl.pallas_call(
        functools.partial(early_kernel, capacity, order, block),
        out_shape=[shape((requests, slots), bf16)]
        + halves
        + [pltpu.VMEM((early, size, HD), bf16), pltpu.HBM((width, quarter), bf16)],
        in_specs=[SMEM_SPEC] + [HBM_SPEC] * 6,
        out_specs=[VMEM_SPEC] * 4 + [HBM_SPEC],
        scratch_shapes=[row]
        + own_scratch
        + [
            pltpu.VMEM((width, quarter), bf16),
            pltpu.SemaphoreType.DMA((4,)),
            pltpu.SemaphoreType.DMA((early,)),
            pltpu.SemaphoreType.DMA,
        ],
        compiler_params=PARAMS,
        cost_estimate=pl.CostEstimate(
            flops=4 * requests * window * HD * block,
            bytes_accessed=2 * early * size * HD * 2 + suffix_cache.size,
            transcendentals=0,
        ),
    )(
        core,
        *in_hbm(owner_row, length_row, queries, suffix_cache, prompt_cache, output_weight),
    )

    chunk = math.gcd(512, size)
    fit = min(48, slots)
    answered = pl.pallas_call(
        functools.partial(prompt_kernel, chunk, fit),
        out_shape=pltpu.VMEM((slots, width + EXTRA), bf16),
        in_specs=[HBM_SPEC, VMEM_SPEC, VMEM_SPEC, HBM_SPEC],
        out_specs=VMEM_SPEC,
        scratch_shapes=[
            pltpu.SMEM((groups,), jnp.int32),
            pltpu.VMEM((2 * groups - early, size, HD), bf16),
            pltpu.VMEM((groups * heads * fit, HD), bf16),
            pltpu.VMEM((groups * fit, width + EXTRA), bf16),
            pltpu.VMEM((heads * slots, HD), f32),
            pltpu.VMEM((heads * slots, 128), f32),
            pltpu.SemaphoreType.DMA((2 * groups - early,)),
            pltpu.SemaphoreType.DMA,
        ],
        compiler_params=PARAMS,
    )(
        *in_hbm(prompt_length),
        got,
        pltpu.with_memory_space_constraint(prefetched, VMEM),
        *in_hbm(prompt_cache),
    )
    returned = exchange(answered)

    num_b, den_b, weight = pl.pallas_call(
        functools.partial(late_kernel, block),
        out_shape=halves + [pltpu.VMEM((3, width, quarter), bf16)],
        in_specs=[SMEM_SPEC] + [HBM_SPEC] * 5,
        out_specs=[VMEM_SPEC] * 3,
        scratch_shapes=own_scratch
        + [pltpu.SemaphoreType.DMA((3,)), pltpu.SemaphoreType.DMA((3,))],
        compiler_params=PARAMS,
        cost_estimate=pl.CostEstimate(
            flops=4 * requests * window * HD * block,
            bytes_accessed=suffix_cache.size + output_weight.size * 2,
            transcendentals=0,
        ),
    )(core, *in_hbm(length_row, queries, suffix_cache, output_weight, answered))
    weight = pltpu.with_memory_space_constraint(weight, VMEM)

    attention, give = call(
        combine_kernel,
        [shape((requests, width), bf16), shape((requests, 2 * quarter), bf16)],
        [returned, back, num_a, den_a, num_b, den_b, weight],
    )
    received = permute(give, 1)
    own = call(
        own_kernel,
        shape((requests, 2 * quarter), f32),
        [attention, weight, last],
    )
    chip, send = call(
        chip_kernel,
        [shape((requests, 2 * quarter), f32), shape((requests, 2 * quarter), bf16)],
        [own, received],
    )
    far = permute(send, 2)
    mine, square = call(
        square_kernel,
        [shape((requests, quarter), f32), shape((requests, 128), f32)],
        [far_row, chip, far],
    )
    beside = permute(square, 1)
    return call(
        functools.partial(final_kernel, features),
        shape((requests, quarter), bf16),
        [mine, square, beside, post_gain.reshape(1, quarter), hidden_input],
    )


def solution(mesh):
    in_specs = (
        P("replica", "tensor"),
        P("replica", "tensor"),
        P("replica", None, None, "tensor"),
        P("replica", None, None, "tensor"),
        P("replica", None),
        P("replica"),
        P("replica"),
        P("replica"),
        P("tensor", None),
        P("tensor"),
    )
    out_specs = P("replica", "tensor")
    return jax.shard_map(shards, mesh=mesh, in_specs=in_specs, out_specs=out_specs, check_vma=False)
```

```python
import functools
import math

import jax
import jax.numpy as jnp
from jax import lax
from jax.experimental import pallas as pl
from jax.experimental.pallas import tpu as pltpu
from jax.sharding import PartitionSpec as P

HD = 256
softcap = 50.0
epsilon = 1e-06
score_scale = 1.0 / (softcap * math.sqrt(HD))
weight_scale = softcap * math.log2(math.e)
EXTRA = 128
f32 = jnp.float32
bf16 = jnp.bfloat16
VMEM = pltpu.MemorySpace.VMEM
SMEM = pltpu.MemorySpace.SMEM
VMEM_SPEC = pl.BlockSpec(memory_space=VMEM)
SMEM_SPEC = pl.BlockSpec(memory_space=SMEM)
HBM_SPEC = pl.BlockSpec(memory_space=pltpu.MemorySpace.HBM)
PARAMS = pltpu.CompilerParams(vmem_limit_bytes=40 * 2**20)


def iota(shape, axis):
    return lax.broadcasted_iota(jnp.int32, shape, axis)


def heads_below(block, heads):
    return jnp.concatenate([block[:, h * HD : (h + 1) * HD] for h in range(heads)], axis=0)


def weights_of(scores, alive):
    return jnp.where(alive, jnp.exp2(weight_scale * jnp.tanh(scores * score_scale)), 0.0)


def orders_of(replicas):
    tuned = {8: ((4, 5, 6, 1, 0, 7, 2, 3), (5, 7, 2, 4, 6, 1, 3, 0))}
    return tuned.get(replicas, (tuple(range(replicas)),) * 2)


def owners(owner_ref, order):
    requests = owner_ref.shape[1]
    rows, cols = iota((requests, requests), 0), iota((requests, requests), 1)
    owner = owner_ref[...]
    place = owner
    for i, replica in enumerate(order):
        if i != replica:
            place = jnp.where(owner == replica, i, place)
    by_col = jnp.broadcast_to(place, (requests, requests)).astype(f32)
    by_row = jnp.sum(jnp.where(rows == cols, by_col, 0.0), axis=1, keepdims=True)
    return by_row, by_col, rows, cols


def route_kernel(
    capacity, order, owner_hbm, group_hbm, queries_hbm, out_ref, owner_ref, group_ref, queries_ref, sems
):
    pairs = ((owner_hbm, owner_ref), (group_hbm, group_ref), (queries_hbm, queries_ref))
    copies = [pltpu.make_async_copy(a, b, sems.at[i]) for i, (a, b) in enumerate(pairs)]
    for copy in copies:
        copy.start()
    for copy in copies:
        copy.wait()
    requests, width = queries_ref.shape
    slots = out_ref.shape[0]
    by_row, by_col, rows, cols = owners(owner_ref, order)
    earlier = jnp.where((by_row == by_col) & (rows < cols), 1.0, 0.0)
    position = (by_col[:1] * capacity + jnp.sum(earlier, axis=0, keepdims=True)).astype(jnp.int32)
    matches = iota((slots, requests), 0) == position
    out_ref[:, :width] = jnp.dot(
        jnp.where(matches, 1.0, 0.0).astype(bf16), queries_ref[...], preferred_element_type=f32
    ).astype(bf16)
    numbered = (group_ref[...] + 1).astype(f32)
    mark = jnp.sum(jnp.where(matches, numbered, 0.0), axis=1, keepdims=True)
    out_ref[:, width:] = jnp.broadcast_to(mark, (slots, EXTRA)).astype(bf16)


def attend_own(block, first, live, queries_ref, cache_ref, num_ref, den_ref):
    requests, _, window, _ = cache_ref.shape
    heads = queries_ref.shape[1] // HD
    at = iota((block, block * window), 1)
    start = iota((block, block * window), 0) * window
    for i in range(requests // block):
        mine = slice(i * block, (i + 1) * block)
        there = slice(first + i * block, first + (i + 1) * block)
        stacked = heads_below(queries_ref[there, :], heads)
        keys = cache_ref[mine, 0].reshape(block * window, HD)
        values = cache_ref[mine, 1].reshape(block * window, HD)
        scores = lax.dot_general(
            stacked, keys, (((1,), (1,)), ((), ())), preferred_element_type=f32
        )
        alive = (at >= start) & (at < start + live[there])
        weights = weights_of(scores, jnp.concatenate([alive] * heads, axis=0))
        numerator = jnp.dot(weights.astype(bf16), values, preferred_element_type=f32)
        denominator = jnp.sum(weights, axis=1, keepdims=True)
        for h in range(heads):
            own = slice(h * block, (h + 1) * block)
            num_ref[mine, h * HD : (h + 1) * HD] = numerator[own]
            den_ref[mine, h * 128 : (h + 1) * 128] = jnp.broadcast_to(
                denominator[own], (block, 128)
            )


def down(row, rows, cols):
    return jnp.sum(jnp.where(rows == cols, row.astype(f32), 0.0), axis=1, keepdims=True)


def early_kernel(
    capacity,
    order,
    block,
    core_ref,
    owner_hbm,
    length_hbm,
    queries_hbm,
    cache_hbm,
    prompt_hbm,
    weight_hbm,
    back_ref,
    num_ref,
    den_ref,
    early_ref,
    last_hbm,
    owner_ref,
    length_ref,
    queries_ref,
    cache_ref,
    staged,
    sems,
    early_sems,
    last_sem,
):
    requests, slots = back_ref.shape
    parts = parts_of(prompt_hbm.shape[0])
    pairs = (
        (owner_hbm, owner_ref),
        (length_hbm, length_ref),
        (queries_hbm, queries_ref),
        (cache_hbm.at[pl.ds(0, cache_ref.shape[0])], cache_ref),
    )
    copies = [pltpu.make_async_copy(a, b, sems.at[i]) for i, (a, b) in enumerate(pairs)]
    quarter = last_hbm.shape[1]
    cols = pl.ds(pl.multiple_of((core_ref[0] + 2) * quarter, 128), quarter)
    stage = pltpu.make_async_copy(weight_hbm.at[:, cols], staged, last_sem)
    unstage = pltpu.make_async_copy(staged, last_hbm, last_sem)
    prompts = [
        pltpu.make_async_copy(prompt_hbm.at[parts[i]], early_ref.at[i], early_sems.at[i])
        for i in range(early_ref.shape[0])
    ]
    for copy in copies + [stage] + prompts:
        copy.start()
    for copy in copies:
        copy.wait()
    stage.wait()
    unstage.start()
    by_row, by_col, rows, cols = owners(owner_ref, order)
    earlier = jnp.where((by_row == by_col) & (cols < rows), 1.0, 0.0)
    rank = jnp.sum(earlier, axis=1, keepdims=True)
    position = (by_row * capacity + rank).astype(jnp.int32)
    back_ref[...] = jnp.where(iota((requests, slots), 1) == position, 1.0, 0.0).astype(bf16)
    live = down(length_ref[...], rows, cols).astype(jnp.int32)
    attend_own(block, 0, live, queries_ref, cache_ref, num_ref, den_ref)
    for copy in prompts + [unstage]:
        copy.wait()


def late_kernel(
    block,
    core_ref,
    length_hbm,
    queries_hbm,
    cache_hbm,
    weight_hbm,
    after_hbm,
    num_ref,
    den_ref,
    weight_ref,
    length_ref,
    queries_ref,
    cache_ref,
    sems,
    weight_sems,
):
    requests = queries_ref.shape[0]
    half = cache_ref.shape[0]
    first = requests - half
    pairs = (
        (length_hbm, length_ref),
        (queries_hbm, queries_ref),
        (cache_hbm.at[pl.ds(first, half)], cache_ref),
    )
    copies = [pltpu.make_async_copy(a, b, sems.at[i]) for i, (a, b) in enumerate(pairs)]
    quarter = weight_ref.shape[2]
    weight_copies = []
    for i, q in enumerate((1 - core_ref[0], 3 - core_ref[0], core_ref[0])):
        cols = pl.ds(pl.multiple_of(q * quarter, 128), quarter)
        weight_copies.append(
            pltpu.make_async_copy(weight_hbm.at[:, cols], weight_ref.at[i], weight_sems.at[i])
        )
    for copy in copies + weight_copies:
        copy.start()
    for copy in copies:
        copy.wait()
    rows, cols = iota((requests, requests), 0), iota((requests, requests), 1)
    live = down(length_ref[...], rows, cols).astype(jnp.int32)
    attend_own(block, first, live, queries_ref, cache_ref, num_ref, den_ref)
    for copy in weight_copies:
        copy.wait()


def parts_of(groups):
    return [(g, part) for g in range(groups) for part in range(2)]


def prompt_kernel(
    chunk,
    window,
    moves,
    length_hbm,
    slots_ref,
    early_ref,
    cache_hbm,
    out_ref,
    length_ref,
    held,
    sorted_ref,
    done_ref,
    num_ref,
    den_ref,
    sems,
    length_sem,
):
    groups, _, size, _ = cache_hbm.shape
    slots = slots_ref.shape[0]
    width = slots_ref.shape[1] - EXTRA
    heads = width // HD
    parts = parts_of(groups)
    early = early_ref.shape[0]
    length_copy = pltpu.make_async_copy(length_hbm, length_ref, length_sem)
    length_copy.start()
    copies = {
        parts[i]: pltpu.make_async_copy(
            cache_hbm.at[parts[i]], held.at[i - early], sems.at[i - early]
        )
        for i in range(early, len(parts))
    }
    for part in parts[early:]:
        copies[part].start()

    def read(g, part, span):
        i = parts.index((g, part))
        return early_ref[i, span, :] if i < early else held[i - early, span, :]

    def moved(block):
        if moves == sorted(moves):
            return block
        step = slots // len(moves)
        return jnp.concatenate([block[m * step : (m + 1) * step] for m in moves], axis=0)

    def pieces(total, rows):
        lanes = iota((1, EXTRA), 1)
        extra = jnp.zeros((rows, EXTRA), f32)
        for h in range(heads):
            rest = total[h * rows : (h + 1) * rows]
            for k in range(3):
                piece = rest.astype(bf16).astype(f32)
                rest = rest - piece
                extra = jnp.where(lanes == 3 * h + k, piece, extra)
        return extra.astype(bf16)

    def fold(weights):
        part = weights[:, :128]
        for k in range(1, weights.shape[1] // 128):
            part = part + weights[:, k * 128 : (k + 1) * 128]
        return part

    rows, cols = iota((slots, slots), 0), iota((slots, slots), 1)
    by_row = jnp.broadcast_to(slots_ref[:, width : width + 1].astype(f32), (slots, slots))
    by_col = jnp.sum(jnp.where(rows == cols, by_row, 0.0), axis=0, keepdims=True)
    same = by_row == by_col
    rank_row = jnp.sum(jnp.where(same & (cols < rows), 1.0, 0.0), axis=1, keepdims=True)
    rank_col = jnp.sum(jnp.where(same & (rows < cols), 1.0, 0.0), axis=0, keepdims=True)
    length_copy.wait()
    crowded = jnp.max(jnp.where(by_col > 0.0, rank_col, 0.0)) >= window

    at_row = (by_row[:, :1] - 1.0) * window + rank_row
    at_row = jnp.where(by_row[:, :1] > 0.0, at_row, -1.0).astype(jnp.int32)
    at_col = jnp.where(by_col > 0.0, (by_col - 1.0) * window + rank_col, -1.0).astype(jnp.int32)
    room = groups * window
    there = jnp.where(iota((room, slots), 0) == at_col, 1.0, 0.0).astype(bf16)
    back = jnp.where(iota((slots, room), 1) == moved(at_row), 1.0, 0.0).astype(bf16)
    for h in range(heads):
        part = jnp.dot(there, slots_ref[:, h * HD : (h + 1) * HD], preferred_element_type=f32)
        for g in range(groups):
            at = (g * heads + h) * window
            sorted_ref[at : at + window, :] = part[g * window : (g + 1) * window].astype(bf16)
    scores = [None] * groups
    waited = early
    everything = slice(0, size)
    for u in range(groups + 1):
        needed = min(2 * u + 1, len(parts))
        if needed > waited:
            needed = min(needed + 1, len(parts))
            for part in parts[waited:needed]:
                copies[part].wait()
            waited = needed
        if u < groups:
            scores[u] = lax.dot_general(
                sorted_ref[u * heads * window : (u + 1) * heads * window, :],
                read(u, 0, everything),
                (((1,), (1,)), ((), ())),
                preferred_element_type=f32,
            )
        if u > 0:
            g = u - 1
            weights = weights_of(scores[g], iota((1, size), 1) < length_ref[g])
            num = jnp.dot(
                weights.astype(bf16), read(g, 1, everything), preferred_element_type=f32
            )
            mine = slice(g * window, (g + 1) * window)
            for h in range(heads):
                done_ref[mine, h * HD : (h + 1) * HD] = num[
                    h * window : (h + 1) * window
                ].astype(bf16)
            den = jnp.sum(fold(weights), axis=1, keepdims=True)
            done_ref[mine, width:] = pieces(den, window)
    out_ref[...] = jnp.dot(back, done_ref[...], preferred_element_type=f32).astype(bf16)

    @pl.when(crowded)
    def _():
        stacked = heads_below(slots_ref[:, :width], heads)
        mark = jnp.concatenate([by_row[:, :1]] * heads, axis=0)
        num_ref[...] = jnp.zeros_like(num_ref)
        den_ref[...] = jnp.zeros_like(den_ref)
        for g in range(groups):
            limit = jnp.where(mark == g + 1.0, length_ref[g], 0)

            @pl.loop(0, (length_ref[g] + chunk - 1) // chunk)
            def _(c):
                span = pl.ds(pl.multiple_of(c * chunk, chunk), chunk)
                scores = lax.dot_general(
                    stacked,
                    read(g, 0, span),
                    (((1,), (1,)), ((), ())),
                    preferred_element_type=f32,
                )
                alive = iota((heads * slots, chunk), 1) < limit - c * chunk
                weights = weights_of(scores, alive)
                num_ref[...] += jnp.dot(
                    weights.astype(bf16), read(g, 1, span), preferred_element_type=f32
                )
                den_ref[...] += fold(weights)

        for h in range(heads):
            num = num_ref[h * slots : (h + 1) * slots]
            out_ref[:, h * HD : (h + 1) * HD] = moved(num).astype(bf16)
        extra = pieces(jnp.sum(den_ref[...], axis=1, keepdims=True), slots)
        out_ref[:, width:] = moved(extra.astype(f32)).astype(bf16)


def combine_kernel(
    returned_ref, back_ref, num_a, den_a, num_b, den_b, weight_ref, att_ref, give_ref
):
    quarter = weight_ref.shape[2]
    width = num_a.shape[1]
    heads = width // HD
    mine = jnp.dot(back_ref[...], returned_ref[...], preferred_element_type=f32)
    for h in range(heads):
        cols = slice(h * HD, (h + 1) * HD)
        numerator = mine[:, cols] + jnp.concatenate([num_a[:, cols], num_b[:, cols]], axis=0)
        at = width + 3 * h
        lane = slice(h * 128, h * 128 + 1)
        denominator = jnp.concatenate([den_a[:, lane], den_b[:, lane]], axis=0) + (
            mine[:, at : at + 1] + mine[:, at + 1 : at + 2] + mine[:, at + 2 : at + 3]
        )
        att_ref[:, cols] = (numerator / denominator).astype(bf16)
    for i in range(2):
        give_ref[:, i * quarter : (i + 1) * quarter] = jnp.dot(
            att_ref[...], weight_ref[i], preferred_element_type=f32
        ).astype(bf16)


def own_kernel(att_ref, weight_ref, last_ref, own_ref):
    quarter = weight_ref.shape[2]
    own_ref[:, :quarter] = jnp.dot(att_ref[...], weight_ref[2], preferred_element_type=f32)
    own_ref[:, quarter:] = jnp.dot(att_ref[...], last_ref[...], preferred_element_type=f32)


def chip_kernel(own_ref, got_ref, sum_ref, send_ref):
    total = own_ref[...] + got_ref[...].astype(f32)
    sum_ref[...] = total
    send_ref[...] = total.astype(bf16)


def square_kernel(row_ref, sum_ref, got_ref, mine_ref, square_ref):
    width = mine_ref.shape[1]
    total = sum_ref[...] + got_ref[...].astype(f32)
    part = jnp.zeros(square_ref.shape, f32)
    for k in range(total.shape[1] // 128):
        piece = total[:, k * 128 : (k + 1) * 128]
        part = part + piece * piece
    square_ref[...] = part
    mine_ref[...] = jnp.where(row_ref[0] == 0, total[:, :width], total[:, width:])


def final_kernel(features, mine_ref, square_ref, got_ref, gain_ref, hidden_ref, out_ref):
    square = jnp.sum(square_ref[...] + got_ref[...], axis=1, keepdims=True)
    scale = lax.rsqrt(square * (1.0 / features) + epsilon)
    normed = mine_ref[...] * scale * gain_ref[...]
    out_ref[...] = (hidden_ref[...].astype(f32) + normed).astype(bf16)


def call(kernel, outs, ins, **kw):
    specs = [
        pl.BlockSpec(memory_space=SMEM if a.ndim == 1 else VMEM) for a in ins
    ]
    return pl.pallas_call(
        kernel,
        out_shape=outs,
        in_specs=specs,
        out_specs=jax.tree.map(lambda _: pl.BlockSpec(memory_space=VMEM), outs),
        compiler_params=PARAMS,
        **kw,
    )(*ins)


def in_hbm(*arrays):
    return [pltpu.with_memory_space_constraint(a, pltpu.MemorySpace.HBM) for a in arrays]


def shape(dims, dtype):
    return jax.ShapeDtypeStruct(dims, dtype)


def shards(
    hidden_input,
    queries,
    prompt_cache,
    suffix_cache,
    owner_replica,
    group_slot,
    prompt_length,
    suffix_length,
    output_weight,
    post_gain,
):
    replicas = lax.axis_size("replica")
    ranks = lax.axis_size("tensor")
    requests, width = queries.shape
    capacity = max(2, (2 * requests + replicas - 1) // replicas)
    slots = replicas * capacity
    groups, _, size, _ = prompt_cache.shape
    window = suffix_cache.shape[2]
    features = output_weight.shape[1]
    quarter = features // ranks
    heads = width // HD
    there, back_again = orders_of(replicas)
    index = lax.axis_index("tensor")
    core = (index % 2).reshape(1)
    far_row = (index // 2).reshape(1)

    def exchange(x, order):
        blocks = x.reshape(replicas, capacity, width + EXTRA)
        blocks = lax.all_to_all(
            blocks, "replica", split_axis=0, concat_axis=0, axis_index_groups=[order], tiled=True
        )
        return blocks.reshape(slots, width + EXTRA)

    def permute(x, bit):
        return lax.ppermute(x, "tensor", [(i, i ^ bit) for i in range(ranks)])

    owner_row = owner_replica.reshape(1, requests)
    sent = pl.pallas_call(
        functools.partial(route_kernel, capacity, there),
        out_shape=pltpu.VMEM((slots, width + EXTRA), bf16),
        in_specs=[HBM_SPEC] * 3,
        out_specs=VMEM_SPEC,
        scratch_shapes=[
            pltpu.VMEM((1, requests), jnp.int32),
            pltpu.VMEM((1, requests), jnp.int32),
            pltpu.VMEM((requests, width), bf16),
            pltpu.SemaphoreType.DMA((3,)),
        ],
        compiler_params=PARAMS,
    )(*in_hbm(owner_row, group_slot.reshape(1, requests), queries))
    got = exchange(sent, there)

    early = 3
    half = requests // 2
    block = math.gcd(16, half)
    length_row = suffix_length.reshape(1, requests)
    halves = [shape((half, width), f32), shape((half, heads * 128), f32)]
    row = pltpu.VMEM((1, requests), jnp.int32)
    own_scratch = [
        row,
        pltpu.VMEM((requests, width), bf16),
        pltpu.VMEM((half,) + suffix_cache.shape[1:], bf16),
    ]
    back, num_a, den_a, prefetched, last = pl.pallas_call(
        functools.partial(early_kernel, capacity, back_again, block),
        out_shape=[shape((requests, slots), bf16)]
        + halves
        + [pltpu.VMEM((early, size, HD), bf16), pltpu.HBM((width, quarter), bf16)],
        in_specs=[SMEM_SPEC] + [HBM_SPEC] * 6,
        out_specs=[VMEM_SPEC] * 4 + [HBM_SPEC],
        scratch_shapes=[row]
        + own_scratch
        + [
            pltpu.VMEM((width, quarter), bf16),
            pltpu.SemaphoreType.DMA((4,)),
            pltpu.SemaphoreType.DMA((early,)),
            pltpu.SemaphoreType.DMA,
        ],
        compiler_params=PARAMS,
        cost_estimate=pl.CostEstimate(
            flops=4 * requests * window * HD * block,
            bytes_accessed=2 * early * size * HD * 2 + suffix_cache.size,
            transcendentals=0,
        ),
    )(
        core,
        *in_hbm(owner_row, length_row, queries, suffix_cache, prompt_cache, output_weight),
    )

    chunk = math.gcd(512, size)
    moves = [there.index(replica) for replica in back_again]
    fit = min(48, slots)
    answered = pl.pallas_call(
        functools.partial(prompt_kernel, chunk, fit, moves),
        out_shape=pltpu.VMEM((slots, width + EXTRA), bf16),
        in_specs=[HBM_SPEC, VMEM_SPEC, VMEM_SPEC, HBM_SPEC],
        out_specs=VMEM_SPEC,
        scratch_shapes=[
            pltpu.SMEM((groups,), jnp.int32),
            pltpu.VMEM((2 * groups - early, size, HD), bf16),
            pltpu.VMEM((groups * heads * fit, HD), bf16),
            pltpu.VMEM((groups * fit, width + EXTRA), bf16),
            pltpu.VMEM((heads * slots, HD), f32),
            pltpu.VMEM((heads * slots, 128), f32),
            pltpu.SemaphoreType.DMA((2 * groups - early,)),
            pltpu.SemaphoreType.DMA,
        ],
        compiler_params=PARAMS,
    )(
        *in_hbm(prompt_length),
        got,
        pltpu.with_memory_space_constraint(prefetched, VMEM),
        *in_hbm(prompt_cache),
    )
    returned = exchange(answered, back_again)

    num_b, den_b, weight = pl.pallas_call(
        functools.partial(late_kernel, block),
        out_shape=halves + [pltpu.VMEM((3, width, quarter), bf16)],
        in_specs=[SMEM_SPEC] + [HBM_SPEC] * 5,
        out_specs=[VMEM_SPEC] * 3,
        scratch_shapes=own_scratch
        + [pltpu.SemaphoreType.DMA((3,)), pltpu.SemaphoreType.DMA((3,))],
        compiler_params=PARAMS,
        cost_estimate=pl.CostEstimate(
            flops=4 * requests * window * HD * block,
            bytes_accessed=suffix_cache.size + output_weight.size * 2,
            transcendentals=0,
        ),
    )(core, *in_hbm(length_row, queries, suffix_cache, output_weight, answered))
    weight = pltpu.with_memory_space_constraint(weight, VMEM)

    attention, give = call(
        combine_kernel,
        [shape((requests, width), bf16), shape((requests, 2 * quarter), bf16)],
        [returned, back, num_a, den_a, num_b, den_b, weight],
    )
    received = permute(give, 1)
    own = call(
        own_kernel,
        shape((requests, 2 * quarter), f32),
        [attention, weight, last],
    )
    chip, send = call(
        chip_kernel,
        [shape((requests, 2 * quarter), f32), shape((requests, 2 * quarter), bf16)],
        [own, received],
    )
    far = permute(send, 2)
    mine, square = call(
        square_kernel,
        [shape((requests, quarter), f32), shape((requests, 128), f32)],
        [far_row, chip, far],
    )
    beside = permute(square, 1)
    return call(
        functools.partial(final_kernel, features),
        shape((requests, quarter), bf16),
        [mine, square, beside, post_gain.reshape(1, quarter), hidden_input],
    )


def solution(mesh):
    in_specs = (
        P("replica", "tensor"),
        P("replica", "tensor"),
        P("replica", None, None, "tensor"),
        P("replica", None, None, "tensor"),
        P("replica", None),
        P("replica"),
        P("replica"),
        P("replica"),
        P("tensor", None),
        P("tensor"),
    )
    out_specs = P("replica", "tensor")
    return jax.shard_map(shards, mesh=mesh, in_specs=in_specs, out_specs=out_specs, check_vma=False)
```

```python
import functools
import math

import jax
import jax.numpy as jnp
from jax import lax
from jax.experimental import pallas as pl
from jax.experimental.pallas import tpu as pltpu
from jax.sharding import PartitionSpec as P

HD = 256
softcap = 50.0
epsilon = 1e-06
score_scale = 1.0 / (softcap * math.sqrt(HD))
weight_scale = softcap * math.log2(math.e)
EXTRA = 128
f32 = jnp.float32
bf16 = jnp.bfloat16
VMEM = pltpu.MemorySpace.VMEM
SMEM = pltpu.MemorySpace.SMEM
VMEM_SPEC = pl.BlockSpec(memory_space=VMEM)
SMEM_SPEC = pl.BlockSpec(memory_space=SMEM)
HBM_SPEC = pl.BlockSpec(memory_space=pltpu.MemorySpace.HBM)
PARAMS = pltpu.CompilerParams(vmem_limit_bytes=40 * 2**20)


def iota(shape, axis):
    return lax.broadcasted_iota(jnp.int32, shape, axis)


def heads_below(block, heads):
    return jnp.concatenate([block[:, h * HD : (h + 1) * HD] for h in range(heads)], axis=0)


def weights_of(scores, alive):
    return jnp.where(alive, jnp.exp2(weight_scale * jnp.tanh(scores * score_scale)), 0.0)


def orders_of(replicas):
    tuned = {8: ((4, 5, 6, 1, 0, 7, 2, 3), (5, 7, 2, 4, 6, 1, 3, 0))}
    return tuned.get(replicas, (tuple(range(replicas)),) * 2)


def owners(owner_ref, order):
    requests = owner_ref.shape[1]
    rows, cols = iota((requests, requests), 0), iota((requests, requests), 1)
    owner = owner_ref[...]
    place = owner
    for i, replica in enumerate(order):
        if i != replica:
            place = jnp.where(owner == replica, i, place)
    by_col = jnp.broadcast_to(place, (requests, requests)).astype(f32)
    by_row = jnp.sum(jnp.where(rows == cols, by_col, 0.0), axis=1, keepdims=True)
    return by_row, by_col, rows, cols


def route_kernel(
    capacity, order, owner_hbm, group_hbm, queries_hbm, out_ref, owner_ref, group_ref, queries_ref, sems
):
    pairs = ((owner_hbm, owner_ref), (group_hbm, group_ref), (queries_hbm, queries_ref))
    copies = [pltpu.make_async_copy(a, b, sems.at[i]) for i, (a, b) in enumerate(pairs)]
    for copy in copies:
        copy.start()
    for copy in copies:
        copy.wait()
    requests, width = queries_ref.shape
    slots = out_ref.shape[0]
    by_row, by_col, rows, cols = owners(owner_ref, order)
    earlier = jnp.where((by_row == by_col) & (rows < cols), 1.0, 0.0)
    position = (by_col[:1] * capacity + jnp.sum(earlier, axis=0, keepdims=True)).astype(jnp.int32)
    matches = iota((slots, requests), 0) == position
    out_ref[:, :width] = jnp.dot(
        jnp.where(matches, 1.0, 0.0).astype(bf16), queries_ref[...], preferred_element_type=f32
    ).astype(bf16)
    numbered = (group_ref[...] + 1).astype(f32)
    mark = jnp.sum(jnp.where(matches, numbered, 0.0), axis=1, keepdims=True)
    out_ref[:, width:] = jnp.broadcast_to(mark, (slots, EXTRA)).astype(bf16)


def attend_own(block, first, live, queries_ref, cache_ref, num_ref, den_ref):
    requests, _, window, _ = cache_ref.shape
    heads = queries_ref.shape[1] // HD
    at = iota((block, block * window), 1)
    start = iota((block, block * window), 0) * window
    for i in range(requests // block):
        mine = slice(i * block, (i + 1) * block)
        there = slice(first + i * block, first + (i + 1) * block)
        stacked = heads_below(queries_ref[there, :], heads)
        keys = cache_ref[mine, 0].reshape(block * window, HD)
        values = cache_ref[mine, 1].reshape(block * window, HD)
        scores = lax.dot_general(
            stacked, keys, (((1,), (1,)), ((), ())), preferred_element_type=f32
        )
        alive = (at >= start) & (at < start + live[there])
        weights = weights_of(scores, jnp.concatenate([alive] * heads, axis=0))
        numerator = jnp.dot(weights.astype(bf16), values, preferred_element_type=f32)
        denominator = jnp.sum(weights, axis=1, keepdims=True)
        for h in range(heads):
            own = slice(h * block, (h + 1) * block)
            num_ref[mine, h * HD : (h + 1) * HD] = numerator[own]
            den_ref[mine, h * 128 : (h + 1) * 128] = jnp.broadcast_to(
                denominator[own], (block, 128)
            )


def down(row, rows, cols):
    return jnp.sum(jnp.where(rows == cols, row.astype(f32), 0.0), axis=1, keepdims=True)


def early_kernel(
    capacity,
    order,
    block,
    core_ref,
    owner_hbm,
    length_hbm,
    queries_hbm,
    cache_hbm,
    prompt_hbm,
    weight_hbm,
    back_ref,
    num_ref,
    den_ref,
    early_ref,
    last_hbm,
    owner_ref,
    length_ref,
    queries_ref,
    cache_ref,
    staged,
    sems,
    early_sems,
    last_sem,
):
    requests, slots = back_ref.shape
    parts = parts_of(prompt_hbm.shape[0])
    pairs = (
        (owner_hbm, owner_ref),
        (length_hbm, length_ref),
        (queries_hbm, queries_ref),
        (cache_hbm.at[pl.ds(0, cache_ref.shape[0])], cache_ref),
    )
    copies = [pltpu.make_async_copy(a, b, sems.at[i]) for i, (a, b) in enumerate(pairs)]
    quarter = last_hbm.shape[1]
    cols = pl.ds(pl.multiple_of((core_ref[0] + 2) * quarter, 128), quarter)
    stage = pltpu.make_async_copy(weight_hbm.at[:, cols], staged, last_sem)
    unstage = pltpu.make_async_copy(staged, last_hbm, last_sem)
    prompts = [
        pltpu.make_async_copy(prompt_hbm.at[parts[i]], early_ref.at[i], early_sems.at[i])
        for i in range(early_ref.shape[0])
    ]
    for copy in copies + [stage] + prompts:
        copy.start()
    for copy in copies:
        copy.wait()
    stage.wait()
    unstage.start()
    by_row, by_col, rows, cols = owners(owner_ref, order)
    earlier = jnp.where((by_row == by_col) & (cols < rows), 1.0, 0.0)
    rank = jnp.sum(earlier, axis=1, keepdims=True)
    position = (by_row * capacity + rank).astype(jnp.int32)
    back_ref[...] = jnp.where(iota((requests, slots), 1) == position, 1.0, 0.0).astype(bf16)
    live = down(length_ref[...], rows, cols).astype(jnp.int32)
    attend_own(block, 0, live, queries_ref, cache_ref, num_ref, den_ref)
    for copy in prompts + [unstage]:
        copy.wait()


def late_kernel(
    block,
    core_ref,
    length_hbm,
    queries_hbm,
    cache_hbm,
    weight_hbm,
    after_hbm,
    num_ref,
    den_ref,
    weight_ref,
    length_ref,
    queries_ref,
    cache_ref,
    sems,
    weight_sems,
):
    requests = queries_ref.shape[0]
    half = cache_ref.shape[0]
    first = requests - half
    pairs = (
        (length_hbm, length_ref),
        (queries_hbm, queries_ref),
        (cache_hbm.at[pl.ds(first, half)], cache_ref),
    )
    copies = [pltpu.make_async_copy(a, b, sems.at[i]) for i, (a, b) in enumerate(pairs)]
    quarter = weight_ref.shape[2]
    weight_copies = []
    for i, q in enumerate((1 - core_ref[0], 3 - core_ref[0], core_ref[0])):
        cols = pl.ds(pl.multiple_of(q * quarter, 128), quarter)
        weight_copies.append(
            pltpu.make_async_copy(weight_hbm.at[:, cols], weight_ref.at[i], weight_sems.at[i])
        )
    for copy in copies + weight_copies:
        copy.start()
    for copy in copies:
        copy.wait()
    rows, cols = iota((requests, requests), 0), iota((requests, requests), 1)
    live = down(length_ref[...], rows, cols).astype(jnp.int32)
    attend_own(block, first, live, queries_ref, cache_ref, num_ref, den_ref)
    for copy in weight_copies:
        copy.wait()


def parts_of(groups):
    return [(g, part) for g in range(groups) for part in range(2)]


def prompt_kernel(
    chunk,
    window,
    moves,
    length_hbm,
    slots_ref,
    early_ref,
    cache_hbm,
    out_ref,
    length_ref,
    held,
    sorted_ref,
    done_ref,
    num_ref,
    den_ref,
    sems,
    length_sem,
):
    groups, _, size, _ = cache_hbm.shape
    slots = slots_ref.shape[0]
    width = slots_ref.shape[1] - EXTRA
    heads = width // HD
    parts = parts_of(groups)
    early = early_ref.shape[0]
    length_copy = pltpu.make_async_copy(length_hbm, length_ref, length_sem)
    length_copy.start()
    copies = {
        parts[i]: pltpu.make_async_copy(
            cache_hbm.at[parts[i]], held.at[i - early], sems.at[i - early]
        )
        for i in range(early, len(parts))
    }
    for part in parts[early:]:
        copies[part].start()

    def read(g, part, span):
        i = parts.index((g, part))
        return early_ref[i, span, :] if i < early else held[i - early, span, :]

    def moved(block):
        if moves == sorted(moves):
            return block
        step = slots // len(moves)
        return jnp.concatenate([block[m * step : (m + 1) * step] for m in moves], axis=0)

    def pieces(total, rows):
        lanes = iota((1, EXTRA), 1)
        extra = jnp.zeros((rows, EXTRA), f32)
        for h in range(heads):
            rest = total[h * rows : (h + 1) * rows]
            for k in range(3):
                piece = rest.astype(bf16).astype(f32)
                rest = rest - piece
                extra = jnp.where(lanes == 3 * h + k, piece, extra)
        return extra.astype(bf16)

    def fold(weights):
        part = weights[:, :128]
        for k in range(1, weights.shape[1] // 128):
            part = part + weights[:, k * 128 : (k + 1) * 128]
        return part

    rows, cols = iota((slots, slots), 0), iota((slots, slots), 1)
    by_row = jnp.broadcast_to(slots_ref[:, width : width + 1].astype(f32), (slots, slots))
    by_col = jnp.sum(jnp.where(rows == cols, by_row, 0.0), axis=0, keepdims=True)
    same = by_row == by_col
    rank_row = jnp.sum(jnp.where(same & (cols < rows), 1.0, 0.0), axis=1, keepdims=True)
    rank_col = jnp.sum(jnp.where(same & (rows < cols), 1.0, 0.0), axis=0, keepdims=True)
    length_copy.wait()
    crowded = jnp.max(jnp.where(by_col > 0.0, rank_col, 0.0)) >= window

    at_row = (by_row[:, :1] - 1.0) * window + rank_row
    at_row = jnp.where(by_row[:, :1] > 0.0, at_row, -1.0).astype(jnp.int32)
    at_col = jnp.where(by_col > 0.0, (by_col - 1.0) * window + rank_col, -1.0).astype(jnp.int32)
    room = groups * window
    there = jnp.where(iota((room, slots), 0) == at_col, 1.0, 0.0).astype(bf16)
    back = jnp.where(iota((slots, room), 1) == moved(at_row), 1.0, 0.0).astype(bf16)
    for h in range(heads):
        part = jnp.dot(there, slots_ref[:, h * HD : (h + 1) * HD], preferred_element_type=f32)
        for g in range(groups):
            at = (g * heads + h) * window
            sorted_ref[at : at + window, :] = part[g * window : (g + 1) * window].astype(bf16)
    scores = [None] * groups
    waited = early
    everything = slice(0, size)
    for u in range(groups + 1):
        needed = min(2 * u + 1, len(parts))
        if needed > waited:
            needed = min(needed + 1, len(parts))
            for part in parts[waited:needed]:
                copies[part].wait()
            waited = needed
        if u < groups:
            scores[u] = lax.dot_general(
                sorted_ref[u * heads * window : (u + 1) * heads * window, :],
                read(u, 0, everything),
                (((1,), (1,)), ((), ())),
                preferred_element_type=f32,
            )
        if u > 0:
            g = u - 1
            weights = weights_of(scores[g], iota((1, size), 1) < length_ref[g])
            num = jnp.dot(
                weights.astype(bf16), read(g, 1, everything), preferred_element_type=f32
            )
            mine = slice(g * window, (g + 1) * window)
            for h in range(heads):
                done_ref[mine, h * HD : (h + 1) * HD] = num[
                    h * window : (h + 1) * window
                ].astype(bf16)
            den = jnp.sum(fold(weights), axis=1, keepdims=True)
            done_ref[mine, width:] = pieces(den, window)
    out_ref[...] = jnp.dot(back, done_ref[...], preferred_element_type=f32).astype(bf16)

    @pl.when(crowded)
    def _():
        stacked = heads_below(slots_ref[:, :width], heads)
        mark = jnp.concatenate([by_row[:, :1]] * heads, axis=0)
        num_ref[...] = jnp.zeros_like(num_ref)
        den_ref[...] = jnp.zeros_like(den_ref)
        for g in range(groups):
            limit = jnp.where(mark == g + 1.0, length_ref[g], 0)

            @pl.loop(0, (length_ref[g] + chunk - 1) // chunk)
            def _(c):
                span = pl.ds(pl.multiple_of(c * chunk, chunk), chunk)
                scores = lax.dot_general(
                    stacked,
                    read(g, 0, span),
                    (((1,), (1,)), ((), ())),
                    preferred_element_type=f32,
                )
                alive = iota((heads * slots, chunk), 1) < limit - c * chunk
                weights = weights_of(scores, alive)
                num_ref[...] += jnp.dot(
                    weights.astype(bf16), read(g, 1, span), preferred_element_type=f32
                )
                den_ref[...] += fold(weights)

        for h in range(heads):
            num = num_ref[h * slots : (h + 1) * slots]
            out_ref[:, h * HD : (h + 1) * HD] = moved(num).astype(bf16)
        extra = pieces(jnp.sum(den_ref[...], axis=1, keepdims=True), slots)
        out_ref[:, width:] = moved(extra.astype(f32)).astype(bf16)


def combine_kernel(
    returned_ref, back_ref, num_a, den_a, num_b, den_b, weight_ref, att_ref, give_ref
):
    width = num_a.shape[1]
    heads = width // HD
    mine = jnp.dot(back_ref[...], returned_ref[...], preferred_element_type=f32)
    for h in range(heads):
        cols = slice(h * HD, (h + 1) * HD)
        numerator = mine[:, cols] + jnp.concatenate([num_a[:, cols], num_b[:, cols]], axis=0)
        at = width + 3 * h
        lane = slice(h * 128, h * 128 + 1)
        denominator = jnp.concatenate([den_a[:, lane], den_b[:, lane]], axis=0) + (
            mine[:, at : at + 1] + mine[:, at + 1 : at + 2] + mine[:, at + 2 : at + 3]
        )
        att_ref[:, cols] = (numerator / denominator).astype(bf16)
    give_ref[...] = jnp.dot(att_ref[...], weight_ref[0], preferred_element_type=f32).astype(bf16)


def give_kernel(att_ref, weight_ref, give_ref):
    give_ref[...] = jnp.dot(att_ref[...], weight_ref[1], preferred_element_type=f32).astype(bf16)


def own_kernel(att_ref, weight_ref, own_ref):
    own_ref[...] = jnp.dot(att_ref[...], weight_ref[2], preferred_element_type=f32)


def chip_kernel(own_ref, got_ref, sum_ref, send_ref):
    total = own_ref[...] + got_ref[...].astype(f32)
    sum_ref[...] = total
    send_ref[...] = total.astype(bf16)


def last_kernel(att_ref, weight_ref, got_ref, after_ref, sum_ref, send_ref):
    total = jnp.dot(att_ref[...], weight_ref[...], preferred_element_type=f32)
    total = total + got_ref[...].astype(f32)
    sum_ref[...] = total
    send_ref[...] = total.astype(bf16)


def square_kernel(row_ref, sum_a, got_a, sum_b, got_b, mine_ref, square_ref):
    part = jnp.zeros(square_ref.shape, f32)
    totals = []
    for sum_ref, got_ref in ((sum_a, got_a), (sum_b, got_b)):
        total = sum_ref[...] + got_ref[...].astype(f32)
        for k in range(total.shape[1] // 128):
            piece = total[:, k * 128 : (k + 1) * 128]
            part = part + piece * piece
        totals.append(total)
    square_ref[...] = part
    mine_ref[...] = jnp.where(row_ref[0] == 0, totals[0], totals[1])


def final_kernel(features, mine_ref, square_ref, got_ref, gain_ref, hidden_ref, out_ref):
    square = jnp.sum(square_ref[...] + got_ref[...], axis=1, keepdims=True)
    scale = lax.rsqrt(square * (1.0 / features) + epsilon)
    normed = mine_ref[...] * scale * gain_ref[...]
    out_ref[...] = (hidden_ref[...].astype(f32) + normed).astype(bf16)


def call(kernel, outs, ins, **kw):
    specs = [
        pl.BlockSpec(memory_space=SMEM if a.ndim == 1 else VMEM) for a in ins
    ]
    return pl.pallas_call(
        kernel,
        out_shape=outs,
        in_specs=specs,
        out_specs=jax.tree.map(lambda _: pl.BlockSpec(memory_space=VMEM), outs),
        compiler_params=PARAMS,
        **kw,
    )(*ins)


def in_hbm(*arrays):
    return [pltpu.with_memory_space_constraint(a, pltpu.MemorySpace.HBM) for a in arrays]


def shape(dims, dtype):
    return jax.ShapeDtypeStruct(dims, dtype)


def shards(
    hidden_input,
    queries,
    prompt_cache,
    suffix_cache,
    owner_replica,
    group_slot,
    prompt_length,
    suffix_length,
    output_weight,
    post_gain,
):
    replicas = lax.axis_size("replica")
    ranks = lax.axis_size("tensor")
    requests, width = queries.shape
    capacity = max(2, (2 * requests + replicas - 1) // replicas)
    slots = replicas * capacity
    groups, _, size, _ = prompt_cache.shape
    window = suffix_cache.shape[2]
    features = output_weight.shape[1]
    quarter = features // ranks
    heads = width // HD
    there, back_again = orders_of(replicas)
    index = lax.axis_index("tensor")
    core = (index % 2).reshape(1)
    far_row = (index // 2).reshape(1)

    def exchange(x, order):
        blocks = x.reshape(replicas, capacity, width + EXTRA)
        blocks = lax.all_to_all(
            blocks, "replica", split_axis=0, concat_axis=0, axis_index_groups=[order], tiled=True
        )
        return blocks.reshape(slots, width + EXTRA)

    def permute(x, bit):
        return lax.ppermute(x, "tensor", [(i, i ^ bit) for i in range(ranks)])

    owner_row = owner_replica.reshape(1, requests)
    sent = pl.pallas_call(
        functools.partial(route_kernel, capacity, there),
        out_shape=pltpu.VMEM((slots, width + EXTRA), bf16),
        in_specs=[HBM_SPEC] * 3,
        out_specs=VMEM_SPEC,
        scratch_shapes=[
            pltpu.VMEM((1, requests), jnp.int32),
            pltpu.VMEM((1, requests), jnp.int32),
            pltpu.VMEM((requests, width), bf16),
            pltpu.SemaphoreType.DMA((3,)),
        ],
        compiler_params=PARAMS,
    )(*in_hbm(owner_row, group_slot.reshape(1, requests), queries))
    got = exchange(sent, there)

    early = 3
    half = requests // 2
    block = math.gcd(16, half)
    length_row = suffix_length.reshape(1, requests)
    halves = [shape((half, width), f32), shape((half, heads * 128), f32)]
    row = pltpu.VMEM((1, requests), jnp.int32)
    own_scratch = [
        row,
        pltpu.VMEM((requests, width), bf16),
        pltpu.VMEM((half,) + suffix_cache.shape[1:], bf16),
    ]
    back, num_a, den_a, prefetched, last = pl.pallas_call(
        functools.partial(early_kernel, capacity, back_again, block),
        out_shape=[shape((requests, slots), bf16)]
        + halves
        + [pltpu.VMEM((early, size, HD), bf16), pltpu.HBM((width, quarter), bf16)],
        in_specs=[SMEM_SPEC] + [HBM_SPEC] * 6,
        out_specs=[VMEM_SPEC] * 4 + [HBM_SPEC],
        scratch_shapes=[row]
        + own_scratch
        + [
            pltpu.VMEM((width, quarter), bf16),
            pltpu.SemaphoreType.DMA((4,)),
            pltpu.SemaphoreType.DMA((early,)),
            pltpu.SemaphoreType.DMA,
        ],
        compiler_params=PARAMS,
        cost_estimate=pl.CostEstimate(
            flops=4 * requests * window * HD * block,
            bytes_accessed=2 * early * size * HD * 2 + suffix_cache.size,
            transcendentals=0,
        ),
    )(
        core,
        *in_hbm(owner_row, length_row, queries, suffix_cache, prompt_cache, output_weight),
    )

    chunk = math.gcd(512, size)
    moves = [there.index(replica) for replica in back_again]
    fit = min(48, slots)
    answered = pl.pallas_call(
        functools.partial(prompt_kernel, chunk, fit, moves),
        out_shape=pltpu.VMEM((slots, width + EXTRA), bf16),
        in_specs=[HBM_SPEC, VMEM_SPEC, VMEM_SPEC, HBM_SPEC],
        out_specs=VMEM_SPEC,
        scratch_shapes=[
            pltpu.SMEM((groups,), jnp.int32),
            pltpu.VMEM((2 * groups - early, size, HD), bf16),
            pltpu.VMEM((groups * heads * fit, HD), bf16),
            pltpu.VMEM((groups * fit, width + EXTRA), bf16),
            pltpu.VMEM((heads * slots, HD), f32),
            pltpu.VMEM((heads * slots, 128), f32),
            pltpu.SemaphoreType.DMA((2 * groups - early,)),
            pltpu.SemaphoreType.DMA,
        ],
        compiler_params=PARAMS,
    )(
        *in_hbm(prompt_length),
        got,
        pltpu.with_memory_space_constraint(prefetched, VMEM),
        *in_hbm(prompt_cache),
    )
    returned = exchange(answered, back_again)

    num_b, den_b, weight = pl.pallas_call(
        functools.partial(late_kernel, block),
        out_shape=halves + [pltpu.VMEM((3, width, quarter), bf16)],
        in_specs=[SMEM_SPEC] + [HBM_SPEC] * 5,
        out_specs=[VMEM_SPEC] * 3,
        scratch_shapes=own_scratch
        + [pltpu.SemaphoreType.DMA((3,)), pltpu.SemaphoreType.DMA((3,))],
        compiler_params=PARAMS,
        cost_estimate=pl.CostEstimate(
            flops=4 * requests * window * HD * block,
            bytes_accessed=suffix_cache.size + output_weight.size * 2,
            transcendentals=0,
        ),
    )(core, *in_hbm(length_row, queries, suffix_cache, output_weight, answered))
    weight = pltpu.with_memory_space_constraint(weight, VMEM)

    block_f32 = shape((requests, quarter), f32)
    block_bf16 = shape((requests, quarter), bf16)
    attention, give_a = call(
        combine_kernel,
        [shape((requests, width), bf16), block_bf16],
        [returned, back, num_a, den_a, num_b, den_b, weight],
    )
    got_a = permute(give_a, 1)
    got_b = permute(call(give_kernel, block_bf16, [attention, weight]), 1)
    own_a = call(own_kernel, block_f32, [attention, weight])
    sum_a, send_a = call(chip_kernel, [block_f32, block_bf16], [own_a, got_a])
    far_a = permute(send_a, 2)
    sum_b, send_b = call(last_kernel, [block_f32, block_bf16], [attention, last, got_b, send_a])
    far_b = permute(send_b, 2)
    mine, square = call(
        square_kernel,
        [block_f32, shape((requests, 128), f32)],
        [far_row, sum_a, far_a, sum_b, far_b],
    )
    beside = permute(square, 1)
    return call(
        functools.partial(final_kernel, features),
        shape((requests, quarter), bf16),
        [mine, square, beside, post_gain.reshape(1, quarter), hidden_input],
    )


def solution(mesh):
    in_specs = (
        P("replica", "tensor"),
        P("replica", "tensor"),
        P("replica", None, None, "tensor"),
        P("replica", None, None, "tensor"),
        P("replica", None),
        P("replica"),
        P("replica"),
        P("replica"),
        P("tensor", None),
        P("tensor"),
    )
    out_specs = P("replica", "tensor")
    return jax.shard_map(shards, mesh=mesh, in_specs=in_specs, out_specs=out_specs, check_vma=False)
```

```python
import functools
import math

import jax
import jax.numpy as jnp
from jax import lax
from jax.experimental import pallas as pl
from jax.experimental.pallas import tpu as pltpu
from jax.sharding import PartitionSpec as P

HD = 256
softcap = 50.0
epsilon = 1e-06
score_scale = 1.0 / (softcap * math.sqrt(HD))
weight_scale = softcap * math.log2(math.e)
EXTRA = 128
f32 = jnp.float32
bf16 = jnp.bfloat16
VMEM = pltpu.MemorySpace.VMEM
SMEM = pltpu.MemorySpace.SMEM
VMEM_SPEC = pl.BlockSpec(memory_space=VMEM)
SMEM_SPEC = pl.BlockSpec(memory_space=SMEM)
HBM_SPEC = pl.BlockSpec(memory_space=pltpu.MemorySpace.HBM)
PARAMS = pltpu.CompilerParams(vmem_limit_bytes=40 * 2**20)


def iota(shape, axis):
    return lax.broadcasted_iota(jnp.int32, shape, axis)


def heads_below(block, heads):
    return jnp.concatenate([block[:, h * HD : (h + 1) * HD] for h in range(heads)], axis=0)


def weights_of(scores, alive):
    return jnp.where(alive, jnp.exp2(weight_scale * jnp.tanh(scores * score_scale)), 0.0)


def orders_of(replicas):
    tuned = {8: ((4, 3, 5, 1, 0, 7, 6, 2), (5, 7, 2, 4, 6, 1, 3, 0))}
    return tuned.get(replicas, (tuple(range(replicas)),) * 2)


def owners(owner_ref, order):
    requests = owner_ref.shape[1]
    rows, cols = iota((requests, requests), 0), iota((requests, requests), 1)
    owner = owner_ref[...]
    place = owner
    for i, replica in enumerate(order):
        if i != replica:
            place = jnp.where(owner == replica, i, place)
    by_col = jnp.broadcast_to(place, (requests, requests)).astype(f32)
    by_row = jnp.sum(jnp.where(rows == cols, by_col, 0.0), axis=1, keepdims=True)
    return by_row, by_col, rows, cols


def route_kernel(
    capacity, order, owner_hbm, group_hbm, queries_hbm, out_ref, owner_ref, group_ref, queries_ref, sems
):
    pairs = ((owner_hbm, owner_ref), (group_hbm, group_ref), (queries_hbm, queries_ref))
    copies = [pltpu.make_async_copy(a, b, sems.at[i]) for i, (a, b) in enumerate(pairs)]
    for copy in copies:
        copy.start()
    for copy in copies:
        copy.wait()
    requests, width = queries_ref.shape
    slots = out_ref.shape[0]
    by_row, by_col, rows, cols = owners(owner_ref, order)
    earlier = jnp.where((by_row == by_col) & (rows < cols), 1.0, 0.0)
    position = (by_col[:1] * capacity + jnp.sum(earlier, axis=0, keepdims=True)).astype(jnp.int32)
    matches = iota((slots, requests), 0) == position
    out_ref[:, :width] = jnp.dot(
        jnp.where(matches, 1.0, 0.0).astype(bf16), queries_ref[...], preferred_element_type=f32
    ).astype(bf16)
    numbered = (group_ref[...] + 1).astype(f32)
    mark = jnp.sum(jnp.where(matches, numbered, 0.0), axis=1, keepdims=True)
    out_ref[:, width:] = jnp.broadcast_to(mark, (slots, EXTRA)).astype(bf16)


def attend_own(block, first, live, queries_ref, cache_ref, num_ref, den_ref):
    requests, _, window, _ = cache_ref.shape
    heads = queries_ref.shape[1] // HD
    at = iota((block, block * window), 1)
    start = iota((block, block * window), 0) * window
    for i in range(requests // block):
        mine = slice(i * block, (i + 1) * block)
        there = slice(first + i * block, first + (i + 1) * block)
        stacked = heads_below(queries_ref[there, :], heads)
        keys = cache_ref[mine, 0].reshape(block * window, HD)
        values = cache_ref[mine, 1].reshape(block * window, HD)
        scores = lax.dot_general(
            stacked, keys, (((1,), (1,)), ((), ())), preferred_element_type=f32
        )
        alive = (at >= start) & (at < start + live[there])
        weights = weights_of(scores, jnp.concatenate([alive] * heads, axis=0))
        numerator = jnp.dot(weights.astype(bf16), values, preferred_element_type=f32)
        denominator = jnp.sum(weights, axis=1, keepdims=True)
        for h in range(heads):
            own = slice(h * block, (h + 1) * block)
            num_ref[mine, h * HD : (h + 1) * HD] = numerator[own]
            den_ref[mine, h * 128 : (h + 1) * 128] = jnp.broadcast_to(
                denominator[own], (block, 128)
            )


def down(row, rows, cols):
    return jnp.sum(jnp.where(rows == cols, row.astype(f32), 0.0), axis=1, keepdims=True)


def early_kernel(
    capacity,
    order,
    block,
    core_ref,
    owner_hbm,
    length_hbm,
    queries_hbm,
    cache_hbm,
    prompt_hbm,
    weight_hbm,
    back_ref,
    num_ref,
    den_ref,
    early_ref,
    last_hbm,
    owner_ref,
    length_ref,
    queries_ref,
    cache_ref,
    staged,
    sems,
    early_sems,
    last_sem,
):
    requests, slots = back_ref.shape
    parts = parts_of(prompt_hbm.shape[0])
    pairs = (
        (owner_hbm, owner_ref),
        (length_hbm, length_ref),
        (queries_hbm, queries_ref),
        (cache_hbm.at[pl.ds(0, cache_ref.shape[0])], cache_ref),
    )
    copies = [pltpu.make_async_copy(a, b, sems.at[i]) for i, (a, b) in enumerate(pairs)]
    quarter = last_hbm.shape[1]
    cols = pl.ds(pl.multiple_of((core_ref[0] + 2) * quarter, 128), quarter)
    stage = pltpu.make_async_copy(weight_hbm.at[:, cols], staged, last_sem)
    unstage = pltpu.make_async_copy(staged, last_hbm, last_sem)
    prompts = [
        pltpu.make_async_copy(prompt_hbm.at[parts[i]], early_ref.at[i], early_sems.at[i])
        for i in range(early_ref.shape[0])
    ]
    for copy in copies + [stage] + prompts:
        copy.start()
    for copy in copies:
        copy.wait()
    stage.wait()
    unstage.start()
    by_row, by_col, rows, cols = owners(owner_ref, order)
    earlier = jnp.where((by_row == by_col) & (cols < rows), 1.0, 0.0)
    rank = jnp.sum(earlier, axis=1, keepdims=True)
    position = (by_row * capacity + rank).astype(jnp.int32)
    back_ref[...] = jnp.where(iota((requests, slots), 1) == position, 1.0, 0.0).astype(bf16)
    live = down(length_ref[...], rows, cols).astype(jnp.int32)
    attend_own(block, 0, live, queries_ref, cache_ref, num_ref, den_ref)
    for copy in prompts + [unstage]:
        copy.wait()


def late_kernel(
    block,
    core_ref,
    length_hbm,
    queries_hbm,
    cache_hbm,
    weight_hbm,
    after_hbm,
    num_ref,
    den_ref,
    weight_ref,
    length_ref,
    queries_ref,
    cache_ref,
    sems,
    weight_sems,
):
    requests = queries_ref.shape[0]
    half = cache_ref.shape[0]
    first = requests - half
    pairs = (
        (length_hbm, length_ref),
        (queries_hbm, queries_ref),
        (cache_hbm.at[pl.ds(first, half)], cache_ref),
    )
    copies = [pltpu.make_async_copy(a, b, sems.at[i]) for i, (a, b) in enumerate(pairs)]
    quarter = weight_ref.shape[2]
    weight_copies = []
    for i, q in enumerate((1 - core_ref[0], 3 - core_ref[0], core_ref[0])):
        cols = pl.ds(pl.multiple_of(q * quarter, 128), quarter)
        weight_copies.append(
            pltpu.make_async_copy(weight_hbm.at[:, cols], weight_ref.at[i], weight_sems.at[i])
        )
    for copy in copies + weight_copies:
        copy.start()
    for copy in copies:
        copy.wait()
    rows, cols = iota((requests, requests), 0), iota((requests, requests), 1)
    live = down(length_ref[...], rows, cols).astype(jnp.int32)
    attend_own(block, first, live, queries_ref, cache_ref, num_ref, den_ref)
    for copy in weight_copies:
        copy.wait()


def parts_of(groups):
    return [(g, part) for g in range(groups) for part in range(2)]


def prompt_kernel(
    chunk,
    window,
    moves,
    length_hbm,
    slots_ref,
    early_ref,
    cache_hbm,
    out_ref,
    length_ref,
    held,
    sorted_ref,
    done_ref,
    num_ref,
    den_ref,
    sems,
    length_sem,
):
    groups, _, size, _ = cache_hbm.shape
    slots = slots_ref.shape[0]
    width = slots_ref.shape[1] - EXTRA
    heads = width // HD
    parts = parts_of(groups)
    early = early_ref.shape[0]
    length_copy = pltpu.make_async_copy(length_hbm, length_ref, length_sem)
    length_copy.start()
    copies = {
        parts[i]: pltpu.make_async_copy(
            cache_hbm.at[parts[i]], held.at[i - early], sems.at[i - early]
        )
        for i in range(early, len(parts))
    }
    for part in parts[early:]:
        copies[part].start()

    def read(g, part, span):
        i = parts.index((g, part))
        return early_ref[i, span, :] if i < early else held[i - early, span, :]

    def moved(block):
        if moves == sorted(moves):
            return block
        step = slots // len(moves)
        return jnp.concatenate([block[m * step : (m + 1) * step] for m in moves], axis=0)

    def pieces(total, rows):
        lanes = iota((1, EXTRA), 1)
        extra = jnp.zeros((rows, EXTRA), f32)
        for h in range(heads):
            rest = total[h * rows : (h + 1) * rows]
            for k in range(3):
                piece = rest.astype(bf16).astype(f32)
                rest = rest - piece
                extra = jnp.where(lanes == 3 * h + k, piece, extra)
        return extra.astype(bf16)

    def fold(weights):
        part = weights[:, :128]
        for k in range(1, weights.shape[1] // 128):
            part = part + weights[:, k * 128 : (k + 1) * 128]
        return part

    rows, cols = iota((slots, slots), 0), iota((slots, slots), 1)
    by_row = jnp.broadcast_to(slots_ref[:, width : width + 1].astype(f32), (slots, slots))
    by_col = jnp.sum(jnp.where(rows == cols, by_row, 0.0), axis=0, keepdims=True)
    same = by_row == by_col
    rank_row = jnp.sum(jnp.where(same & (cols < rows), 1.0, 0.0), axis=1, keepdims=True)
    rank_col = jnp.sum(jnp.where(same & (rows < cols), 1.0, 0.0), axis=0, keepdims=True)
    length_copy.wait()
    crowded = jnp.max(jnp.where(by_col > 0.0, rank_col, 0.0)) >= window

    at_row = (by_row[:, :1] - 1.0) * window + rank_row
    at_row = jnp.where(by_row[:, :1] > 0.0, at_row, -1.0).astype(jnp.int32)
    at_col = jnp.where(by_col > 0.0, (by_col - 1.0) * window + rank_col, -1.0).astype(jnp.int32)
    room = groups * window
    there = jnp.where(iota((room, slots), 0) == at_col, 1.0, 0.0).astype(bf16)
    back = jnp.where(iota((slots, room), 1) == moved(at_row), 1.0, 0.0).astype(bf16)
    for h in range(heads):
        part = jnp.dot(there, slots_ref[:, h * HD : (h + 1) * HD], preferred_element_type=f32)
        for g in range(groups):
            at = (g * heads + h) * window
            sorted_ref[at : at + window, :] = part[g * window : (g + 1) * window].astype(bf16)
    scores = [None] * groups
    waited = early
    everything = slice(0, size)
    for u in range(groups + 1):
        needed = min(2 * u + 1, len(parts))
        if needed > waited:
            needed = min(needed + 1, len(parts))
            for part in parts[waited:needed]:
                copies[part].wait()
            waited = needed
        if u < groups:
            scores[u] = lax.dot_general(
                sorted_ref[u * heads * window : (u + 1) * heads * window, :],
                read(u, 0, everything),
                (((1,), (1,)), ((), ())),
                preferred_element_type=f32,
            )
        if u > 0:
            g = u - 1
            weights = weights_of(scores[g], iota((1, size), 1) < length_ref[g])
            num = jnp.dot(
                weights.astype(bf16), read(g, 1, everything), preferred_element_type=f32
            )
            mine = slice(g * window, (g + 1) * window)
            for h in range(heads):
                done_ref[mine, h * HD : (h + 1) * HD] = num[
                    h * window : (h + 1) * window
                ].astype(bf16)
            den = jnp.sum(fold(weights), axis=1, keepdims=True)
            done_ref[mine, width:] = pieces(den, window)
    out_ref[...] = jnp.dot(back, done_ref[...], preferred_element_type=f32).astype(bf16)

    @pl.when(crowded)
    def _():
        stacked = heads_below(slots_ref[:, :width], heads)
        mark = jnp.concatenate([by_row[:, :1]] * heads, axis=0)
        num_ref[...] = jnp.zeros_like(num_ref)
        den_ref[...] = jnp.zeros_like(den_ref)
        for g in range(groups):
            limit = jnp.where(mark == g + 1.0, length_ref[g], 0)

            @pl.loop(0, (length_ref[g] + chunk - 1) // chunk)
            def _(c):
                span = pl.ds(pl.multiple_of(c * chunk, chunk), chunk)
                scores = lax.dot_general(
                    stacked,
                    read(g, 0, span),
                    (((1,), (1,)), ((), ())),
                    preferred_element_type=f32,
                )
                alive = iota((heads * slots, chunk), 1) < limit - c * chunk
                weights = weights_of(scores, alive)
                num_ref[...] += jnp.dot(
                    weights.astype(bf16), read(g, 1, span), preferred_element_type=f32
                )
                den_ref[...] += fold(weights)

        for h in range(heads):
            num = num_ref[h * slots : (h + 1) * slots]
            out_ref[:, h * HD : (h + 1) * HD] = moved(num).astype(bf16)
        extra = pieces(jnp.sum(den_ref[...], axis=1, keepdims=True), slots)
        out_ref[:, width:] = moved(extra.astype(f32)).astype(bf16)


def combine_kernel(
    returned_ref, back_ref, num_a, den_a, num_b, den_b, weight_ref, att_ref, give_ref
):
    width = num_a.shape[1]
    heads = width // HD
    mine = jnp.dot(back_ref[...], returned_ref[...], preferred_element_type=f32)
    for h in range(heads):
        cols = slice(h * HD, (h + 1) * HD)
        numerator = mine[:, cols] + jnp.concatenate([num_a[:, cols], num_b[:, cols]], axis=0)
        at = width + 3 * h
        lane = slice(h * 128, h * 128 + 1)
        denominator = jnp.concatenate([den_a[:, lane], den_b[:, lane]], axis=0) + (
            mine[:, at : at + 1] + mine[:, at + 1 : at + 2] + mine[:, at + 2 : at + 3]
        )
        att_ref[:, cols] = (numerator / denominator).astype(bf16)
    give_ref[...] = jnp.dot(att_ref[...], weight_ref[0], preferred_element_type=f32).astype(bf16)


def give_kernel(att_ref, weight_ref, give_ref):
    give_ref[...] = jnp.dot(att_ref[...], weight_ref[1], preferred_element_type=f32).astype(bf16)


def own_kernel(att_ref, weight_ref, own_ref):
    own_ref[...] = jnp.dot(att_ref[...], weight_ref[2], preferred_element_type=f32)


def chip_kernel(own_ref, got_ref, sum_ref, send_ref):
    total = own_ref[...] + got_ref[...].astype(f32)
    sum_ref[...] = total
    send_ref[...] = total.astype(bf16)


def last_kernel(att_ref, weight_ref, got_ref, after_ref, sum_ref, send_ref):
    total = jnp.dot(att_ref[...], weight_ref[...], preferred_element_type=f32)
    total = total + got_ref[...].astype(f32)
    sum_ref[...] = total
    send_ref[...] = total.astype(bf16)


def square_kernel(row_ref, sum_a, got_a, sum_b, got_b, mine_ref, square_ref):
    part = jnp.zeros(square_ref.shape, f32)
    totals = []
    for sum_ref, got_ref in ((sum_a, got_a), (sum_b, got_b)):
        total = sum_ref[...] + got_ref[...].astype(f32)
        for k in range(total.shape[1] // 128):
            piece = total[:, k * 128 : (k + 1) * 128]
            part = part + piece * piece
        totals.append(total)
    square_ref[...] = part
    mine_ref[...] = jnp.where(row_ref[0] == 0, totals[0], totals[1])


def final_kernel(features, mine_ref, square_ref, got_ref, gain_ref, hidden_ref, out_ref):
    square = jnp.sum(square_ref[...] + got_ref[...], axis=1, keepdims=True)
    scale = lax.rsqrt(square * (1.0 / features) + epsilon)
    normed = mine_ref[...] * scale * gain_ref[...]
    out_ref[...] = (hidden_ref[...].astype(f32) + normed).astype(bf16)


def call(kernel, outs, ins, **kw):
    specs = [
        pl.BlockSpec(memory_space=SMEM if a.ndim == 1 else VMEM) for a in ins
    ]
    return pl.pallas_call(
        kernel,
        out_shape=outs,
        in_specs=specs,
        out_specs=jax.tree.map(lambda _: pl.BlockSpec(memory_space=VMEM), outs),
        compiler_params=PARAMS,
        **kw,
    )(*ins)


def in_hbm(*arrays):
    return [pltpu.with_memory_space_constraint(a, pltpu.MemorySpace.HBM) for a in arrays]


def shape(dims, dtype):
    return jax.ShapeDtypeStruct(dims, dtype)


def shards(
    hidden_input,
    queries,
    prompt_cache,
    suffix_cache,
    owner_replica,
    group_slot,
    prompt_length,
    suffix_length,
    output_weight,
    post_gain,
):
    replicas = lax.axis_size("replica")
    ranks = lax.axis_size("tensor")
    requests, width = queries.shape
    capacity = max(2, (2 * requests + replicas - 1) // replicas)
    slots = replicas * capacity
    groups, _, size, _ = prompt_cache.shape
    window = suffix_cache.shape[2]
    features = output_weight.shape[1]
    quarter = features // ranks
    heads = width // HD
    there, back_again = orders_of(replicas)
    index = lax.axis_index("tensor")
    core = (index % 2).reshape(1)
    far_row = (index // 2).reshape(1)

    def exchange(x, order):
        blocks = x.reshape(replicas, capacity, width + EXTRA)
        blocks = lax.all_to_all(
            blocks, "replica", split_axis=0, concat_axis=0, axis_index_groups=[order], tiled=True
        )
        return blocks.reshape(slots, width + EXTRA)

    def permute(x, bit):
        return lax.ppermute(x, "tensor", [(i, i ^ bit) for i in range(ranks)])

    owner_row = owner_replica.reshape(1, requests)
    sent = pl.pallas_call(
        functools.partial(route_kernel, capacity, there),
        out_shape=pltpu.VMEM((slots, width + EXTRA), bf16),
        in_specs=[HBM_SPEC] * 3,
        out_specs=VMEM_SPEC,
        scratch_shapes=[
            pltpu.VMEM((1, requests), jnp.int32),
            pltpu.VMEM((1, requests), jnp.int32),
            pltpu.VMEM((requests, width), bf16),
            pltpu.SemaphoreType.DMA((3,)),
        ],
        compiler_params=PARAMS,
    )(*in_hbm(owner_row, group_slot.reshape(1, requests), queries))
    got = exchange(sent, there)

    early = 3
    half = requests // 2
    block = math.gcd(16, half)
    length_row = suffix_length.reshape(1, requests)
    halves = [shape((half, width), f32), shape((half, heads * 128), f32)]
    row = pltpu.VMEM((1, requests), jnp.int32)
    own_scratch = [
        row,
        pltpu.VMEM((requests, width), bf16),
        pltpu.VMEM((half,) + suffix_cache.shape[1:], bf16),
    ]
    back, num_a, den_a, prefetched, last = pl.pallas_call(
        functools.partial(early_kernel, capacity, back_again, block),
        out_shape=[shape((requests, slots), bf16)]
        + halves
        + [pltpu.VMEM((early, size, HD), bf16), pltpu.HBM((width, quarter), bf16)],
        in_specs=[SMEM_SPEC] + [HBM_SPEC] * 6,
        out_specs=[VMEM_SPEC] * 4 + [HBM_SPEC],
        scratch_shapes=[row]
        + own_scratch
        + [
            pltpu.VMEM((width, quarter), bf16),
            pltpu.SemaphoreType.DMA((4,)),
            pltpu.SemaphoreType.DMA((early,)),
            pltpu.SemaphoreType.DMA,
        ],
        compiler_params=PARAMS,
        cost_estimate=pl.CostEstimate(
            flops=4 * requests * window * HD * block,
            bytes_accessed=2 * early * size * HD * 2 + suffix_cache.size,
            transcendentals=0,
        ),
    )(
        core,
        *in_hbm(owner_row, length_row, queries, suffix_cache, prompt_cache, output_weight),
    )

    chunk = math.gcd(512, size)
    moves = [there.index(replica) for replica in back_again]
    fit = min(48, slots)
    answered = pl.pallas_call(
        functools.partial(prompt_kernel, chunk, fit, moves),
        out_shape=pltpu.VMEM((slots, width + EXTRA), bf16),
        in_specs=[HBM_SPEC, VMEM_SPEC, VMEM_SPEC, HBM_SPEC],
        out_specs=VMEM_SPEC,
        scratch_shapes=[
            pltpu.SMEM((groups,), jnp.int32),
            pltpu.VMEM((2 * groups - early, size, HD), bf16),
            pltpu.VMEM((groups * heads * fit, HD), bf16),
            pltpu.VMEM((groups * fit, width + EXTRA), bf16),
            pltpu.VMEM((heads * slots, HD), f32),
            pltpu.VMEM((heads * slots, 128), f32),
            pltpu.SemaphoreType.DMA((2 * groups - early,)),
            pltpu.SemaphoreType.DMA,
        ],
        compiler_params=PARAMS,
    )(
        *in_hbm(prompt_length),
        got,
        pltpu.with_memory_space_constraint(prefetched, VMEM),
        *in_hbm(prompt_cache),
    )
    returned = exchange(answered, back_again)

    num_b, den_b, weight = pl.pallas_call(
        functools.partial(late_kernel, block),
        out_shape=halves + [pltpu.VMEM((3, width, quarter), bf16)],
        in_specs=[SMEM_SPEC] + [HBM_SPEC] * 5,
        out_specs=[VMEM_SPEC] * 3,
        scratch_shapes=own_scratch
        + [pltpu.SemaphoreType.DMA((3,)), pltpu.SemaphoreType.DMA((3,))],
        compiler_params=PARAMS,
        cost_estimate=pl.CostEstimate(
            flops=4 * requests * window * HD * block,
            bytes_accessed=suffix_cache.size + output_weight.size * 2,
            transcendentals=0,
        ),
    )(core, *in_hbm(length_row, queries, suffix_cache, output_weight, answered))
    weight = pltpu.with_memory_space_constraint(weight, VMEM)

    block_f32 = shape((requests, quarter), f32)
    block_bf16 = shape((requests, quarter), bf16)
    attention, give_a = call(
        combine_kernel,
        [shape((requests, width), bf16), block_bf16],
        [returned, back, num_a, den_a, num_b, den_b, weight],
    )
    got_a = permute(give_a, 1)
    got_b = permute(call(give_kernel, block_bf16, [attention, weight]), 1)
    own_a = call(own_kernel, block_f32, [attention, weight])
    sum_a, send_a = call(chip_kernel, [block_f32, block_bf16], [own_a, got_a])
    far_a = permute(send_a, 2)
    sum_b, send_b = call(last_kernel, [block_f32, block_bf16], [attention, last, got_b, send_a])
    far_b = permute(send_b, 2)
    mine, square = call(
        square_kernel,
        [block_f32, shape((requests, 128), f32)],
        [far_row, sum_a, far_a, sum_b, far_b],
    )
    beside = permute(square, 1)
    return call(
        functools.partial(final_kernel, features),
        shape((requests, quarter), bf16),
        [mine, square, beside, post_gain.reshape(1, quarter), hidden_input],
    )


def solution(mesh):
    in_specs = (
        P("replica", "tensor"),
        P("replica", "tensor"),
        P("replica", None, None, "tensor"),
        P("replica", None, None, "tensor"),
        P("replica", None),
        P("replica"),
        P("replica"),
        P("replica"),
        P("tensor", None),
        P("tensor"),
    )
    out_specs = P("replica", "tensor")
    return jax.shard_map(shards, mesh=mesh, in_specs=in_specs, out_specs=out_specs, check_vma=False)
```

```python
import functools
import math

import jax
import jax.numpy as jnp
from jax import lax
from jax.experimental import pallas as pl
from jax.experimental.pallas import tpu as pltpu
from jax.sharding import PartitionSpec as P

HD = 256
softcap = 50.0
epsilon = 1e-06
score_scale = 1.0 / (softcap * math.sqrt(HD))
weight_scale = softcap * math.log2(math.e)
EXTRA = 128
f32 = jnp.float32
bf16 = jnp.bfloat16
VMEM = pltpu.MemorySpace.VMEM
SMEM = pltpu.MemorySpace.SMEM
VMEM_SPEC = pl.BlockSpec(memory_space=VMEM)
SMEM_SPEC = pl.BlockSpec(memory_space=SMEM)
HBM_SPEC = pl.BlockSpec(memory_space=pltpu.MemorySpace.HBM)
PARAMS = pltpu.CompilerParams(vmem_limit_bytes=40 * 2**20)


def iota(shape, axis):
    return lax.broadcasted_iota(jnp.int32, shape, axis)


def heads_below(block, heads):
    return jnp.concatenate([block[:, h * HD : (h + 1) * HD] for h in range(heads)], axis=0)


def weights_of(scores, alive):
    return jnp.where(alive, jnp.exp2(weight_scale * jnp.tanh(scores * score_scale)), 0.0)


def orders_of(replicas):
    tuned = {8: ((4, 3, 5, 1, 0, 7, 6, 2), (5, 7, 2, 4, 6, 1, 3, 0))}
    return tuned.get(replicas, (tuple(range(replicas)),) * 2)


def owners(owner_ref, order):
    requests = owner_ref.shape[1]
    rows, cols = iota((requests, requests), 0), iota((requests, requests), 1)
    owner = owner_ref[...]
    place = owner
    for i, replica in enumerate(order):
        if i != replica:
            place = jnp.where(owner == replica, i, place)
    by_col = jnp.broadcast_to(place, (requests, requests)).astype(f32)
    by_row = jnp.sum(jnp.where(rows == cols, by_col, 0.0), axis=1, keepdims=True)
    return by_row, by_col, rows, cols


def route_kernel(
    capacity, order, owner_hbm, group_hbm, queries_hbm, out_ref, owner_ref, group_ref, queries_ref, sems
):
    pairs = ((owner_hbm, owner_ref), (group_hbm, group_ref), (queries_hbm, queries_ref))
    copies = [pltpu.make_async_copy(a, b, sems.at[i]) for i, (a, b) in enumerate(pairs)]
    for copy in copies:
        copy.start()
    for copy in copies:
        copy.wait()
    requests, width = queries_ref.shape
    slots = out_ref.shape[0]
    by_row, by_col, rows, cols = owners(owner_ref, order)
    earlier = jnp.where((by_row == by_col) & (rows < cols), 1.0, 0.0)
    position = (by_col[:1] * capacity + jnp.sum(earlier, axis=0, keepdims=True)).astype(jnp.int32)
    matches = iota((slots, requests), 0) == position
    out_ref[:, :width] = jnp.dot(
        jnp.where(matches, 1.0, 0.0).astype(bf16), queries_ref[...], preferred_element_type=f32
    ).astype(bf16)
    numbered = (group_ref[...] + 1).astype(f32)
    mark = jnp.sum(jnp.where(matches, numbered, 0.0), axis=1, keepdims=True)
    out_ref[:, width:] = jnp.broadcast_to(mark, (slots, EXTRA)).astype(bf16)


def attend_own(block, first, live, queries_ref, cache_ref, num_ref, den_ref):
    requests, _, window, _ = cache_ref.shape
    heads = queries_ref.shape[1] // HD
    at = iota((block, block * window), 1)
    start = iota((block, block * window), 0) * window
    for i in range(requests // block):
        mine = slice(i * block, (i + 1) * block)
        there = slice(first + i * block, first + (i + 1) * block)
        stacked = heads_below(queries_ref[there, :], heads)
        keys = cache_ref[mine, 0].reshape(block * window, HD)
        values = cache_ref[mine, 1].reshape(block * window, HD)
        scores = lax.dot_general(
            stacked, keys, (((1,), (1,)), ((), ())), preferred_element_type=f32
        )
        alive = (at >= start) & (at < start + live[there])
        weights = weights_of(scores, jnp.concatenate([alive] * heads, axis=0))
        numerator = jnp.dot(weights.astype(bf16), values, preferred_element_type=f32)
        denominator = jnp.sum(weights, axis=1, keepdims=True)
        for h in range(heads):
            own = slice(h * block, (h + 1) * block)
            num_ref[mine, h * HD : (h + 1) * HD] = numerator[own]
            den_ref[mine, h * 128 : (h + 1) * 128] = jnp.broadcast_to(
                denominator[own], (block, 128)
            )


def down(row, rows, cols):
    return jnp.sum(jnp.where(rows == cols, row.astype(f32), 0.0), axis=1, keepdims=True)


def early_kernel(
    capacity,
    order,
    block,
    core_ref,
    owner_hbm,
    length_hbm,
    queries_hbm,
    cache_hbm,
    prompt_hbm,
    weight_hbm,
    back_ref,
    num_ref,
    den_ref,
    early_ref,
    last_hbm,
    owner_ref,
    length_ref,
    queries_ref,
    cache_ref,
    staged,
    sems,
    early_sems,
    last_sem,
):
    requests, slots = back_ref.shape
    parts = parts_of(prompt_hbm.shape[0])
    pairs = (
        (owner_hbm, owner_ref),
        (length_hbm, length_ref),
        (queries_hbm, queries_ref),
        (cache_hbm.at[pl.ds(0, cache_ref.shape[0])], cache_ref),
    )
    copies = [pltpu.make_async_copy(a, b, sems.at[i]) for i, (a, b) in enumerate(pairs)]
    quarter = last_hbm.shape[1]
    cols = pl.ds(pl.multiple_of((core_ref[0] + 2) * quarter, 128), quarter)
    stage = pltpu.make_async_copy(weight_hbm.at[:, cols], staged, last_sem)
    unstage = pltpu.make_async_copy(staged, last_hbm, last_sem)
    prompts = [
        pltpu.make_async_copy(prompt_hbm.at[parts[i]], early_ref.at[i], early_sems.at[i])
        for i in range(early_ref.shape[0])
    ]
    for copy in copies + [stage] + prompts:
        copy.start()
    for copy in copies:
        copy.wait()
    stage.wait()
    unstage.start()
    by_row, by_col, rows, cols = owners(owner_ref, order)
    earlier = jnp.where((by_row == by_col) & (cols < rows), 1.0, 0.0)
    rank = jnp.sum(earlier, axis=1, keepdims=True)
    position = (by_row * capacity + rank).astype(jnp.int32)
    back_ref[...] = jnp.where(iota((requests, slots), 1) == position, 1.0, 0.0).astype(bf16)
    live = down(length_ref[...], rows, cols).astype(jnp.int32)
    attend_own(block, 0, live, queries_ref, cache_ref, num_ref, den_ref)
    for copy in prompts + [unstage]:
        copy.wait()


def late_kernel(
    block,
    core_ref,
    length_hbm,
    queries_hbm,
    cache_hbm,
    weight_hbm,
    after_hbm,
    num_ref,
    den_ref,
    weight_ref,
    length_ref,
    queries_ref,
    cache_ref,
    sems,
    weight_sems,
):
    requests = queries_ref.shape[0]
    half = cache_ref.shape[0]
    first = requests - half
    pairs = (
        (length_hbm, length_ref),
        (queries_hbm, queries_ref),
        (cache_hbm.at[pl.ds(first, half)], cache_ref),
    )
    copies = [pltpu.make_async_copy(a, b, sems.at[i]) for i, (a, b) in enumerate(pairs)]
    quarter = weight_ref.shape[2]
    weight_copies = []
    for i, q in enumerate((1 - core_ref[0], 3 - core_ref[0], core_ref[0])):
        cols = pl.ds(pl.multiple_of(q * quarter, 128), quarter)
        weight_copies.append(
            pltpu.make_async_copy(weight_hbm.at[:, cols], weight_ref.at[i], weight_sems.at[i])
        )
    for copy in copies + weight_copies:
        copy.start()
    for copy in copies:
        copy.wait()
    rows, cols = iota((requests, requests), 0), iota((requests, requests), 1)
    live = down(length_ref[...], rows, cols).astype(jnp.int32)
    attend_own(block, first, live, queries_ref, cache_ref, num_ref, den_ref)
    for copy in weight_copies:
        copy.wait()


def parts_of(groups):
    return [(g, part) for g in range(groups) for part in range(2)]


def prompt_kernel(
    chunk,
    window,
    moves,
    length_hbm,
    slots_ref,
    early_ref,
    cache_hbm,
    out_ref,
    length_ref,
    held,
    sorted_ref,
    done_ref,
    num_ref,
    den_ref,
    sems,
    length_sem,
):
    groups, _, size, _ = cache_hbm.shape
    slots = slots_ref.shape[0]
    width = slots_ref.shape[1] - EXTRA
    heads = width // HD
    parts = parts_of(groups)
    early = early_ref.shape[0]
    length_copy = pltpu.make_async_copy(length_hbm, length_ref, length_sem)
    length_copy.start()
    copies = {
        parts[i]: pltpu.make_async_copy(
            cache_hbm.at[parts[i]], held.at[i - early], sems.at[i - early]
        )
        for i in range(early, len(parts))
    }
    for part in parts[early:]:
        copies[part].start()

    def read(g, part, span):
        i = parts.index((g, part))
        return early_ref[i, span, :] if i < early else held[i - early, span, :]

    def moved(block):
        if moves == sorted(moves):
            return block
        step = slots // len(moves)
        return jnp.concatenate([block[m * step : (m + 1) * step] for m in moves], axis=0)

    def pieces(total, rows):
        lanes = iota((1, EXTRA), 1)
        extra = jnp.zeros((rows, EXTRA), f32)
        for h in range(heads):
            rest = total[h * rows : (h + 1) * rows]
            for k in range(3):
                piece = rest.astype(bf16).astype(f32)
                rest = rest - piece
                extra = jnp.where(lanes == 3 * h + k, piece, extra)
        return extra.astype(bf16)

    def fold(weights):
        part = weights[:, :128]
        for k in range(1, weights.shape[1] // 128):
            part = part + weights[:, k * 128 : (k + 1) * 128]
        return part

    rows, cols = iota((slots, slots), 0), iota((slots, slots), 1)
    by_row = jnp.broadcast_to(slots_ref[:, width : width + 1].astype(f32), (slots, slots))
    by_col = jnp.sum(jnp.where(rows == cols, by_row, 0.0), axis=0, keepdims=True)
    same = by_row == by_col
    rank_row = jnp.sum(jnp.where(same & (cols < rows), 1.0, 0.0), axis=1, keepdims=True)
    rank_col = jnp.sum(jnp.where(same & (rows < cols), 1.0, 0.0), axis=0, keepdims=True)
    length_copy.wait()
    crowded = jnp.max(jnp.where(by_col > 0.0, rank_col, 0.0)) >= window

    at_row = (by_row[:, :1] - 1.0) * window + rank_row
    at_row = jnp.where(by_row[:, :1] > 0.0, at_row, -1.0).astype(jnp.int32)
    at_col = jnp.where(by_col > 0.0, (by_col - 1.0) * window + rank_col, -1.0).astype(jnp.int32)
    room = groups * window
    there = jnp.where(iota((room, slots), 0) == at_col, 1.0, 0.0).astype(bf16)
    back = jnp.where(iota((slots, room), 1) == moved(at_row), 1.0, 0.0).astype(bf16)
    for h in range(heads):
        part = jnp.dot(there, slots_ref[:, h * HD : (h + 1) * HD], preferred_element_type=f32)
        for g in range(groups):
            at = (g * heads + h) * window
            sorted_ref[at : at + window, :] = part[g * window : (g + 1) * window].astype(bf16)
    scores = [None] * groups
    waited = early
    everything = slice(0, size)
    for u in range(groups + 1):
        needed = min(2 * u + 1, len(parts))
        if needed > waited:
            needed = min(needed + 1, len(parts))
            for part in parts[waited:needed]:
                copies[part].wait()
            waited = needed
        if u < groups:
            scores[u] = lax.dot_general(
                sorted_ref[u * heads * window : (u + 1) * heads * window, :],
                read(u, 0, everything),
                (((1,), (1,)), ((), ())),
                preferred_element_type=f32,
            )
        if u > 0:
            g = u - 1
            weights = weights_of(scores[g], iota((1, size), 1) < length_ref[g])
            num = jnp.dot(
                weights.astype(bf16), read(g, 1, everything), preferred_element_type=f32
            )
            mine = slice(g * window, (g + 1) * window)
            for h in range(heads):
                done_ref[mine, h * HD : (h + 1) * HD] = num[
                    h * window : (h + 1) * window
                ].astype(bf16)
            den = jnp.sum(fold(weights), axis=1, keepdims=True)
            done_ref[mine, width:] = pieces(den, window)
    out_ref[...] = jnp.dot(back, done_ref[...], preferred_element_type=f32).astype(bf16)

    @pl.when(crowded)
    def _():
        stacked = heads_below(slots_ref[:, :width], heads)
        mark = jnp.concatenate([by_row[:, :1]] * heads, axis=0)
        num_ref[...] = jnp.zeros_like(num_ref)
        den_ref[...] = jnp.zeros_like(den_ref)
        for g in range(groups):
            limit = jnp.where(mark == g + 1.0, length_ref[g], 0)

            @pl.loop(0, (length_ref[g] + chunk - 1) // chunk)
            def _(c):
                span = pl.ds(pl.multiple_of(c * chunk, chunk), chunk)
                scores = lax.dot_general(
                    stacked,
                    read(g, 0, span),
                    (((1,), (1,)), ((), ())),
                    preferred_element_type=f32,
                )
                alive = iota((heads * slots, chunk), 1) < limit - c * chunk
                weights = weights_of(scores, alive)
                num_ref[...] += jnp.dot(
                    weights.astype(bf16), read(g, 1, span), preferred_element_type=f32
                )
                den_ref[...] += fold(weights)

        for h in range(heads):
            num = num_ref[h * slots : (h + 1) * slots]
            out_ref[:, h * HD : (h + 1) * HD] = moved(num).astype(bf16)
        extra = pieces(jnp.sum(den_ref[...], axis=1, keepdims=True), slots)
        out_ref[:, width:] = moved(extra.astype(f32)).astype(bf16)


def combine_kernel(
    returned_ref, back_ref, num_a, den_a, num_b, den_b, weight_ref, att_ref, give_ref
):
    width = num_a.shape[1]
    heads = width // HD
    mine = jnp.dot(back_ref[...], returned_ref[...], preferred_element_type=f32)
    for h in range(heads):
        cols = slice(h * HD, (h + 1) * HD)
        numerator = mine[:, cols] + jnp.concatenate([num_a[:, cols], num_b[:, cols]], axis=0)
        at = width + 3 * h
        lane = slice(h * 128, h * 128 + 1)
        denominator = jnp.concatenate([den_a[:, lane], den_b[:, lane]], axis=0) + (
            mine[:, at : at + 1] + mine[:, at + 1 : at + 2] + mine[:, at + 2 : at + 3]
        )
        att_ref[:, cols] = (numerator / denominator).astype(bf16)
    give_ref[...] = jnp.dot(att_ref[...], weight_ref[0], preferred_element_type=f32).astype(bf16)


def give_kernel(att_ref, weight_ref, give_ref):
    give_ref[...] = jnp.dot(att_ref[...], weight_ref[1], preferred_element_type=f32).astype(bf16)


def own_kernel(att_ref, weight_ref, own_ref):
    own_ref[...] = jnp.dot(att_ref[...], weight_ref[2], preferred_element_type=f32)


def chip_kernel(own_ref, got_ref, sum_ref, send_ref):
    total = own_ref[...] + got_ref[...].astype(f32)
    sum_ref[...] = total
    send_ref[...] = total.astype(bf16)


def last_kernel(att_ref, weight_ref, got_ref, after_ref, sum_ref, send_ref):
    total = jnp.dot(att_ref[...], weight_ref[...], preferred_element_type=f32)
    total = total + got_ref[...].astype(f32)
    sum_ref[...] = total
    send_ref[...] = total.astype(bf16)


def squares(total):
    part = jnp.zeros((total.shape[0], 128), f32)
    for k in range(total.shape[1] // 128):
        piece = total[:, k * 128 : (k + 1) * 128]
        part = part + piece * piece
    return part


def first_square_kernel(sum_ref, got_ref, total_ref, square_ref):
    total = sum_ref[...] + got_ref[...].astype(f32)
    total_ref[...] = total
    square_ref[...] = squares(total)


def square_kernel(row_ref, total_ref, first_ref, sum_ref, got_ref, mine_ref, square_ref):
    total = sum_ref[...] + got_ref[...].astype(f32)
    square_ref[...] = first_ref[...] + squares(total)
    mine_ref[...] = jnp.where(row_ref[0] == 0, total_ref[...], total)


def final_kernel(features, mine_ref, square_ref, got_ref, gain_ref, hidden_ref, out_ref):
    square = jnp.sum(square_ref[...] + got_ref[...], axis=1, keepdims=True)
    scale = lax.rsqrt(square * (1.0 / features) + epsilon)
    normed = mine_ref[...] * scale * gain_ref[...]
    out_ref[...] = (hidden_ref[...].astype(f32) + normed).astype(bf16)


def call(kernel, outs, ins, **kw):
    specs = [
        pl.BlockSpec(memory_space=SMEM if a.ndim == 1 else VMEM) for a in ins
    ]
    return pl.pallas_call(
        kernel,
        out_shape=outs,
        in_specs=specs,
        out_specs=jax.tree.map(lambda _: pl.BlockSpec(memory_space=VMEM), outs),
        compiler_params=PARAMS,
        **kw,
    )(*ins)


def in_hbm(*arrays):
    return [pltpu.with_memory_space_constraint(a, pltpu.MemorySpace.HBM) for a in arrays]


def shape(dims, dtype):
    return jax.ShapeDtypeStruct(dims, dtype)


def shards(
    hidden_input,
    queries,
    prompt_cache,
    suffix_cache,
    owner_replica,
    group_slot,
    prompt_length,
    suffix_length,
    output_weight,
    post_gain,
):
    replicas = lax.axis_size("replica")
    ranks = lax.axis_size("tensor")
    requests, width = queries.shape
    capacity = max(2, (2 * requests + replicas - 1) // replicas)
    slots = replicas * capacity
    groups, _, size, _ = prompt_cache.shape
    window = suffix_cache.shape[2]
    features = output_weight.shape[1]
    quarter = features // ranks
    heads = width // HD
    there, back_again = orders_of(replicas)
    index = lax.axis_index("tensor")
    core = (index % 2).reshape(1)
    far_row = (index // 2).reshape(1)

    def exchange(x, order):
        blocks = x.reshape(replicas, capacity, width + EXTRA)
        blocks = lax.all_to_all(
            blocks, "replica", split_axis=0, concat_axis=0, axis_index_groups=[order], tiled=True
        )
        return blocks.reshape(slots, width + EXTRA)

    def permute(x, bit):
        return lax.ppermute(x, "tensor", [(i, i ^ bit) for i in range(ranks)])

    owner_row = owner_replica.reshape(1, requests)
    sent = pl.pallas_call(
        functools.partial(route_kernel, capacity, there),
        out_shape=pltpu.VMEM((slots, width + EXTRA), bf16),
        in_specs=[HBM_SPEC] * 3,
        out_specs=VMEM_SPEC,
        scratch_shapes=[
            pltpu.VMEM((1, requests), jnp.int32),
            pltpu.VMEM((1, requests), jnp.int32),
            pltpu.VMEM((requests, width), bf16),
            pltpu.SemaphoreType.DMA((3,)),
        ],
        compiler_params=PARAMS,
    )(*in_hbm(owner_row, group_slot.reshape(1, requests), queries))
    got = exchange(sent, there)

    early = 3
    half = requests // 2
    block = math.gcd(16, half)
    length_row = suffix_length.reshape(1, requests)
    halves = [shape((half, width), f32), shape((half, heads * 128), f32)]
    row = pltpu.VMEM((1, requests), jnp.int32)
    own_scratch = [
        row,
        pltpu.VMEM((requests, width), bf16),
        pltpu.VMEM((half,) + suffix_cache.shape[1:], bf16),
    ]
    back, num_a, den_a, prefetched, last = pl.pallas_call(
        functools.partial(early_kernel, capacity, back_again, block),
        out_shape=[shape((requests, slots), bf16)]
        + halves
        + [pltpu.VMEM((early, size, HD), bf16), pltpu.HBM((width, quarter), bf16)],
        in_specs=[SMEM_SPEC] + [HBM_SPEC] * 6,
        out_specs=[VMEM_SPEC] * 4 + [HBM_SPEC],
        scratch_shapes=[row]
        + own_scratch
        + [
            pltpu.VMEM((width, quarter), bf16),
            pltpu.SemaphoreType.DMA((4,)),
            pltpu.SemaphoreType.DMA((early,)),
            pltpu.SemaphoreType.DMA,
        ],
        compiler_params=PARAMS,
        cost_estimate=pl.CostEstimate(
            flops=4 * requests * window * HD * block,
            bytes_accessed=2 * early * size * HD * 2 + suffix_cache.size,
            transcendentals=0,
        ),
    )(
        core,
        *in_hbm(owner_row, length_row, queries, suffix_cache, prompt_cache, output_weight),
    )

    chunk = math.gcd(512, size)
    moves = [there.index(replica) for replica in back_again]
    fit = min(48, slots)
    answered = pl.pallas_call(
        functools.partial(prompt_kernel, chunk, fit, moves),
        out_shape=pltpu.VMEM((slots, width + EXTRA), bf16),
        in_specs=[HBM_SPEC, VMEM_SPEC, VMEM_SPEC, HBM_SPEC],
        out_specs=VMEM_SPEC,
        scratch_shapes=[
            pltpu.SMEM((groups,), jnp.int32),
            pltpu.VMEM((2 * groups - early, size, HD), bf16),
            pltpu.VMEM((groups * heads * fit, HD), bf16),
            pltpu.VMEM((groups * fit, width + EXTRA), bf16),
            pltpu.VMEM((heads * slots, HD), f32),
            pltpu.VMEM((heads * slots, 128), f32),
            pltpu.SemaphoreType.DMA((2 * groups - early,)),
            pltpu.SemaphoreType.DMA,
        ],
        compiler_params=PARAMS,
    )(
        *in_hbm(prompt_length),
        got,
        pltpu.with_memory_space_constraint(prefetched, VMEM),
        *in_hbm(prompt_cache),
    )
    returned = exchange(answered, back_again)

    num_b, den_b, weight = pl.pallas_call(
        functools.partial(late_kernel, block),
        out_shape=halves + [pltpu.VMEM((3, width, quarter), bf16)],
        in_specs=[SMEM_SPEC] + [HBM_SPEC] * 5,
        out_specs=[VMEM_SPEC] * 3,
        scratch_shapes=own_scratch
        + [pltpu.SemaphoreType.DMA((3,)), pltpu.SemaphoreType.DMA((3,))],
        compiler_params=PARAMS,
        cost_estimate=pl.CostEstimate(
            flops=4 * requests * window * HD * block,
            bytes_accessed=suffix_cache.size + output_weight.size * 2,
            transcendentals=0,
        ),
    )(core, *in_hbm(length_row, queries, suffix_cache, output_weight, answered))
    weight = pltpu.with_memory_space_constraint(weight, VMEM)

    block_f32 = shape((requests, quarter), f32)
    block_bf16 = shape((requests, quarter), bf16)
    attention, give_a = call(
        combine_kernel,
        [shape((requests, width), bf16), block_bf16],
        [returned, back, num_a, den_a, num_b, den_b, weight],
    )
    got_a = permute(give_a, 1)
    got_b = permute(call(give_kernel, block_bf16, [attention, weight]), 1)
    own_a = call(own_kernel, block_f32, [attention, weight])
    sum_a, send_a = call(chip_kernel, [block_f32, block_bf16], [own_a, got_a])
    far_a = permute(send_a, 2)
    sum_b, send_b = call(last_kernel, [block_f32, block_bf16], [attention, last, got_b, send_a])
    far_b = permute(send_b, 2)
    outs = [block_f32, shape((requests, 128), f32)]
    total_a, square_a = call(first_square_kernel, outs, [sum_a, far_a])
    mine, square = call(square_kernel, outs, [far_row, total_a, square_a, sum_b, far_b])
    beside = permute(square, 1)
    return call(
        functools.partial(final_kernel, features),
        shape((requests, quarter), bf16),
        [mine, square, beside, post_gain.reshape(1, quarter), hidden_input],
    )


def solution(mesh):
    in_specs = (
        P("replica", "tensor"),
        P("replica", "tensor"),
        P("replica", None, None, "tensor"),
        P("replica", None, None, "tensor"),
        P("replica", None),
        P("replica"),
        P("replica"),
        P("replica"),
        P("tensor", None),
        P("tensor"),
    )
    out_specs = P("replica", "tensor")
    return jax.shard_map(shards, mesh=mesh, in_specs=in_specs, out_specs=out_specs, check_vma=False)
```

```python
import functools
import math

import jax
import jax.numpy as jnp
from jax import lax
from jax.experimental import pallas as pl
from jax.experimental.pallas import tpu as pltpu
from jax.sharding import PartitionSpec as P

HD = 256
softcap = 50.0
epsilon = 1e-06
score_scale = 1.0 / (softcap * math.sqrt(HD))
weight_scale = softcap * math.log2(math.e)
EXTRA = 128
f32 = jnp.float32
bf16 = jnp.bfloat16
VMEM = pltpu.MemorySpace.VMEM
SMEM = pltpu.MemorySpace.SMEM
VMEM_SPEC = pl.BlockSpec(memory_space=VMEM)
SMEM_SPEC = pl.BlockSpec(memory_space=SMEM)
HBM_SPEC = pl.BlockSpec(memory_space=pltpu.MemorySpace.HBM)
PARAMS = pltpu.CompilerParams(vmem_limit_bytes=40 * 2**20)


def iota(shape, axis):
    return lax.broadcasted_iota(jnp.int32, shape, axis)


def heads_below(block, heads):
    return jnp.concatenate([block[:, h * HD : (h + 1) * HD] for h in range(heads)], axis=0)


def weights_of(scores, alive):
    return jnp.where(alive, jnp.exp2(weight_scale * jnp.tanh(scores * score_scale)), 0.0)


def orders_of(replicas):
    tuned = {8: ((4, 3, 5, 1, 0, 7, 6, 2), (5, 7, 2, 4, 6, 1, 3, 0))}
    return tuned.get(replicas, (tuple(range(replicas)),) * 2)


def owners(owner_ref, order):
    requests = owner_ref.shape[1]
    rows, cols = iota((requests, requests), 0), iota((requests, requests), 1)
    owner = owner_ref[...]
    place = owner
    for i, replica in enumerate(order):
        if i != replica:
            place = jnp.where(owner == replica, i, place)
    by_col = jnp.broadcast_to(place, (requests, requests)).astype(f32)
    by_row = jnp.sum(jnp.where(rows == cols, by_col, 0.0), axis=1, keepdims=True)
    return by_row, by_col, rows, cols


def route_kernel(
    capacity, order, owner_hbm, group_hbm, queries_hbm, out_ref, owner_ref, group_ref, queries_ref, sems
):
    pairs = ((owner_hbm, owner_ref), (group_hbm, group_ref), (queries_hbm, queries_ref))
    copies = [pltpu.make_async_copy(a, b, sems.at[i]) for i, (a, b) in enumerate(pairs)]
    for copy in copies:
        copy.start()
    for copy in copies[:2]:
        copy.wait()
    requests, width = queries_ref.shape
    slots = out_ref.shape[0]
    by_row, by_col, rows, cols = owners(owner_ref, order)
    earlier = jnp.where((by_row == by_col) & (rows < cols), 1.0, 0.0)
    position = (by_col[:1] * capacity + jnp.sum(earlier, axis=0, keepdims=True)).astype(jnp.int32)
    matches = iota((slots, requests), 0) == position
    copies[2].wait()
    out_ref[:, :width] = jnp.dot(
        jnp.where(matches, 1.0, 0.0).astype(bf16), queries_ref[...], preferred_element_type=f32
    ).astype(bf16)
    numbered = (group_ref[...] + 1).astype(f32)
    mark = jnp.sum(jnp.where(matches, numbered, 0.0), axis=1, keepdims=True)
    out_ref[:, width:] = jnp.broadcast_to(mark, (slots, EXTRA)).astype(bf16)


def attend_own(block, first, live, queries_ref, cache_ref, num_ref, den_ref):
    requests, _, window, _ = cache_ref.shape
    heads = queries_ref.shape[1] // HD
    at = iota((block, block * window), 1)
    start = iota((block, block * window), 0) * window
    for i in range(requests // block):
        mine = slice(i * block, (i + 1) * block)
        there = slice(first + i * block, first + (i + 1) * block)
        stacked = heads_below(queries_ref[there, :], heads)
        keys = cache_ref[mine, 0].reshape(block * window, HD)
        values = cache_ref[mine, 1].reshape(block * window, HD)
        scores = lax.dot_general(
            stacked, keys, (((1,), (1,)), ((), ())), preferred_element_type=f32
        )
        alive = (at >= start) & (at < start + live[there])
        weights = weights_of(scores, jnp.concatenate([alive] * heads, axis=0))
        numerator = jnp.dot(weights.astype(bf16), values, preferred_element_type=f32)
        denominator = jnp.sum(weights, axis=1, keepdims=True)
        for h in range(heads):
            own = slice(h * block, (h + 1) * block)
            num_ref[mine, h * HD : (h + 1) * HD] = numerator[own]
            den_ref[mine, h * 128 : (h + 1) * 128] = jnp.broadcast_to(
                denominator[own], (block, 128)
            )


def down(row, rows, cols):
    return jnp.sum(jnp.where(rows == cols, row.astype(f32), 0.0), axis=1, keepdims=True)


def early_kernel(
    capacity,
    order,
    block,
    core_ref,
    owner_hbm,
    length_hbm,
    queries_hbm,
    cache_hbm,
    prompt_hbm,
    weight_hbm,
    back_ref,
    num_ref,
    den_ref,
    early_ref,
    last_hbm,
    owner_ref,
    length_ref,
    queries_ref,
    cache_ref,
    staged,
    sems,
    early_sems,
    last_sem,
):
    requests, slots = back_ref.shape
    parts = parts_of(prompt_hbm.shape[0])
    pairs = (
        (owner_hbm, owner_ref),
        (length_hbm, length_ref),
        (queries_hbm, queries_ref),
        (cache_hbm.at[pl.ds(0, cache_ref.shape[0])], cache_ref),
    )
    copies = [pltpu.make_async_copy(a, b, sems.at[i]) for i, (a, b) in enumerate(pairs)]
    quarter = last_hbm.shape[1]
    cols = pl.ds(pl.multiple_of((core_ref[0] + 2) * quarter, 128), quarter)
    stage = pltpu.make_async_copy(weight_hbm.at[:, cols], staged, last_sem)
    unstage = pltpu.make_async_copy(staged, last_hbm, last_sem)
    prompts = [
        pltpu.make_async_copy(prompt_hbm.at[parts[i]], early_ref.at[i], early_sems.at[i])
        for i in range(early_ref.shape[0])
    ]
    for copy in copies + [stage] + prompts:
        copy.start()
    for copy in copies:
        copy.wait()
    stage.wait()
    unstage.start()
    by_row, by_col, rows, cols = owners(owner_ref, order)
    earlier = jnp.where((by_row == by_col) & (cols < rows), 1.0, 0.0)
    rank = jnp.sum(earlier, axis=1, keepdims=True)
    position = (by_row * capacity + rank).astype(jnp.int32)
    back_ref[...] = jnp.where(iota((requests, slots), 1) == position, 1.0, 0.0).astype(bf16)
    live = down(length_ref[...], rows, cols).astype(jnp.int32)
    attend_own(block, 0, live, queries_ref, cache_ref, num_ref, den_ref)
    for copy in prompts + [unstage]:
        copy.wait()


def late_kernel(
    block,
    core_ref,
    length_hbm,
    queries_hbm,
    cache_hbm,
    weight_hbm,
    after_hbm,
    num_ref,
    den_ref,
    weight_ref,
    length_ref,
    queries_ref,
    cache_ref,
    sems,
    weight_sems,
):
    requests = queries_ref.shape[0]
    half = cache_ref.shape[0]
    first = requests - half
    pairs = (
        (length_hbm, length_ref),
        (queries_hbm, queries_ref),
        (cache_hbm.at[pl.ds(first, half)], cache_ref),
    )
    copies = [pltpu.make_async_copy(a, b, sems.at[i]) for i, (a, b) in enumerate(pairs)]
    quarter = weight_ref.shape[2]
    weight_copies = []
    for i, q in enumerate((1 - core_ref[0], 3 - core_ref[0], core_ref[0])):
        cols = pl.ds(pl.multiple_of(q * quarter, 128), quarter)
        weight_copies.append(
            pltpu.make_async_copy(weight_hbm.at[:, cols], weight_ref.at[i], weight_sems.at[i])
        )
    for copy in copies + weight_copies:
        copy.start()
    for copy in copies:
        copy.wait()
    rows, cols = iota((requests, requests), 0), iota((requests, requests), 1)
    live = down(length_ref[...], rows, cols).astype(jnp.int32)
    attend_own(block, first, live, queries_ref, cache_ref, num_ref, den_ref)
    for copy in weight_copies:
        copy.wait()


def parts_of(groups):
    return [(g, part) for g in range(groups) for part in range(2)]


def prompt_kernel(
    chunk,
    window,
    moves,
    length_hbm,
    slots_ref,
    early_ref,
    cache_hbm,
    out_ref,
    length_ref,
    held,
    sorted_ref,
    done_ref,
    num_ref,
    den_ref,
    sems,
    length_sem,
):
    groups, _, size, _ = cache_hbm.shape
    slots = slots_ref.shape[0]
    width = slots_ref.shape[1] - EXTRA
    heads = width // HD
    parts = parts_of(groups)
    early = early_ref.shape[0]
    length_copy = pltpu.make_async_copy(length_hbm, length_ref, length_sem)
    length_copy.start()
    copies = {
        parts[i]: pltpu.make_async_copy(
            cache_hbm.at[parts[i]], held.at[i - early], sems.at[i - early]
        )
        for i in range(early, len(parts))
    }
    for part in parts[early:]:
        copies[part].start()

    def read(g, part, span):
        i = parts.index((g, part))
        return early_ref[i, span, :] if i < early else held[i - early, span, :]

    def moved(block):
        if moves == sorted(moves):
            return block
        step = slots // len(moves)
        return jnp.concatenate([block[m * step : (m + 1) * step] for m in moves], axis=0)

    def pieces(total, rows):
        lanes = iota((1, EXTRA), 1)
        extra = jnp.zeros((rows, EXTRA), f32)
        for h in range(heads):
            rest = total[h * rows : (h + 1) * rows]
            for k in range(3):
                piece = rest.astype(bf16).astype(f32)
                rest = rest - piece
                extra = jnp.where(lanes == 3 * h + k, piece, extra)
        return extra.astype(bf16)

    def fold(weights):
        part = weights[:, :128]
        for k in range(1, weights.shape[1] // 128):
            part = part + weights[:, k * 128 : (k + 1) * 128]
        return part

    rows, cols = iota((slots, slots), 0), iota((slots, slots), 1)
    by_row = jnp.broadcast_to(slots_ref[:, width : width + 1].astype(f32), (slots, slots))
    by_col = jnp.sum(jnp.where(rows == cols, by_row, 0.0), axis=0, keepdims=True)
    same = by_row == by_col
    rank_row = jnp.sum(jnp.where(same & (cols < rows), 1.0, 0.0), axis=1, keepdims=True)
    rank_col = jnp.sum(jnp.where(same & (rows < cols), 1.0, 0.0), axis=0, keepdims=True)
    length_copy.wait()
    crowded = jnp.max(jnp.where(by_col > 0.0, rank_col, 0.0)) >= window

    at_row = (by_row[:, :1] - 1.0) * window + rank_row
    at_row = jnp.where(by_row[:, :1] > 0.0, at_row, -1.0).astype(jnp.int32)
    at_col = jnp.where(by_col > 0.0, (by_col - 1.0) * window + rank_col, -1.0).astype(jnp.int32)
    room = groups * window
    there = jnp.where(iota((room, slots), 0) == at_col, 1.0, 0.0).astype(bf16)
    back = jnp.where(iota((slots, room), 1) == moved(at_row), 1.0, 0.0).astype(bf16)
    for h in range(heads):
        part = jnp.dot(there, slots_ref[:, h * HD : (h + 1) * HD], preferred_element_type=f32)
        for g in range(groups):
            at = (g * heads + h) * window
            sorted_ref[at : at + window, :] = part[g * window : (g + 1) * window].astype(bf16)
    scores = [None] * groups
    waited = early
    everything = slice(0, size)
    for u in range(groups + 1):
        needed = min(2 * u + 1, len(parts))
        if needed > waited:
            needed = min(needed + 1, len(parts))
            for part in parts[waited:needed]:
                copies[part].wait()
            waited = needed
        if u < groups:
            scores[u] = lax.dot_general(
                sorted_ref[u * heads * window : (u + 1) * heads * window, :],
                read(u, 0, everything),
                (((1,), (1,)), ((), ())),
                preferred_element_type=f32,
            )
        if u > 0:
            g = u - 1
            weights = weights_of(scores[g], iota((1, size), 1) < length_ref[g])
            num = jnp.dot(
                weights.astype(bf16), read(g, 1, everything), preferred_element_type=f32
            )
            mine = slice(g * window, (g + 1) * window)
            for h in range(heads):
                done_ref[mine, h * HD : (h + 1) * HD] = num[
                    h * window : (h + 1) * window
                ].astype(bf16)
            den = jnp.sum(fold(weights), axis=1, keepdims=True)
            done_ref[mine, width:] = pieces(den, window)
    out_ref[...] = jnp.dot(back, done_ref[...], preferred_element_type=f32).astype(bf16)

    @pl.when(crowded)
    def _():
        stacked = heads_below(slots_ref[:, :width], heads)
        mark = jnp.concatenate([by_row[:, :1]] * heads, axis=0)
        num_ref[...] = jnp.zeros_like(num_ref)
        den_ref[...] = jnp.zeros_like(den_ref)
        for g in range(groups):
            limit = jnp.where(mark == g + 1.0, length_ref[g], 0)

            @pl.loop(0, (length_ref[g] + chunk - 1) // chunk)
            def _(c):
                span = pl.ds(pl.multiple_of(c * chunk, chunk), chunk)
                scores = lax.dot_general(
                    stacked,
                    read(g, 0, span),
                    (((1,), (1,)), ((), ())),
                    preferred_element_type=f32,
                )
                alive = iota((heads * slots, chunk), 1) < limit - c * chunk
                weights = weights_of(scores, alive)
                num_ref[...] += jnp.dot(
                    weights.astype(bf16), read(g, 1, span), preferred_element_type=f32
                )
                den_ref[...] += fold(weights)

        for h in range(heads):
            num = num_ref[h * slots : (h + 1) * slots]
            out_ref[:, h * HD : (h + 1) * HD] = moved(num).astype(bf16)
        extra = pieces(jnp.sum(den_ref[...], axis=1, keepdims=True), slots)
        out_ref[:, width:] = moved(extra.astype(f32)).astype(bf16)


def combine_kernel(
    returned_ref, back_ref, num_a, den_a, num_b, den_b, weight_ref, att_ref, give_ref
):
    width = num_a.shape[1]
    heads = width // HD
    mine = jnp.dot(back_ref[...], returned_ref[...], preferred_element_type=f32)
    for h in range(heads):
        cols = slice(h * HD, (h + 1) * HD)
        numerator = mine[:, cols] + jnp.concatenate([num_a[:, cols], num_b[:, cols]], axis=0)
        at = width + 3 * h
        lane = slice(h * 128, h * 128 + 1)
        denominator = jnp.concatenate([den_a[:, lane], den_b[:, lane]], axis=0) + (
            mine[:, at : at + 1] + mine[:, at + 1 : at + 2] + mine[:, at + 2 : at + 3]
        )
        att_ref[:, cols] = (numerator / denominator).astype(bf16)
    give_ref[...] = jnp.dot(att_ref[...], weight_ref[0], preferred_element_type=f32).astype(bf16)


def give_kernel(att_ref, weight_ref, give_ref):
    give_ref[...] = jnp.dot(att_ref[...], weight_ref[1], preferred_element_type=f32).astype(bf16)


def own_kernel(att_ref, weight_ref, own_ref):
    own_ref[...] = jnp.dot(att_ref[...], weight_ref[2], preferred_element_type=f32)


def chip_kernel(own_ref, got_ref, sum_ref, send_ref):
    total = own_ref[...] + got_ref[...].astype(f32)
    sum_ref[...] = total
    send_ref[...] = total.astype(bf16)


def last_kernel(att_ref, weight_ref, got_ref, after_ref, sum_ref, send_ref):
    total = jnp.dot(att_ref[...], weight_ref[...], preferred_element_type=f32)
    total = total + got_ref[...].astype(f32)
    sum_ref[...] = total
    send_ref[...] = total.astype(bf16)


def squares(total):
    part = jnp.zeros((total.shape[0], 128), f32)
    for k in range(total.shape[1] // 128):
        piece = total[:, k * 128 : (k + 1) * 128]
        part = part + piece * piece
    return part


def first_square_kernel(sum_ref, got_ref, total_ref, square_ref):
    total = sum_ref[...] + got_ref[...].astype(f32)
    total_ref[...] = total
    square_ref[...] = squares(total)


def square_kernel(row_ref, total_ref, first_ref, sum_ref, got_ref, mine_ref, square_ref):
    total = sum_ref[...] + got_ref[...].astype(f32)
    square_ref[...] = first_ref[...] + squares(total)
    mine_ref[...] = jnp.where(row_ref[0] == 0, total_ref[...], total)


def final_kernel(features, mine_ref, square_ref, got_ref, gain_ref, hidden_ref, out_ref):
    square = jnp.sum(square_ref[...] + got_ref[...], axis=1, keepdims=True)
    scale = lax.rsqrt(square * (1.0 / features) + epsilon)
    normed = mine_ref[...] * scale * gain_ref[...]
    out_ref[...] = (hidden_ref[...].astype(f32) + normed).astype(bf16)


def call(kernel, outs, ins, **kw):
    specs = [
        pl.BlockSpec(memory_space=SMEM if a.ndim == 1 else VMEM) for a in ins
    ]
    return pl.pallas_call(
        kernel,
        out_shape=outs,
        in_specs=specs,
        out_specs=jax.tree.map(lambda _: pl.BlockSpec(memory_space=VMEM), outs),
        compiler_params=PARAMS,
        **kw,
    )(*ins)


def in_hbm(*arrays):
    return [pltpu.with_memory_space_constraint(a, pltpu.MemorySpace.HBM) for a in arrays]


def shape(dims, dtype):
    return jax.ShapeDtypeStruct(dims, dtype)


def shards(
    hidden_input,
    queries,
    prompt_cache,
    suffix_cache,
    owner_replica,
    group_slot,
    prompt_length,
    suffix_length,
    output_weight,
    post_gain,
):
    replicas = lax.axis_size("replica")
    ranks = lax.axis_size("tensor")
    requests, width = queries.shape
    capacity = max(2, (2 * requests + replicas - 1) // replicas)
    slots = replicas * capacity
    groups, _, size, _ = prompt_cache.shape
    window = suffix_cache.shape[2]
    features = output_weight.shape[1]
    quarter = features // ranks
    heads = width // HD
    there, back_again = orders_of(replicas)
    index = lax.axis_index("tensor")
    core = (index % 2).reshape(1)
    far_row = (index // 2).reshape(1)

    def exchange(x, order):
        blocks = x.reshape(replicas, capacity, width + EXTRA)
        blocks = lax.all_to_all(
            blocks, "replica", split_axis=0, concat_axis=0, axis_index_groups=[order], tiled=True
        )
        return blocks.reshape(slots, width + EXTRA)

    def permute(x, bit):
        return lax.ppermute(x, "tensor", [(i, i ^ bit) for i in range(ranks)])

    owner_row = owner_replica.reshape(1, requests)
    sent = pl.pallas_call(
        functools.partial(route_kernel, capacity, there),
        out_shape=pltpu.VMEM((slots, width + EXTRA), bf16),
        in_specs=[HBM_SPEC] * 3,
        out_specs=VMEM_SPEC,
        scratch_shapes=[
            pltpu.VMEM((1, requests), jnp.int32),
            pltpu.VMEM((1, requests), jnp.int32),
            pltpu.VMEM((requests, width), bf16),
            pltpu.SemaphoreType.DMA((3,)),
        ],
        compiler_params=PARAMS,
    )(*in_hbm(owner_row, group_slot.reshape(1, requests), queries))
    got = exchange(sent, there)

    early = 3
    half = requests // 2
    block = math.gcd(16, half)
    length_row = suffix_length.reshape(1, requests)
    halves = [shape((half, width), f32), shape((half, heads * 128), f32)]
    row = pltpu.VMEM((1, requests), jnp.int32)
    own_scratch = [
        row,
        pltpu.VMEM((requests, width), bf16),
        pltpu.VMEM((half,) + suffix_cache.shape[1:], bf16),
    ]
    back, num_a, den_a, prefetched, last = pl.pallas_call(
        functools.partial(early_kernel, capacity, back_again, block),
        out_shape=[shape((requests, slots), bf16)]
        + halves
        + [pltpu.VMEM((early, size, HD), bf16), pltpu.HBM((width, quarter), bf16)],
        in_specs=[SMEM_SPEC] + [HBM_SPEC] * 6,
        out_specs=[VMEM_SPEC] * 4 + [HBM_SPEC],
        scratch_shapes=[row]
        + own_scratch
        + [
            pltpu.VMEM((width, quarter), bf16),
            pltpu.SemaphoreType.DMA((4,)),
            pltpu.SemaphoreType.DMA((early,)),
            pltpu.SemaphoreType.DMA,
        ],
        compiler_params=PARAMS,
        cost_estimate=pl.CostEstimate(
            flops=4 * requests * window * HD * block,
            bytes_accessed=2 * early * size * HD * 2 + suffix_cache.size,
            transcendentals=0,
        ),
    )(
        core,
        *in_hbm(owner_row, length_row, queries, suffix_cache, prompt_cache, output_weight),
    )

    chunk = math.gcd(512, size)
    moves = [there.index(replica) for replica in back_again]
    fit = min(48, slots)
    answered = pl.pallas_call(
        functools.partial(prompt_kernel, chunk, fit, moves),
        out_shape=pltpu.VMEM((slots, width + EXTRA), bf16),
        in_specs=[HBM_SPEC, VMEM_SPEC, VMEM_SPEC, HBM_SPEC],
        out_specs=VMEM_SPEC,
        scratch_shapes=[
            pltpu.SMEM((groups,), jnp.int32),
            pltpu.VMEM((2 * groups - early, size, HD), bf16),
            pltpu.VMEM((groups * heads * fit, HD), bf16),
            pltpu.VMEM((groups * fit, width + EXTRA), bf16),
            pltpu.VMEM((heads * slots, HD), f32),
            pltpu.VMEM((heads * slots, 128), f32),
            pltpu.SemaphoreType.DMA((2 * groups - early,)),
            pltpu.SemaphoreType.DMA,
        ],
        compiler_params=PARAMS,
    )(
        *in_hbm(prompt_length),
        got,
        pltpu.with_memory_space_constraint(prefetched, VMEM),
        *in_hbm(prompt_cache),
    )
    returned = exchange(answered, back_again)

    num_b, den_b, weight = pl.pallas_call(
        functools.partial(late_kernel, block),
        out_shape=halves + [pltpu.VMEM((3, width, quarter), bf16)],
        in_specs=[SMEM_SPEC] + [HBM_SPEC] * 5,
        out_specs=[VMEM_SPEC] * 3,
        scratch_shapes=own_scratch
        + [pltpu.SemaphoreType.DMA((3,)), pltpu.SemaphoreType.DMA((3,))],
        compiler_params=PARAMS,
        cost_estimate=pl.CostEstimate(
            flops=4 * requests * window * HD * block,
            bytes_accessed=suffix_cache.size + output_weight.size * 2,
            transcendentals=0,
        ),
    )(core, *in_hbm(length_row, queries, suffix_cache, output_weight, answered))
    weight = pltpu.with_memory_space_constraint(weight, VMEM)

    block_f32 = shape((requests, quarter), f32)
    block_bf16 = shape((requests, quarter), bf16)
    attention, give_a = call(
        combine_kernel,
        [shape((requests, width), bf16), block_bf16],
        [returned, back, num_a, den_a, num_b, den_b, weight],
    )
    got_a = permute(give_a, 1)
    got_b = permute(call(give_kernel, block_bf16, [attention, weight]), 1)
    own_a = call(own_kernel, block_f32, [attention, weight])
    sum_a, send_a = call(chip_kernel, [block_f32, block_bf16], [own_a, got_a])
    far_a = permute(send_a, 2)
    sum_b, send_b = call(last_kernel, [block_f32, block_bf16], [attention, last, got_b, send_a])
    far_b = permute(send_b, 2)
    outs = [block_f32, shape((requests, 128), f32)]
    total_a, square_a = call(first_square_kernel, outs, [sum_a, far_a])
    mine, square = call(square_kernel, outs, [far_row, total_a, square_a, sum_b, far_b])
    beside = permute(square, 1)
    return call(
        functools.partial(final_kernel, features),
        shape((requests, quarter), bf16),
        [mine, square, beside, post_gain.reshape(1, quarter), hidden_input],
    )


def solution(mesh):
    in_specs = (
        P("replica", "tensor"),
        P("replica", "tensor"),
        P("replica", None, None, "tensor"),
        P("replica", None, None, "tensor"),
        P("replica", None),
        P("replica"),
        P("replica"),
        P("replica"),
        P("tensor", None),
        P("tensor"),
    )
    out_specs = P("replica", "tensor")
    return jax.shard_map(shards, mesh=mesh, in_specs=in_specs, out_specs=out_specs, check_vma=False)
```
